32 devices in a mesh: dp: 4 (over y, core), fsdp: 8 (over z, x).
Axes of the slice: x: 2, y: 2, z: 4, core: 2. Of those that a mesh axis runs over, the one named last changes fastest.
Arguments:
- images: bfloat16 [32, 26, 38, 768], P(('dp', 'fsdp')), may hold values from -6 to 6
- grad_out: bfloat16 [32, 26, 38, 768], P(('dp', 'fsdp')), may hold values from -6 to 6
- box_rows: int32 [32, 300, 2], P(('dp', 'fsdp')), may hold values from 0 to 26
- box_cols: int32 [32, 300, 2], P(('dp', 'fsdp')), may hold values from 0 to 38
- box_valid: int32 [32, 300], P(('dp', 'fsdp')), may hold values 0 or 1
- box_count: int32 [32], P(('dp', 'fsdp')), may hold values from 1 to 300
- in_weight: bfloat16 [768, 2304], P(('dp', 'fsdp')), may hold values from -0.21875 to 0.21875
- query_bias: bfloat16 [768], P(('dp', 'fsdp')), may hold values from -2 to 2
- value_bias: bfloat16 [768], P(('dp', 'fsdp')), may hold values from -2 to 2
- out_weight: bfloat16 [768, 768], P(('dp', 'fsdp')), may hold values from -1.75 to 1.75
- out_bias: bfloat16 [768], P(('dp', 'fsdp')), may hold values from -2 to 2
- first_gain: bfloat16 [768], P(('dp', 'fsdp')), may hold values from 0.099609375 to 1.8984375
- first_shift: bfloat16 [768], P(('dp', 'fsdp')), may hold values from -2 to 2
- second_gain: bfloat16 [768], P(('dp', 'fsdp')), may hold values from 0.099609375 to 1.8984375
- second_shift: bfloat16 [768], P(('dp', 'fsdp')), may hold values from -2 to 2
- up_weight: bfloat16 [768, 3072], P(('dp', 'fsdp')), may hold values from -0.21875 to 0.21875
- up_bias: bfloat16 [3072], P(('dp', 'fsdp')), may hold values from -2 to 2
- down_weight: bfloat16 [3072, 768], P(('dp', 'fsdp')), may hold values from -0.109375 to 0.109375
- down_bias: bfloat16 [768], P(('dp', 'fsdp')), may hold values from -2 to 2
- row_table: bfloat16 [27, 64], replicated, may hold values from -1 to 1
- col_table: bfloat16 [27, 64], replicated, may hold values from -1 to 1
Outputs:
- block_out: bfloat16 [32, 26, 38, 768], P(('dp', 'fsdp'))
- image_grad: bfloat16 [32, 26, 38, 768], P(('dp', 'fsdp'))
- in_weight_grad: float32 [768, 2304], P(('dp', 'fsdp'))
- query_bias_grad: float32 [768], P(('dp', 'fsdp'))
- value_bias_grad: float32 [768], P(('dp', 'fsdp'))
- out_weight_grad: float32 [768, 768], P(('dp', 'fsdp'))
- out_bias_grad: float32 [768], P(('dp', 'fsdp'))
- first_gain_grad: float32 [768], P(('dp', 'fsdp'))
- first_shift_grad: float32 [768], P(('dp', 'fsdp'))
- second_gain_grad: float32 [768], P(('dp', 'fsdp'))
- second_shift_grad: float32 [768], P(('dp', 'fsdp'))
- up_weight_grad: float32 [768, 3072], P(('dp', 'fsdp'))
- up_bias_grad: float32 [3072], P(('dp', 'fsdp'))
- down_weight_grad: float32 [3072, 768], P(('dp', 'fsdp'))
- down_bias_grad: float32 [768], P(('dp', 'fsdp'))
- row_table_grad: float32 [27, 64], replicated
- col_table_grad: float32 [27, 64], replicated
The draws below stay inside these ranges and needn't reach their ends.
All inputs are finite; a program needn't handle non-finite values. No bound on the sum of `box_valid` on one device may be relied on, other than what follows from the above.
Results may differ from the reference program's by a relative error of at most 0.013.
Values may be sent and summed in bfloat16 or wider, within the bound.
No kernel may reach another device: no remote copies, remote signals or barrier semaphores. Data moves between devices by JAX's collectives and lax.ppermute only.
A program may use at most 256 MiB of HBM per device.

```python
import jax
import jax.numpy as jnp
from jax import lax

D = 768
HEADS = 12
HD = 64
FF = 3072
WIN = 14
GH = 26
GW = 38
NBOX = 300
HP = 28
WP = 42
IMAGES = 32


def touch_ends(array, own_key, low, largest):
    index_at = [jax.random.randint(jax.random.fold_in(own_key, axis), (), 0, length) for axis, length in enumerate(array.shape)]
    longest = array.shape.index(max(array.shape))
    next_to = index_at[:longest] + [(index_at[longest] + 1) % array.shape[longest]] + index_at[longest + 1:]
    return array.at[tuple(index_at)].set(low).at[tuple(next_to)].set(largest)


def level_of(rng, shape, split, least, top_value):
    level = 1.0
    for dim, parts in split:
        draws = jax.random.uniform(jax.random.fold_in(jax.random.fold_in(rng, 6), dim), (parts,), jnp.float32, least / len(split), top_value / len(split))
        level = level * jnp.repeat(jnp.exp(draws), shape[dim] // parts).reshape((-1,) + (1,) * (len(shape) - 1 - dim))
    return level


def gaussian(stream_key, shape, deviation, most, cuts=(), kind=jnp.bfloat16):
    gain = level_of(stream_key, shape, cuts, -0.22, 0.18) if cuts else 1.0
    array = jax.random.normal(stream_key, shape, jnp.float32) * deviation * gain
    return jnp.minimum(jnp.maximum(array, -most), most).astype(kind)


def setup_inputs(seed: int = 0) -> dict:
    key_of = jax.random.split(jax.random.key(seed), 22)
    images = gaussian(key_of[0], (IMAGES, GH, GW, D), 1.0, 6.0, ((0, 32),))
    grad_out = gaussian(key_of[1], (IMAGES, GH, GW, D), 1.0, 6.0, ((0, 32),))
    box_rows = touch_ends(jax.random.randint(key_of[2], (IMAGES, NBOX, 2), 0, GH + 1), jax.random.fold_in(key_of[2], 1), 0, GH).astype(jnp.int32)
    box_cols = touch_ends(jax.random.randint(key_of[3], (IMAGES, NBOX, 2), 0, GW + 1), jax.random.fold_in(key_of[3], 1), 0, GW).astype(jnp.int32)
    box_valid = touch_ends((jax.random.randint(key_of[4], (IMAGES, NBOX), 0, 4) < 3).astype(jnp.int32), jax.random.fold_in(key_of[4], 1), 0, 1)
    box_count = touch_ends(jax.random.randint(key_of[5], (IMAGES,), 1, NBOX + 1), jax.random.fold_in(key_of[5], 1), 1, NBOX).astype(jnp.int32)
    in_weight = gaussian(key_of[6], (D, 3 * D), D ** -0.5, 0.21875, ((0, 32),))
    query_bias = gaussian(key_of[7], (D,), 0.3, 2.0, ((0, 32),))
    value_bias = gaussian(key_of[8], (D,), 0.3, 2.0, ((0, 32),))
    out_weight = gaussian(key_of[9], (D, D), (D // 64) ** -0.5, 1.75, ((0, 32),))
    out_bias = gaussian(key_of[10], (D,), 0.3, 2.0, ((0, 32),))
    first_gain = jnp.clip(1.0 + 0.18 * jax.random.normal(key_of[11], (D,), jnp.float32), 0.099609375, 1.8984375).astype(jnp.bfloat16)
    first_shift = gaussian(key_of[12], (D,), 0.3, 2.0, ((0, 32),))
    second_gain = jnp.clip(1.0 + 0.18 * jax.random.normal(key_of[13], (D,), jnp.float32), 0.099609375, 1.8984375).astype(jnp.bfloat16)
    second_shift = gaussian(key_of[14], (D,), 0.3, 2.0, ((0, 32),))
    up_weight = gaussian(key_of[15], (D, FF), D ** -0.5, 0.21875, ((0, 32),))
    up_bias = gaussian(key_of[16], (FF,), 0.3, 2.0, ((0, 32),))
    down_weight = gaussian(key_of[17], (FF, D), FF ** -0.5, 0.109375, ((0, 32),))
    down_bias = gaussian(key_of[18], (D,), 0.3, 2.0, ((0, 32),))
    row_table = gaussian(key_of[19], (2 * WIN - 1, HD), 0.15, 1.0)
    col_table = gaussian(key_of[20], (2 * WIN - 1, HD), 0.15, 1.0)
    return {"images": images, "grad_out": grad_out, "box_rows": box_rows, "box_cols": box_cols, "box_valid": box_valid, "box_count": box_count, "in_weight": in_weight, "query_bias": query_bias, "value_bias": value_bias, "out_weight": out_weight, "out_bias": out_bias, "first_gain": first_gain, "first_shift": first_shift, "second_gain": second_gain, "second_shift": second_shift, "up_weight": up_weight, "up_bias": up_bias, "down_weight": down_weight, "down_bias": down_bias, "row_table": row_table, "col_table": col_table}


highest = lax.Precision.HIGHEST
epsilon = 1e-06

@jax.custom_vjp
def low(v):
    return lax.optimization_barrier(v.astype(jnp.bfloat16)).astype(jnp.float32)

@jax.custom_vjp
def low_back(v):
    return v

def low_keep(v):
    return (low(v), None)

def low_pass(kept, grad):
    return (grad,)

def back_keep(v):
    return (v, None)

def back_low(kept, grad):
    return (low(grad),)
low.defvjp(low_keep, low_pass)
low_back.defvjp(back_keep, back_low)

def normalize(tensor):
    center = tensor - lax.optimization_barrier(jnp.mean(tensor, axis=-1, keepdims=True))
    spread = lax.optimization_barrier(jnp.mean(center * center, axis=-1, keepdims=True))
    return center * lax.rsqrt(spread + epsilon)

def windows_of(field_in):
    number = field_in.shape[0]
    width = field_in.shape[-1]
    padded = jnp.pad(field_in, ((0, 0), (0, HP - GH), (0, WP - GW), (0, 0)))
    pieces = padded.reshape(number, HP // WIN, WIN, WP // WIN, WIN, width)
    return pieces.transpose(0, 1, 3, 2, 4, 5).reshape(-1, WIN * WIN, width)

def field_of(pieces, number):
    width = pieces.shape[-1]
    layout = pieces.reshape(number, HP // WIN, WP // WIN, WIN, WIN, width).transpose(0, 1, 3, 2, 4, 5)
    return layout.reshape(number, HP, WP, width)[:, :GH, :GW, :]

def expand_table(table):
    places = jnp.arange(WIN, dtype=jnp.int32)
    offsets = places[:, None] - places[None, :] + WIN - 1
    return table[offsets]

def patch_weights(rows, cols, valid, number):
    slot_ids = jnp.arange(NBOX, dtype=jnp.int32)
    live_box = ((slot_ids < number) & (valid == 1)).astype(jnp.float32)
    top_row = jnp.minimum(rows[:, 0], rows[:, 1])
    low_row = jnp.maximum(rows[:, 0], rows[:, 1])
    left_col = jnp.minimum(cols[:, 0], cols[:, 1])
    right_col = jnp.maximum(cols[:, 0], cols[:, 1])
    grid_rows = jnp.arange(GH, dtype=jnp.int32)
    grid_cols = jnp.arange(GW, dtype=jnp.int32)
    in_rows = ((grid_rows[None, :] >= top_row[:, None]) & (grid_rows[None, :] < low_row[:, None])).astype(jnp.float32) * live_box[:, None]
    in_cols = ((grid_cols[None, :] >= left_col[:, None]) & (grid_cols[None, :] < right_col[:, None])).astype(jnp.float32)
    inside = lax.optimization_barrier(jnp.sum(in_rows[:, :, None] * in_cols[:, None, :], axis=0))
    return 1.0 + 2.0 * inside / jnp.maximum(jnp.sum(live_box), 1.0)

def block(picture, params, row_table, col_table):
    in_weight, query_bias, value_bias, out_weight, out_bias, first_gain, first_shift, second_gain, second_shift, up_weight, up_bias, down_weight, down_bias = params
    field_in = picture[None]
    normed = normalize(field_in) * first_gain + first_shift
    pieces = low(windows_of(normed))
    number = pieces.shape[0]
    bias_all = jnp.concatenate([query_bias, jnp.zeros_like(query_bias), value_bias])
    packed = jnp.einsum('wsd,de->wse', pieces, in_weight, precision=highest) + bias_all
    packed = low(low_back(packed)).reshape(number, WIN, WIN, 3, HEADS, HD)
    queries = packed[:, :, :, 0]
    key_rows = packed[:, :, :, 1]
    values = packed[:, :, :, 2]
    rows_full = expand_table(row_table)
    cols_full = expand_table(col_table)
    scores = jnp.einsum('wxyhc,wuvhc->whxyuv', queries, key_rows, precision=highest) * HD ** (-0.5)
    scores = scores + jnp.einsum('wxyhc,xuc->whxyu', queries, rows_full, precision=highest)[..., None]
    scores = scores + jnp.einsum('wxyhc,yvc->whxyv', queries, cols_full, precision=highest)[..., None, :]
    scores = low_back(scores.reshape(number, HEADS, WIN * WIN, WIN * WIN))
    soft = low(jax.nn.softmax(scores, axis=-1))
    attended = jnp.einsum('whqk,wkhc->wqhc', soft, values.reshape(number, WIN * WIN, HEADS, HD), precision=highest)
    attended = low(low_back(attended.reshape(number, WIN * WIN, D)))
    branch = jnp.einsum('wsd,de->wse', attended, out_weight, precision=highest) + out_bias
    branch = low_back(field_of(branch, 1))
    middle = field_in + branch
    normed_two = low(normalize(middle) * second_gain + second_shift)
    hidden = jnp.einsum('bhwd,df->bhwf', normed_two, up_weight, precision=highest) + up_bias
    active = low(jax.nn.gelu(low_back(hidden), approximate=False))
    update = low_back(jnp.einsum('bhwf,fd->bhwd', active, down_weight, precision=highest) + down_bias)
    return (middle + update)[0]

def reference(images, grad_out, box_rows, box_cols, box_valid, box_count, in_weight, query_bias, value_bias, out_weight, out_bias, first_gain, first_shift, second_gain, second_shift, up_weight, up_bias, down_weight, down_bias, row_table, col_table):
    params = tuple((entry.astype(jnp.float32) for entry in (in_weight, query_bias, value_bias, out_weight, out_bias, first_gain, first_shift, second_gain, second_shift, up_weight, up_bias, down_weight, down_bias)))
    rows_f = row_table.astype(jnp.float32)
    cols_f = col_table.astype(jnp.float32)

    def one_image(carry, item):
        picture, cotangent, rows, cols, valid, number = item
        weighting = patch_weights(rows, cols, valid, number)
        result, pullback = jax.vjp(block, picture.astype(jnp.float32), params, rows_f, cols_f)
        grad_picture, grad_params, grad_rows, grad_cols = pullback(cotangent.astype(jnp.float32) * weighting[:, :, None])
        carry = jax.tree.map(lambda total, term: total + term, carry, (grad_params, grad_rows, grad_cols))
        return (carry, (result.astype(jnp.bfloat16), grad_picture.astype(jnp.bfloat16)))
    start = jax.tree.map(jnp.zeros_like, (params, rows_f, cols_f))
    (grad_params, grad_rows, grad_cols), (outputs, grad_images) = lax.scan(one_image, start, (images, grad_out, box_rows, box_cols, box_valid, box_count))
    g_in, g_qbias, g_vbias, g_out, g_obias, g_gain1, g_shift1, g_gain2, g_shift2, g_up, g_upbias, g_down, g_downbias = grad_params
    return (outputs, grad_images, g_in, g_qbias, g_vbias, g_out, g_obias, g_gain1, g_shift1, g_gain2, g_shift2, g_up, g_upbias, g_down, g_downbias, grad_rows, grad_cols)
```

```python
import jax
import jax.numpy as jnp
import numpy as np
from jax import lax
from jax.experimental import pallas as pl
from jax.experimental.pallas import tpu as pltpu
from jax.sharding import PartitionSpec as P

D = 768
HEADS = 12
HD = 64
FF = 3072
WIN = 14
GH = 26
GW = 38
NBOX = 300
ACROSS = 3
WINDOWS = 6
LINE = 16
TOK = WIN * LINE
REAL = GH * GW
DENSE = 992
PAIRS = HEADS // 2
STARTS = (0, 14, 28)
WIDTHS = (14, 14, 10)
CHUNK = 512
SPLITS = ((0, 256), (256, 256), (512, 256), (768, 224))
epsilon = 1e-06
f32 = jnp.float32
bf16 = jnp.bfloat16
LIMIT = 60 * 1024 * 1024


def dot(a, b):
    return lax.dot_general(a, b, (((1,), (0,)), ((), ())), preferred_element_type=f32)


def dot_bt(a, b):
    return lax.dot_general(a, b, (((1,), (1,)), ((), ())), preferred_element_type=f32)


def dot_at(a, b):
    return lax.dot_general(a, b, (((0,), (0,)), ((), ())), preferred_element_type=f32)


def unit_of(x):
    center = x - jnp.mean(x, axis=-1, keepdims=True)
    inverse = lax.rsqrt(jnp.mean(center * center, axis=-1, keepdims=True) + epsilon)
    return center * inverse, inverse


def norm_back(grad, unit, inverse, gain):
    scaled = grad * gain
    return inverse * (
        scaled
        - jnp.mean(scaled, axis=-1, keepdims=True)
        - unit * jnp.mean(scaled * unit, axis=-1, keepdims=True)
    )


def place_of(row):
    return (row // WIN) * ACROSS, row % WIN


def spread_row(row, value, out_ref):
    first, place = place_of(row)
    for piece, (start, width) in enumerate(zip(STARTS, WIDTHS)):
        part = value[start : start + width]
        part = jnp.concatenate([part, jnp.zeros((LINE - width, part.shape[1]), part.dtype)], axis=0)
        out_ref[(first + piece) * WIN + place] = part.astype(out_ref.dtype)


def join_row(row, in_ref):
    first, place = place_of(row)
    return jnp.concatenate(
        [
            in_ref[(first + piece) * WIN + place].astype(f32)[:width]
            for piece, width in enumerate(WIDTHS)
        ],
        axis=0,
    )


def begin_kernel(img_ref, vec_ref, tiles_ref):
    tiles_ref[...] = jnp.zeros_like(tiles_ref)
    gain = vec_ref[0:1, :]
    shift = vec_ref[1:2, :]
    for row in range(GH):
        unit, _ = unit_of(img_ref[row].astype(f32))
        spread_row(row, unit * gain + shift, tiles_ref)


def weight_kernel(count_ref, grad_ref, rows_ref, cols_ref, valid_ref, cot_ref, upd_ref):
    slot = lax.broadcasted_iota(jnp.int32, (NBOX, 1), 0)
    live = (slot < count_ref[0]) & (valid_ref[...] == 1)
    rows = rows_ref[...]
    cols = cols_ref[...]
    top = jnp.minimum(rows[:, 0:1], rows[:, 1:2])
    low = jnp.maximum(rows[:, 0:1], rows[:, 1:2])
    left = jnp.minimum(cols[:, 0:1], cols[:, 1:2])
    right = jnp.maximum(cols[:, 0:1], cols[:, 1:2])
    grid_r = lax.broadcasted_iota(jnp.int32, (NBOX, GH), 1)
    grid_c = lax.broadcasted_iota(jnp.int32, (NBOX, GW), 1)
    in_rows = jnp.where((grid_r >= top) & (grid_r < low) & live, 1.0, 0.0)
    in_cols = jnp.where((grid_c >= left) & (grid_c < right), 1.0, 0.0)
    inside = dot_at(in_cols.astype(bf16), in_rows.astype(bf16))
    total = jnp.sum(jnp.where(live, 1.0, 0.0))
    weight = 1.0 + 2.0 * inside / jnp.maximum(total, 1.0)
    for row in range(GH):
        cot_ref[row * GW : (row + 1) * GW, :] = grad_ref[row].astype(f32) * weight[:, row : row + 1]
    cot_ref[REAL:, :] = jnp.zeros((DENSE - REAL, D), f32)
    upd_ref[...] = cot_ref[...].astype(bf16)


def lane_iota(shape):
    return lax.broadcasted_iota(jnp.int32, shape, len(shape) - 1)


def position_terms(queries, table):
    both = dot(queries, table)
    row_part = both[:, :128].reshape(WIN, LINE, 128)
    col_part = both[:, 128:].reshape(WIN, LINE, 128)
    lane = lane_iota((LINE, 128))
    local = lane % 32
    out = []
    for place in range(WIN):
        rolled_r = pltpu.roll(row_part[place], (place - 13) % 128, 1)
        rolled_c = pltpu.roll(col_part[place], 0, 1, stride=1, stride_axis=0)
        value = jnp.where(local < 16, rolled_r, rolled_c)
        high = value.astype(bf16).astype(f32)
        value = jnp.where(lane < 64, high, value - high)
        value = jnp.where(lane == 14, 1.0, value)
        out.append(value)
    return jnp.concatenate(out, axis=0).astype(bf16)


def keep_head(value, head):
    lane = lane_iota(value.shape)
    return jnp.where((lane < HD) == (head == 0), value, jnp.zeros_like(value))


def forward_kernel(
    tiles_ref, weight_ref, bias_ref, out_w_ref, out_b_ref, table_ref, hot_ref, packed_ref, soft_ref, att_ref, branch_ref
):
    packed_ref[...] = (dot(tiles_ref[...], weight_ref[...]) + bias_ref[...]).astype(bf16)
    for pair in range(PAIRS):
        at = pair * 128
        queries = packed_ref[:, at : at + 128]
        keys = packed_ref[:, D + at : D + at + 128]
        values = packed_ref[:, 2 * D + at : 2 * D + at + 128]
        left = jnp.concatenate([queries, position_terms(queries, table_ref[...])], axis=1)
        parts = []
        for head in range(2):
            scaled = (keep_head(keys.astype(f32), head) * 0.125).astype(bf16)
            right = jnp.concatenate([scaled, hot_ref[head]], axis=1)
            scores = dot_bt(left, right)
            power = jnp.exp(scores - jnp.max(scores, axis=-1, keepdims=True))
            soft = (power * (1.0 / jnp.sum(power, axis=-1, keepdims=True))).astype(bf16)
            soft_ref[2 * pair + head] = soft
            parts.append(dot(soft, values))
        lane = lane_iota((TOK, 128))
        att_ref[:, at : at + 128] = jnp.where(lane < HD, parts[0], parts[1]).astype(bf16)
    branch_ref[...] = dot(att_ref[...], out_w_ref[...]) + out_b_ref[...]


def backward_kernel(
    packed_ref,
    soft_ref,
    att_ref,
    gbr_ref,
    tiles_ref,
    out_w_ref,
    table_ref,
    hot_ref,
    gpacked_ref,
    gin_ref,
    gout_ref,
    gbias_ref,
    gtab_ref,
    att_all,
    gbr_all,
    gpacked_all,
    gatt_ref,
):
    step = pl.program_id(0)

    @pl.when(step == 0)
    def _():
        gbias_ref[...] = jnp.zeros_like(gbias_ref)
        gtab_ref[...] = jnp.zeros_like(gtab_ref)

    gatt_ref[...] = dot_bt(gbr_ref[...], out_w_ref[...]).astype(bf16)
    lane = lane_iota((LINE, 128))
    local = lane % 32
    wide = lane_iota((TOK, 128))
    for pair in range(PAIRS):
        at = pair * 128
        queries = packed_ref[:, at : at + 128]
        keys = packed_ref[:, D + at : D + at + 128]
        values = packed_ref[:, 2 * D + at : 2 * D + at + 128]
        gatt = gatt_ref[:, at : at + 128]
        product = gatt.astype(f32) * att_ref[:, at : at + 128].astype(f32)
        left = []
        right = []
        gvalues = []
        gkeys = []
        for head in range(2):
            soft = soft_ref[2 * pair + head]
            delta = jnp.sum(keep_head(product, head), axis=-1, keepdims=True)
            gprobs = dot_bt(gatt, keep_head(values.astype(f32), head).astype(bf16))
            gscores = (soft.astype(f32) * (gprobs - delta)).astype(bf16)
            scaled = (keep_head(keys.astype(f32), head) * 0.125).astype(bf16)
            left.append(gscores)
            right.append(jnp.concatenate([scaled, hot_ref[head]], axis=1))
            gvalues.append(dot_at(soft, gatt))
            gkeys.append(dot_at(gscores, queries))
        both = dot(left[0], right[0]) + dot(left[1], right[1])
        terms = both[:, 128:].reshape(WIN, LINE, 128)
        rolled = []
        for place in range(WIN):
            value = terms[place]
            high = value.astype(bf16).astype(f32)
            value = jnp.where(lane < 64, high, value - high)
            row_part = jnp.where(local < WIN, value, 0.0)
            col_part = jnp.where((local >= 16) & (local < 16 + WIN), value, 0.0)
            row_part = pltpu.roll(row_part, 13 - place, 1)
            col_part = pltpu.roll(col_part, 0, 1, stride=1, stride_axis=0)
            rolled.append(jnp.concatenate([row_part, col_part], axis=1))
        rolled = jnp.concatenate(rolled, axis=0).astype(bf16)
        gqueries = both[:, :128] + dot_bt(rolled, table_ref[...])
        gtab_ref[...] += dot_at(rolled, queries)
        gq = gqueries.astype(bf16)
        gk = (jnp.where(wide < HD, gkeys[0], gkeys[1]) * 0.125).astype(bf16)
        gv = jnp.where(wide < HD, gvalues[0], gvalues[1]).astype(bf16)
        gpacked_ref[:, at : at + 128] = gq
        gpacked_ref[:, D + at : D + at + 128] = gk
        gpacked_ref[:, 2 * D + at : 2 * D + at + 128] = gv
        gbias_ref[0:1, at : at + 128] += jnp.sum(gq.astype(f32), axis=0, keepdims=True)
        gbias_ref[1:2, at : at + 128] += jnp.sum(gv.astype(f32), axis=0, keepdims=True)
    here = pl.ds(pl.multiple_of(step * TOK, TOK), TOK)
    att_all[here, :] = att_ref[...]
    gbr_all[here, :] = gbr_ref[...]
    gpacked_all[here, :] = gpacked_ref[...]

    @pl.when(step == WINDOWS - 1)
    def _():
        gout_ref[...] = dot_at(att_all[...], gbr_all[...]).astype(bf16)
        for part in range(0, 3 * D, D):
            gin_ref[:, part : part + D] = dot_at(tiles_ref[...], gpacked_all[:, part : part + D]).astype(bf16)


def gelu_parts(hidden):
    size = jnp.abs(hidden)
    power = jnp.exp(hidden * hidden * -0.5)
    denominator = 1.0 + (0.3275911 * 0.7071067811865476) * size
    near = pl.reciprocal(denominator, approx=True)
    near = near * (2.0 - denominator * near)
    series = near * (
        0.254829592
        + near * (-0.284496736 + near * (1.421413741 + near * (-1.453152027 + near * 1.061405429)))
    )
    tail = 0.5 * series * power
    normal = jnp.where(hidden >= 0, 1.0 - tail, tail)
    return hidden * normal, normal + hidden * power * 0.3989422804014327


def middle_kernel(
    img_ref,
    branch_ref,
    cot_ref,
    gupd_ref,
    vec_ref,
    up_ref,
    upb_ref,
    down_ref,
    out_ref,
    gbr_ref,
    gup_ref,
    gdown_ref,
    gupb_ref,
    sums_ref,
    mid,
    normed,
    update,
    gnorm,
    active,
    ghidden,
):
    step = pl.program_id(0)
    gain = vec_ref[2:3, :]
    shift = vec_ref[3:4, :]

    @pl.when(step == 0)
    def _():
        for row in range(GH):
            mid[row * GW : (row + 1) * GW, :] = img_ref[row].astype(f32) + join_row(row, branch_ref)
        mid[REAL:, :] = jnp.zeros((DENSE - REAL, D), f32)
        update[...] = jnp.zeros_like(update)
        gnorm[...] = jnp.zeros_like(gnorm)

        def chunk(index, carry):
            here = pl.ds(pl.multiple_of(index * 32, 32), 32)
            unit, _ = unit_of(mid[here, :])
            normed[here, :] = (unit * gain + shift).astype(bf16)
            return carry

        lax.fori_loop(0, DENSE // 32, chunk, 0)

    for start, size in SPLITS:
        here = slice(start, start + size)
        hidden = dot(normed[here, :], up_ref[...]) + upb_ref[...]
        gactive = dot_bt(gupd_ref[here, :], down_ref[...])
        act, slope = gelu_parts(hidden)
        act = act.astype(bf16)
        gh = (gactive * slope).astype(bf16)
        active[here, :] = act
        ghidden[here, :] = gh
        update[here, :] += dot(act, down_ref[...])
        gnorm[here, :] += dot_bt(gh, up_ref[...])
    gupb_ref[...] = jnp.sum(ghidden[...].astype(f32), axis=0, keepdims=True)
    gdown_ref[...] = dot_at(active[...], gupd_ref[...]).astype(bf16)
    gup_ref[...] = dot_at(normed[...], ghidden[...]).astype(bf16)

    @pl.when(step == pl.num_programs(0) - 1)
    def _():
        down_bias = vec_ref[4:5, :]
        for row in range(GH):
            here = slice(row * GW, (row + 1) * GW)
            out_ref[row] = (mid[here, :] + update[here, :] + down_bias).astype(bf16)

        def chunk(index, carry):
            here = pl.ds(pl.multiple_of(index * 32, 32), 32)
            unit, inverse = unit_of(mid[here, :])
            grad = gnorm[here, :]
            cot = cot_ref[here, :]
            result = cot + norm_back(grad, unit, inverse, gain)
            rounded = result.astype(bf16).astype(f32)
            update[here, :] = rounded
            gain_sum, shift_sum, branch_sum, bias_sum = carry
            return (
                gain_sum + jnp.sum((grad * unit).reshape(4, 8, D), axis=0),
                shift_sum + jnp.sum(grad.reshape(4, 8, D), axis=0),
                branch_sum + jnp.sum(rounded.reshape(4, 8, D), axis=0),
                bias_sum + jnp.sum(cot.astype(bf16).astype(f32).reshape(4, 8, D), axis=0),
            )

        zero = jnp.zeros((8, D), f32)
        sums = lax.fori_loop(0, DENSE // 32, chunk, (zero,) * 4)
        sums_ref[...] = jnp.concatenate(
            [jnp.sum(s, axis=0, keepdims=True) for s in sums] + [jnp.zeros((4, D), f32)], axis=0
        )
        gbr_ref[...] = jnp.zeros_like(gbr_ref)
        for row in range(GH):
            spread_row(row, update[row * GW : (row + 1) * GW, :], gbr_ref)


def end_kernel(img_ref, gbr_ref, gpacked_ref, weight_ref, vec_ref, out_ref, sums_ref, gtiles):
    gain = vec_ref[0:1, :]
    for window in range(WINDOWS):
        value = dot_bt(gpacked_ref[window * TOK : (window + 1) * TOK, :], weight_ref[...])
        gtiles[window * WIN : (window + 1) * WIN] = value.reshape(WIN, LINE, D)
    gain_sum = jnp.zeros((1, D), f32)
    shift_sum = jnp.zeros((1, D), f32)
    for row in range(GH):
        unit, inverse = unit_of(img_ref[row].astype(f32))
        grad = join_row(row, gtiles)
        gain_sum += jnp.sum(grad * unit, axis=0, keepdims=True)
        shift_sum += jnp.sum(grad, axis=0, keepdims=True)
        out_ref[row] = (join_row(row, gbr_ref) + norm_back(grad, unit, inverse, gain)).astype(bf16)
    sums_ref[...] = jnp.concatenate([gain_sum, shift_sum, jnp.zeros((6, D), f32)], axis=0)


def params(steps=0):
    return pltpu.CompilerParams(
        vmem_limit_bytes=LIMIT, dimension_semantics=("arbitrary",) * steps if steps else None
    )


VMEM = pl.BlockSpec(memory_space=pltpu.VMEM)
SMEM = pl.BlockSpec(memory_space=pltpu.SMEM)


def whole(shape):
    return pl.BlockSpec(shape, lambda i: (0,) * len(shape))


def shaped(shape, dtype):
    return jax.ShapeDtypeStruct(shape, dtype)


def begin(images, vectors):
    return pl.pallas_call(
        begin_kernel,
        out_shape=shaped((WINDOWS * WIN, LINE, D), bf16),
        in_specs=[VMEM, VMEM],
        out_specs=VMEM,
        compiler_params=params(),
        cost_estimate=pl.CostEstimate(flops=30_000_000, bytes_accessed=4_000_000, transcendentals=0),
        name="begin",
    )(images, vectors)


def weigh(count, grad_out, rows, cols, valid):
    return pl.pallas_call(
        weight_kernel,
        out_shape=(shaped((DENSE, D), f32), shaped((DENSE, D), bf16)),
        in_specs=[SMEM] + [VMEM] * 4,
        out_specs=(VMEM, VMEM),
        compiler_params=params(),
        cost_estimate=pl.CostEstimate(flops=30_000_000, bytes_accessed=6_000_000, transcendentals=0),
        name="weigh",
    )(count, grad_out, rows, cols, valid)


def forward(tiles, weight, bias, out_w, out_b, table, hot):
    per = lambda *shape: pl.BlockSpec(shape, lambda i: (i,) + (0,) * (len(shape) - 1))
    return pl.pallas_call(
        forward_kernel,
        grid=(WINDOWS,),
        out_shape=(
            shaped((WINDOWS * TOK, 3 * D), bf16),
            shaped((WINDOWS * HEADS, TOK, TOK), bf16),
            shaped((WINDOWS * TOK, D), bf16),
            shaped((WINDOWS * TOK, D), f32),
        ),
        in_specs=[
            per(TOK, D),
            whole((D, 3 * D)),
            whole((1, 3 * D)),
            whole((D, D)),
            whole((1, D)),
            whole((128, 256)),
            whole((2, TOK, 128)),
        ],
        out_specs=(per(TOK, 3 * D), per(HEADS, TOK, TOK), per(TOK, D), per(TOK, D)),
        compiler_params=params(1),
        cost_estimate=pl.CostEstimate(flops=9_000_000_000, bytes_accessed=25_000_000, transcendentals=4_000_000),
        name="attend",
    )(tiles, weight, bias, out_w, out_b, table, hot)


def middle(images, branch, cot, gupd, vectors, up, up_bias, down):
    return pl.pallas_call(
        middle_kernel,
        grid=(FF // CHUNK,),
        out_shape=(
            shaped((GH, GW, D), bf16),
            shaped((WINDOWS * WIN, LINE, D), bf16),
            shaped((D, FF), bf16),
            shaped((FF, D), bf16),
            shaped((1, FF), f32),
            shaped((8, D), f32),
        ),
        in_specs=[
            whole((GH, GW, D)),
            whole((WINDOWS * WIN, LINE, D)),
            whole((DENSE, D)),
            whole((DENSE, D)),
            whole((8, D)),
            pl.BlockSpec((D, CHUNK), lambda i: (0, i)),
            pl.BlockSpec((1, CHUNK), lambda i: (0, i)),
            pl.BlockSpec((CHUNK, D), lambda i: (i, 0)),
        ],
        out_specs=(
            whole((GH, GW, D)),
            whole((WINDOWS * WIN, LINE, D)),
            pl.BlockSpec((D, CHUNK), lambda i: (0, i)),
            pl.BlockSpec((CHUNK, D), lambda i: (i, 0)),
            pl.BlockSpec((1, CHUNK), lambda i: (0, i)),
            whole((8, D)),
        ),
        scratch_shapes=[
            pltpu.VMEM((DENSE, D), f32),
            pltpu.VMEM((DENSE, D), bf16),
            pltpu.VMEM((DENSE, D), f32),
            pltpu.VMEM((DENSE, D), f32),
            pltpu.VMEM((DENSE, CHUNK), bf16),
            pltpu.VMEM((DENSE, CHUNK), bf16),
        ],
        compiler_params=params(1),
        cost_estimate=pl.CostEstimate(flops=28_000_000_000, bytes_accessed=36_000_000, transcendentals=6_000_000),
        name="feed",
    )(images, branch, cot, gupd, vectors, up, up_bias, down)


def backward(packed, soft, att, gbr, tiles, out_w, table, hot):
    per = lambda *shape: pl.BlockSpec(shape, lambda i: (i,) + (0,) * (len(shape) - 1))
    return pl.pallas_call(
        backward_kernel,
        grid=(WINDOWS,),
        out_shape=(
            shaped((WINDOWS * TOK, 3 * D), bf16),
            shaped((D, 3 * D), bf16),
            shaped((D, D), bf16),
            shaped((8, D), f32),
            shaped((256, 128), f32),
        ),
        in_specs=[
            per(TOK, 3 * D),
            per(HEADS, TOK, TOK),
            per(TOK, D),
            per(TOK, D),
            whole((WINDOWS * TOK, D)),
            whole((D, D)),
            whole((128, 256)),
            whole((2, TOK, 128)),
        ],
        out_specs=(per(TOK, 3 * D), whole((D, 3 * D)), whole((D, D)), whole((8, D)), whole((256, 128))),
        scratch_shapes=[
            pltpu.VMEM((WINDOWS * TOK, D), bf16),
            pltpu.VMEM((WINDOWS * TOK, D), bf16),
            pltpu.VMEM((WINDOWS * TOK, 3 * D), bf16),
            pltpu.VMEM((TOK, D), bf16),
        ],
        compiler_params=params(1),
        cost_estimate=pl.CostEstimate(flops=20_000_000_000, bytes_accessed=35_000_000, transcendentals=0),
        name="attend_back",
    )(packed, soft, att, gbr, tiles, out_w, table, hot)


def end(images, gbr, gpacked, weight, vectors):
    return pl.pallas_call(
        end_kernel,
        out_shape=(shaped((GH, GW, D), bf16), shaped((8, D), f32)),
        in_specs=[VMEM] * 5,
        out_specs=(VMEM, VMEM),
        scratch_shapes=[pltpu.VMEM((WINDOWS * WIN, LINE, D), f32)],
        compiler_params=params(),
        cost_estimate=pl.CostEstimate(flops=5_000_000_000, bytes_accessed=17_000_000, transcendentals=0),
        name="end",
    )(images, gbr, gpacked, weight, vectors)


def one_hot_keys(flip):
    token = np.arange(TOK)
    row, col = token // LINE, token % LINE
    lane = np.arange(128)
    group, local = lane // 32, lane % 32
    hot = []
    for head in range(2):
        mine = (group % 2 == head)[None, :]
        value = ((local[None, :] == row[:, None]) & (local < WIN)[None, :]) | (
            (local[None, :] - 16 == (13 - col if flip else col)[:, None]) & (col < WIN)[:, None]
        )
        value = np.where(mine & value, 1.0, 0.0)
        value[:, 14] = np.where(col >= WIN, -1e30, 0.0)
        hot.append(value)
    return jnp.asarray(np.stack(hot), dtype=bf16)


def pair_table(row_table, col_table, offset):
    rows = jnp.pad(row_table.T, ((0, 0), (0, 5)))
    cols = jnp.pad(col_table.T, ((0, 0), (0, 5)))
    zero = jnp.zeros_like(rows)

    def lanes(part):
        top = jnp.concatenate([part, zero, part, zero], axis=1)
        bottom = jnp.concatenate([zero, part, zero, part], axis=1)
        return jnp.concatenate([top, bottom], axis=0)

    return jnp.concatenate([lanes(rows), jnp.roll(lanes(cols), offset, axis=1)], axis=1)


def table_grads(total):
    rows = total[:128]
    cols = jnp.roll(total[128:], -16, axis=0)

    def pick(part):
        part = part.reshape(4, 32, 2, HD)
        value = part[0, :, 0] + part[1, :, 1] + part[2, :, 0] + part[3, :, 1]
        return value[:27]

    return pick(rows)[::-1], pick(cols)


def compute(gathered, images, grad_out, box_rows, box_cols, box_valid, box_count, row_table, col_table):
    (in_w, out_w, up_w, down_w, small) = gathered
    (qb, vb, ob, g1, s1, g2, s2, ub, db) = small
    image = images[0]
    vectors = jnp.stack([g1, s1, g2, s2, db, ob, qb, vb]).astype(f32)
    zero = jnp.zeros((1, D), f32)
    bias = jnp.concatenate([vectors[6:7], zero, vectors[7:8]], axis=1)
    table = pair_table(row_table[::-1], col_table[::-1], 3)
    table_back = pair_table(row_table[::-1], col_table, 16)
    hot = one_hot_keys(False)
    hot_back = one_hot_keys(True)
    tiles = begin(image, vectors).reshape(WINDOWS * TOK, D)
    cot, gupd = weigh(box_count, grad_out[0], box_rows[0], box_cols[0], box_valid.reshape(NBOX, 1))
    packed, soft, att, branch = forward(tiles, in_w, bias, out_w, vectors[5:6], table, hot)
    block_out, gbr, gup, gdown, gupb, sums2 = middle(
        image, branch.reshape(WINDOWS * WIN, LINE, D), cot, gupd, vectors, up_w, ub.astype(f32)[None], down_w
    )
    gpacked, gin, gout, gbias, gtab = backward(
        packed, soft, att, gbr.reshape(WINDOWS * TOK, D), tiles, out_w, table_back, hot_back
    )
    image_grad, sums1 = end(image, gbr, gpacked, in_w, vectors)
    row_grad, col_grad = table_grads(gtab)
    return (
        block_out[None],
        image_grad[None],
        gin,
        gout,
        gup,
        gdown,
        (gbias[0], gbias[1], sums2[2], sums1[0], sums1[1], sums2[0], sums2[1], gupb[0], sums2[3]),
        row_grad,
        col_grad,
    )


AXES = ("dp", "fsdp")


def gather(x):
    return lax.all_gather(x, AXES, axis=0, tiled=True)


def scatter(x):
    return lax.psum_scatter(x, AXES, scatter_dimension=0, tiled=True)


def local(
    images,
    grad_out,
    box_rows,
    box_cols,
    box_valid,
    box_count,
    in_weight,
    query_bias,
    value_bias,
    out_weight,
    out_bias,
    first_gain,
    first_shift,
    second_gain,
    second_shift,
    up_weight,
    up_bias,
    down_weight,
    down_bias,
    row_table,
    col_table,
):
    own = in_weight.shape[0]
    vectors = [query_bias, value_bias, out_bias, first_gain, first_shift, second_gain, second_shift, down_bias]
    columns = jnp.concatenate([jnp.stack(vectors, axis=1), up_bias.reshape(own, 4)], axis=1)
    columns = jnp.pad(columns, ((0, 0), (0, 128 - 12)))
    first = gather(jnp.concatenate([columns, in_weight, out_weight], axis=1))
    up_w = gather(up_weight)
    down_w = gather(down_weight)
    small = first[:, :12]
    flat = small[:, :8].T
    small = (flat[0], flat[1], flat[2], flat[3], flat[4], flat[5], flat[6], small[:, 8:].reshape(FF), flat[7])
    in_w = first[:, 128 : 128 + 3 * D]
    out_w = first[:, 128 + 3 * D :]
    block_out, image_grad, gin, gout, gup, gdown, grads, row_grad, col_grad = compute(
        (in_w, out_w, up_w, down_w, small), images, grad_out, box_rows, box_cols, box_valid, box_count, row_table, col_table
    )
    gup = scatter(gup).astype(f32)
    gdown = scatter(gdown).astype(f32)
    attention = scatter(jnp.concatenate([gin, gout], axis=1)).astype(f32)
    flat = jnp.concatenate([g for g in grads] + [row_grad.reshape(-1), col_grad.reshape(-1)])
    flat = lax.psum(flat, AXES)
    index = lax.axis_index(AXES)
    out = []
    at = 0
    for g in grads:
        size = g.shape[0]
        part = size // (D // own)
        out.append(lax.dynamic_slice(flat, (at + index * part,), (part,)))
        at += size
    table = 27 * HD
    row_grad = flat[at : at + table].reshape(27, HD)
    col_grad = flat[at + table : at + 2 * table].reshape(27, HD)
    return (
        block_out,
        image_grad,
        attention[:, : 3 * D],
        out[0],
        out[1],
        attention[:, 3 * D :],
        out[2],
        out[3],
        out[4],
        out[5],
        out[6],
        gup,
        out[7],
        gdown,
        out[8],
        row_grad,
        col_grad,
    )


def solution(mesh):
    rows = P(AXES)
    return jax.shard_map(
        local,
        mesh=mesh,
        in_specs=(rows,) * 19 + (P(), P()),
        out_specs=(rows,) * 15 + (P(), P()),
        check_vma=False,
    )
```

```python
import functools

import jax
import jax.numpy as jnp
import numpy as np
from jax import lax
from jax.experimental import pallas as pl
from jax.experimental.pallas import tpu as pltpu
from jax.sharding import PartitionSpec as P

D = 768
HEADS = 12
HD = 64
FF = 3072
WIN = 14
GH = 26
GW = 38
NBOX = 300
ACROSS = 3
WINDOWS = 6
LINE = 16
TOK = WIN * LINE
REAL = GH * GW
DENSE = 992
PAIRS = HEADS // 2
STARTS = (0, 14, 28)
WIDTHS = (14, 14, 10)
CHUNK = 768
CALLS = 3
SPLITS = ((0, 256), (256, 256), (512, 256), (768, 224))
epsilon = 1e-06
f32 = jnp.float32
bf16 = jnp.bfloat16
LIMIT = 60 * 1024 * 1024


def dot(a, b):
    return lax.dot_general(a, b, (((1,), (0,)), ((), ())), preferred_element_type=f32)


def dot_bt(a, b):
    return lax.dot_general(a, b, (((1,), (1,)), ((), ())), preferred_element_type=f32)


def dot_at(a, b):
    return lax.dot_general(a, b, (((0,), (0,)), ((), ())), preferred_element_type=f32)


def unit_of(x):
    center = x - jnp.mean(x, axis=-1, keepdims=True)
    inverse = lax.rsqrt(jnp.mean(center * center, axis=-1, keepdims=True) + epsilon)
    return center * inverse, inverse


def norm_back(grad, unit, inverse, gain):
    scaled = grad * gain
    return inverse * (
        scaled
        - jnp.mean(scaled, axis=-1, keepdims=True)
        - unit * jnp.mean(scaled * unit, axis=-1, keepdims=True)
    )


def place_of(row):
    return (row // WIN) * ACROSS, row % WIN


def spread_row(row, value, out_ref):
    first, place = place_of(row)
    for piece, (start, width) in enumerate(zip(STARTS, WIDTHS)):
        part = value[start : start + width]
        part = jnp.concatenate([part, jnp.zeros((LINE - width, part.shape[1]), part.dtype)], axis=0)
        out_ref[(first + piece) * WIN + place] = part.astype(out_ref.dtype)


def join_row(row, refs):
    first, place = place_of(row)
    each = WINDOWS // len(refs)
    parts = []
    for piece, width in enumerate(WIDTHS):
        window = first + piece
        line = refs[window // each][(window % each) * WIN + place]
        parts.append(line.astype(f32)[:width])
    return jnp.concatenate(parts, axis=0)


def begin_kernel(img_ref, *refs):
    unit_ref, flag_ref = refs[-2:]
    flag_ref[0] = 0
    unit_ref[...] = jnp.zeros_like(unit_ref)
    for row in range(GH):
        unit, _ = unit_of(img_ref[row].astype(f32))
        spread_row(row, unit, unit_ref)


def pair_tables(row_table, col_table, entry_row, entry_col):
    parts = []
    for table, place in ((row_table, entry_row), (col_table, entry_col)):
        pieces = jnp.zeros((128, 128), f32)
        entries = lax.broadcasted_iota(jnp.int32, (2 * WIN - 1, 128), 0)
        lane = lane_iota((2 * WIN - 1, 128))
        row = lax.broadcasted_iota(jnp.int32, (128, 128), 0)
        for head in range(2):
            where = place(entries) + 32 * head
            pick = ((lane - where) % 64) == 0
            spread = dot_at(table, jnp.where(pick, 1.0, 0.0).astype(bf16))
            both = jnp.concatenate([spread, spread], axis=0)
            pieces = jnp.where((row < HD) == (head == 0), both, pieces)
        parts.append(pieces)
    return jnp.concatenate(parts, axis=1).astype(bf16)


def weight_kernel(count_ref, grad_ref, rows_ref, cols_ref, valid_ref, rowt_ref, colt_ref, *refs):
    cot_ref, upd_ref, table_ref, back_ref, flag_ref = refs[-5:]
    flag_ref[0] = 0
    table_ref[...] = pair_tables(rowt_ref[...], colt_ref[...], lambda e: 26 - e, lambda e: 29 - e)
    back_ref[...] = pair_tables(rowt_ref[...], colt_ref[...], lambda e: 26 - e, lambda e: 16 + e)
    slot = lax.broadcasted_iota(jnp.int32, (NBOX, 1), 0)
    live = (slot < count_ref[0]) & (valid_ref[...] == 1)
    rows = rows_ref[...]
    cols = cols_ref[...]
    top = jnp.minimum(rows[:, 0:1], rows[:, 1:2])
    low = jnp.maximum(rows[:, 0:1], rows[:, 1:2])
    left = jnp.minimum(cols[:, 0:1], cols[:, 1:2])
    right = jnp.maximum(cols[:, 0:1], cols[:, 1:2])
    grid_r = lax.broadcasted_iota(jnp.int32, (NBOX, GH), 1)
    grid_c = lax.broadcasted_iota(jnp.int32, (NBOX, GW), 1)
    in_rows = jnp.where((grid_r >= top) & (grid_r < low) & live, 1.0, 0.0)
    in_cols = jnp.where((grid_c >= left) & (grid_c < right), 1.0, 0.0)
    inside = dot_at(in_cols.astype(bf16), in_rows.astype(bf16))
    total = jnp.sum(jnp.where(live, 1.0, 0.0))
    weight = 1.0 + 2.0 * inside / jnp.maximum(total, 1.0)
    for row in range(GH):
        cot_ref[row * GW : (row + 1) * GW, :] = grad_ref[row].astype(f32) * weight[:, row : row + 1]
    cot_ref[REAL:, :] = jnp.zeros((DENSE - REAL, D), f32)
    upd_ref[...] = cot_ref[...].astype(bf16)


def lane_iota(shape):
    return lax.broadcasted_iota(jnp.int32, shape, len(shape) - 1)


def position_terms(queries, table):
    both = dot(queries, table)
    row_part = both[:, :128].reshape(WIN, LINE, 128)
    col_part = both[:, 128:].reshape(WIN, LINE, 128)
    lane = lane_iota((LINE, 128))
    local = lane % 32
    out = []
    for place in range(WIN):
        rolled_r = pltpu.roll(row_part[place], (place - 13) % 128, 1)
        rolled_c = pltpu.roll(col_part[place], 0, 1, stride=1, stride_axis=0)
        value = jnp.where(local < 16, rolled_r, rolled_c)
        high = value.astype(bf16).astype(f32)
        value = jnp.where(lane < 64, high, value - high)
        value = jnp.where(lane == 14, 1.0, value)
        out.append(value)
    return jnp.concatenate(out, axis=0).astype(bf16)


def keep_head(value, head):
    lane = lane_iota(value.shape)
    return jnp.where((lane < HD) == (head == 0), value, jnp.zeros_like(value))


def forward_kernel(call, unit_ref, one_ref, two_ref, table_ref, hot_ref, *refs):
    if call == 0:
        core_ref, one_half, two_half = unit_ref, one_ref, two_ref
        one_other, two_other, unit_ref, table_ref, hot_ref = table_ref, hot_ref, *refs[:3]
        refs, (one_ref, two_ref, sems) = refs[:-3], refs[-3:]
    tiles_ref, packed_ref, soft_ref, att_ref, branch_ref, vec_ref, flag_ref = refs[-7:]
    step = pl.program_id(0)

    @pl.when(step == 0)
    def _():
        if call == 0:
            core = core_ref[1]
            made = []
            for i, (half, whole_ref, place) in enumerate(
                [
                    (one_half, one_ref, core),
                    (two_half, two_ref, core),
                    (one_other, one_ref, 1 - core),
                    (two_other, two_ref, 1 - core),
                ]
            ):
                for y in range(2):
                    here = pl.ds(pl.multiple_of((2 * y + place) * (D // 4), D // 4), D // 4)
                    copy = pltpu.make_async_copy(half.at[y], whole_ref.at[here, :], sems.at[2 * i + y])
                    copy.start()
                    made.append(copy)
            for copy in made:
                copy.wait()
        vec_ref[...] = one_ref[:, :128].astype(f32).T[:16]
        flag_ref[0] = 0

    window = call * (WINDOWS // CALLS) + step
    token = lax.broadcasted_iota(jnp.int32, (TOK, 1), 0)
    row_limit = jnp.where(window < ACROSS, WIN, GH - WIN)
    col_limit = jnp.where(window % ACROSS == ACROSS - 1, WIDTHS[2], WIN)
    valid = (token // LINE < row_limit) & (token % LINE < col_limit)
    tiles_ref[...] = (unit_ref[...] * vec_ref[3:4, :] + jnp.where(valid, vec_ref[4:5, :], 0.0)).astype(bf16)
    tiles = tiles_ref[...]
    packed_ref[:, :D] = (dot(tiles, one_ref[:, 128 : 128 + D]) + vec_ref[0:1, :]).astype(bf16)
    packed_ref[:, D : 2 * D] = dot(tiles, one_ref[:, 128 + D :]).astype(bf16)
    packed_ref[:, 2 * D :] = (dot(tiles, two_ref[:, :D]) + vec_ref[1:2, :]).astype(bf16)
    for pair in range(PAIRS):
        at = pair * 128
        queries = packed_ref[:, at : at + 128]
        keys = packed_ref[:, D + at : D + at + 128]
        values = packed_ref[:, 2 * D + at : 2 * D + at + 128]
        left = jnp.concatenate([queries, position_terms(queries, table_ref[...])], axis=1)
        parts = []
        for head in range(2):
            scaled = (keep_head(keys.astype(f32), head) * 0.125).astype(bf16)
            right = jnp.concatenate([scaled, hot_ref[head]], axis=1)
            scores = dot_bt(left, right)
            power = jnp.exp(scores - jnp.max(scores, axis=-1, keepdims=True))
            soft = (power * (1.0 / jnp.sum(power, axis=-1, keepdims=True))).astype(bf16)
            soft_ref[2 * pair + head] = soft
            parts.append(dot(soft, values))
        lane = lane_iota((TOK, 128))
        att_ref[:, at : at + 128] = jnp.where(lane < HD, parts[0], parts[1]).astype(bf16)
    branch_ref[...] = dot(att_ref[...], two_ref[:, D:]) + vec_ref[2:3, :]


def backward_kernel(packed_ref, soft_ref, att_ref, gbr_ref, two_ref, table_ref, hot_ref, *refs):
    gpacked_ref, gbias_ref, gtab_ref, flag_ref, gatt_ref = refs[-5:]

    @pl.when(pl.program_id(0) == 0)
    def _():
        flag_ref[0] = 0
        gbias_ref[...] = jnp.zeros_like(gbias_ref)
        gtab_ref[...] = jnp.zeros_like(gtab_ref)

    gatt_ref[...] = dot_bt(gbr_ref[...], two_ref[:, D:]).astype(bf16)
    lane = lane_iota((LINE, 128))
    local = lane % 32
    wide = lane_iota((TOK, 128))
    for pair in range(PAIRS):
        at = pair * 128
        queries = packed_ref[:, at : at + 128]
        keys = packed_ref[:, D + at : D + at + 128]
        values = packed_ref[:, 2 * D + at : 2 * D + at + 128]
        gatt = gatt_ref[:, at : at + 128]
        product = gatt.astype(f32) * att_ref[:, at : at + 128].astype(f32)
        left = []
        right = []
        gvalues = []
        gkeys = []
        for head in range(2):
            soft = soft_ref[2 * pair + head]
            delta = jnp.sum(keep_head(product, head), axis=-1, keepdims=True)
            gprobs = dot_bt(gatt, keep_head(values.astype(f32), head).astype(bf16))
            gscores = (soft.astype(f32) * (gprobs - delta)).astype(bf16)
            scaled = (keep_head(keys.astype(f32), head) * 0.125).astype(bf16)
            left.append(gscores)
            right.append(jnp.concatenate([scaled, hot_ref[head]], axis=1))
            gvalues.append(dot_at(soft, gatt))
            gkeys.append(dot_at(gscores, queries))
        both = dot(left[0], right[0]) + dot(left[1], right[1])
        terms = both[:, 128:].reshape(WIN, LINE, 128)
        rolled = []
        for place in range(WIN):
            value = terms[place]
            high = value.astype(bf16).astype(f32)
            value = jnp.where(lane < 64, high, value - high)
            row_part = jnp.where(local < WIN, value, 0.0)
            col_part = jnp.where((local >= 16) & (local < 16 + WIN), value, 0.0)
            row_part = pltpu.roll(row_part, 13 - place, 1)
            col_part = pltpu.roll(col_part, 0, 1, stride=1, stride_axis=0)
            rolled.append(jnp.concatenate([row_part, col_part], axis=1))
        rolled = jnp.concatenate(rolled, axis=0).astype(bf16)
        gqueries = both[:, :128] + dot_bt(rolled, table_ref[...])
        gtab_ref[...] += dot_at(rolled, queries)
        gq = gqueries.astype(bf16)
        gk = (jnp.where(wide < HD, gkeys[0], gkeys[1]) * 0.125).astype(bf16)
        gv = jnp.where(wide < HD, gvalues[0], gvalues[1]).astype(bf16)
        gpacked_ref[:, at : at + 128] = gq
        gpacked_ref[:, D + at : D + at + 128] = gk
        gpacked_ref[:, 2 * D + at : 2 * D + at + 128] = gv
        gbias_ref[0:1, at : at + 128] += jnp.sum(gq.astype(f32), axis=0, keepdims=True)
        gbias_ref[1:2, at : at + 128] += jnp.sum(gv.astype(f32), axis=0, keepdims=True)


def halve(core, value, keep_ref, send_ref, at):
    size = value.shape[0] // 4

    def put(first, second):
        for y in range(2):
            first[y * size : (y + 1) * size, at] = value[2 * y * size : (2 * y + 1) * size]
            second[y * size : (y + 1) * size, at] = value[(2 * y + 1) * size : (2 * y + 2) * size]

    @pl.when(core == 0)
    def _():
        put(keep_ref, send_ref)

    @pl.when(core == 1)
    def _():
        put(send_ref, keep_ref)


def attention_weights_kernel(core_ref, *refs):
    keep_ref, send_ref, flag_ref, gpacked_all, tiles_all = refs[-5:]
    flag_ref[0] = 0
    size = WINDOWS * TOK // CALLS
    for i in range(CALLS):
        gpacked_all[i * size : (i + 1) * size, :] = refs[2 * i][...]
        tiles_all[i * size : (i + 1) * size, :] = refs[2 * i + 1][...]
    for part in range(0, 3 * D, D):
        value = dot_at(tiles_all[...], gpacked_all[:, part : part + D]).astype(bf16)
        halve(core_ref[0], value, keep_ref, send_ref, slice(part, part + D))


def gelu_parts(hidden):
    size = jnp.abs(hidden)
    power = jnp.exp(hidden * hidden * -0.5)
    denominator = 1.0 + (0.3275911 * 0.7071067811865476) * size
    near = pl.reciprocal(denominator, approx=True)
    near = near * (2.0 - denominator * near)
    series = near * (
        0.254829592
        + near * (-0.284496736 + near * (1.421413741 + near * (-1.453152027 + near * 1.061405429)))
    )
    tail = 0.5 * series * power
    normal = jnp.where(hidden >= 0, 1.0 - tail, tail)
    return hidden * normal, normal + hidden * power * 0.3989422804014327


def middle_kernel(
    core_ref,
    img_ref,
    cot_ref,
    gupd_ref,
    vec_ref,
    up_ref,
    down_ref,
    *refs,
):
    branch_refs = refs[:CALLS]
    att_refs = refs[CALLS : 2 * CALLS]
    out_ref, gbr_ref, gupk_ref, gups_ref, gdownk_ref, gdowns_ref, gupb_ref, sums_ref = refs[2 * CALLS : 2 * CALLS + 8]
    mid, normed, update, gnorm, active, ghidden = refs[2 * CALLS + 8 :]
    step = pl.program_id(0)
    gain = vec_ref[5:6, :]
    shift = vec_ref[6:7, :]

    @pl.when(step == 0)
    def _():
        for row in range(GH):
            mid[row * GW : (row + 1) * GW, :] = img_ref[row].astype(f32) + join_row(row, branch_refs)
        mid[REAL:, :] = jnp.zeros((DENSE - REAL, D), f32)
        update[...] = jnp.zeros_like(update)
        gnorm[...] = jnp.zeros_like(gnorm)

        def chunk(index, carry):
            here = pl.ds(pl.multiple_of(index * 32, 32), 32)
            unit, _ = unit_of(mid[here, :])
            normed[here, :] = (unit * gain + shift).astype(bf16)
            return carry

        lax.fori_loop(0, DENSE // 32, chunk, 0)

    @pl.when(step < FF // CHUNK)
    def _():
        up_bias = vec_ref[pl.ds(8 + step, 1), :]
        for start, size in SPLITS:
            here = slice(start, start + size)
            hidden = dot(normed[here, :], up_ref[...]) + up_bias
            gactive = dot_bt(gupd_ref[here, :], down_ref[...])
            act, slope = gelu_parts(hidden)
            act = act.astype(bf16)
            gh = (gactive * slope).astype(bf16)
            active[here, :] = act
            ghidden[here, :] = gh
            update[here, :] += dot(act, down_ref[...])
            gnorm[here, :] += dot_bt(gh, up_ref[...])
        gupb_ref[pl.ds(step, 1), :] = jnp.sum(ghidden[...].astype(f32), axis=0, keepdims=True)
        gdown = dot_at(active[...], gupd_ref[...]).astype(bf16)
        halve(core_ref[0], gdown, gdownk_ref, gdowns_ref, slice(None))
        gup = dot_at(normed[...], ghidden[...]).astype(bf16)
        halve(core_ref[0], gup, gupk_ref, gups_ref, slice(None))

    @pl.when(step == FF // CHUNK)
    def _():
        down_bias = vec_ref[7:8, :]
        for row in range(GH):
            here = slice(row * GW, (row + 1) * GW)
            out_ref[row] = (mid[here, :] + update[here, :] + down_bias).astype(bf16)

        def chunk(index, carry):
            here = pl.ds(pl.multiple_of(index * 32, 32), 32)
            unit, inverse = unit_of(mid[here, :])
            grad = gnorm[here, :]
            cot = cot_ref[here, :]
            result = cot + norm_back(grad, unit, inverse, gain)
            rounded = result.astype(bf16).astype(f32)
            update[here, :] = rounded
            gain_sum, shift_sum, branch_sum, bias_sum = carry
            return (
                gain_sum + jnp.sum((grad * unit).reshape(4, 8, D), axis=0),
                shift_sum + jnp.sum(grad.reshape(4, 8, D), axis=0),
                branch_sum + jnp.sum(rounded.reshape(4, 8, D), axis=0),
                bias_sum + jnp.sum(cot.astype(bf16).astype(f32).reshape(4, 8, D), axis=0),
            )

        zero = jnp.zeros((8, D), f32)
        sums = lax.fori_loop(0, DENSE // 32, chunk, (zero,) * 4)
        sums_ref[...] = jnp.concatenate(
            [jnp.sum(s, axis=0, keepdims=True) for s in sums] + [jnp.zeros((4, D), f32)], axis=0
        )
        gbr_ref[...] = jnp.zeros_like(gbr_ref)
        for row in range(GH):
            spread_row(row, update[row * GW : (row + 1) * GW, :], gbr_ref)
        each = WINDOWS * WIN // CALLS
        gout = jnp.zeros((D, D), f32)
        for i, att_ref in enumerate(att_refs):
            gout += dot_at(att_ref[...], gbr_ref[i * each : (i + 1) * each].reshape(each * LINE, D))
        halve(core_ref[0], gout.astype(bf16), gupk_ref, gups_ref, slice(None))


def end_kernel(img_ref, gbr_ref, one_ref, two_ref, vec_ref, *refs):
    gpacked_refs = refs[:CALLS]
    out_ref, sums_ref, gtiles = refs[-3:]
    gain = vec_ref[3:4, :]
    each = WINDOWS // CALLS
    for window in range(WINDOWS):
        here = slice((window % each) * TOK, (window % each + 1) * TOK)
        gpacked_ref = gpacked_refs[window // each]
        value = dot_bt(gpacked_ref[here, : 2 * D], one_ref[:, 128:]) + dot_bt(gpacked_ref[here, 2 * D :], two_ref[:, :D])
        gtiles[window * WIN : (window + 1) * WIN] = value.reshape(WIN, LINE, D)
    gain_sum = jnp.zeros((1, D), f32)
    shift_sum = jnp.zeros((1, D), f32)
    for row in range(GH):
        unit, inverse = unit_of(img_ref[row].astype(f32))
        grad = join_row(row, [gtiles])
        gain_sum += jnp.sum(grad * unit, axis=0, keepdims=True)
        shift_sum += jnp.sum(grad, axis=0, keepdims=True)
        out_ref[row] = (join_row(row, [gbr_ref]) + norm_back(grad, unit, inverse, gain)).astype(bf16)
    sums_ref[...] = jnp.concatenate([gain_sum, shift_sum, jnp.zeros((6, D), f32)], axis=0)


def pack_kernel(eight_ref, upb_ref, weight_ref, out_ref):
    own = weight_ref.shape[0]
    flat = upb_ref[...].astype(f32)
    rows = [eight_ref[...].astype(f32)] + [flat[:, own * i : own * (i + 1)] for i in range(4)]
    rows = jnp.concatenate(rows, axis=0)
    rows = jnp.concatenate([rows, jnp.zeros((12, 128 - own), f32)], axis=1)
    square = jnp.concatenate([rows, jnp.zeros((116, 128), f32)], axis=0)
    out_ref[:, :128] = square.T[:own].astype(bf16)
    out_ref[:, 128:] = weight_ref[:, : 2 * D]


def regroup(value, own, back=False):
    count = value.shape[1] // (4 * own)
    parts = []
    for i in range(count if back else 4):
        for j in range(4 if back else count):
            at = (j * count + i) * own if back else (4 * j + i) * own
            parts.append(value[:, at : at + own])
    return jnp.concatenate(parts, axis=1)


def pack_feed_kernel(up_ref, down_ref, out_ref):
    own = up_ref.shape[0]
    out_ref[:, :FF] = regroup(up_ref[...].astype(f32), own).astype(bf16)
    for k in range(4):
        part = down_ref[...].astype(f32)[k * own : (k + 1) * own]
        out_ref[:, FF + k * D : FF + (k + 1) * D] = part.astype(bf16)


def unpack_feed_kernel(first_ref, first_recv_ref, second_ref, second_recv_ref, up_ref, out_ref, down_ref):
    own = up_ref.shape[0]
    first = first_ref[...] + first_recv_ref[...].astype(f32)
    up_ref[...] = regroup(first[:, :FF], own, back=True)
    out_ref[...] = first[:, FF:]
    second = second_ref[...] + second_recv_ref[...].astype(f32)
    for k in range(4):
        down_ref[k * own : (k + 1) * own, :] = second[:, k * D : (k + 1) * D]


def params(steps=0):
    return pltpu.CompilerParams(
        vmem_limit_bytes=LIMIT, dimension_semantics=("arbitrary",) * steps if steps else None
    )


VMEM = pl.BlockSpec(memory_space=pltpu.VMEM)
SMEM = pl.BlockSpec(memory_space=pltpu.SMEM)


def whole(shape):
    return pl.BlockSpec(shape, lambda i: (0,) * len(shape))


def shaped(shape, dtype):
    return jax.ShapeDtypeStruct(shape, dtype)


def pack_feed(up, down):
    own = up.shape[0]
    return pl.pallas_call(
        pack_feed_kernel,
        out_shape=shaped((own, 2 * FF), bf16),
        in_specs=[VMEM] * 2,
        out_specs=VMEM,
        compiler_params=params(),
        name="pack_feed",
    )(up, down)


def unpack_feed(first, second):
    flat = [value.reshape(value.shape[-2:]) for value in first + second]
    own = flat[0].shape[0]
    return pl.pallas_call(
        unpack_feed_kernel,
        out_shape=(shaped((own, FF), f32), shaped((own, D), f32), shaped((4 * own, D), f32)),
        in_specs=[VMEM] * 4,
        out_specs=(VMEM,) * 3,
        compiler_params=params(),
        name="unpack_feed",
    )(*flat)


FLAG = pl.BlockSpec(memory_space=pltpu.SMEM)
ANY = pl.BlockSpec(memory_space=pl.ANY)
flag_shape = jax.ShapeDtypeStruct((1,), jnp.int32)


def begin(images, before):
    return pl.pallas_call(
        begin_kernel,
        out_shape=(shaped((WINDOWS * WIN, LINE, D), f32), flag_shape),
        in_specs=[VMEM] + [ANY] * len(before),
        out_specs=(VMEM, FLAG),
        compiler_params=params(),
        cost_estimate=pl.CostEstimate(flops=30_000_000, bytes_accessed=6_000_000, transcendentals=0),
        name="begin",
    )(images, *before)


def weigh(count, grad_out, rows, cols, valid, row_table, col_table, before):
    return pl.pallas_call(
        weight_kernel,
        out_shape=(
            shaped((DENSE, D), f32),
            shaped((DENSE, D), bf16),
            shaped((128, 256), bf16),
            shaped((128, 256), bf16),
            flag_shape,
        ),
        in_specs=[SMEM] + [VMEM] * 6 + [ANY] * len(before),
        out_specs=(VMEM,) * 4 + (FLAG,),
        compiler_params=params(),
        cost_estimate=pl.CostEstimate(flops=30_000_000, bytes_accessed=6_000_000, transcendentals=0),
        name="weigh",
    )(count, grad_out, rows, cols, valid, row_table, col_table, *before)


def forward(call, unit, weights, table, hot, before=()):
    per = lambda *shape: pl.BlockSpec(shape, lambda i: (i,) + (0,) * (len(shape) - 1))
    each = WINDOWS // CALLS
    both = [((D, 128 + 2 * D), bf16), ((D, 2 * D), bf16)]
    if call == 0:
        specs = [SMEM] + [ANY] * 4
        more_shapes = tuple(shaped(*b) for b in both)
        more_specs = tuple(whole(b[0]) for b in both)
        scratch = [pltpu.SemaphoreType.DMA((8,))]
    else:
        specs, more_shapes, more_specs, scratch = [], (), (), []
    tail = [whole(b[0]) for b in both] if call else []
    return pl.pallas_call(
        functools.partial(forward_kernel, call),
        grid=(each,),
        out_shape=(
            shaped((each * TOK, D), bf16),
            shaped((each * TOK, 3 * D), bf16),
            shaped((each * HEADS, TOK, TOK), bf16),
            shaped((each * TOK, D), bf16),
            shaped((each * TOK, D), f32),
            shaped((16, D), f32),
            flag_shape,
        )
        + more_shapes,
        in_specs=specs
        + [pl.BlockSpec((TOK, D), lambda i: (call * each + i, 0))]
        + tail
        + [whole((128, 256)), whole((2, TOK, 128))]
        + [ANY] * len(before),
        out_specs=(per(TOK, D), per(TOK, 3 * D), per(HEADS, TOK, TOK), per(TOK, D), per(TOK, D), whole((16, D)), FLAG)
        + more_specs,
        scratch_shapes=scratch,
        compiler_params=params(1),
        cost_estimate=pl.CostEstimate(flops=10_000_000_000, bytes_accessed=9_000_000, transcendentals=1_300_000),
        name="attend",
    )(*(list(weights) + [unit] if call == 0 else [unit] + list(weights)), table, hot, *before)


def middle(core, images, cot, gupd, vec, weights, branches, attended):
    steps = FF // CHUNK
    at = lambda i: jnp.minimum(i, steps - 1)
    return pl.pallas_call(
        middle_kernel,
        grid=(steps + 1,),
        out_shape=(
            shaped((GH, GW, D), bf16),
            shaped((WINDOWS * WIN, LINE, D), bf16),
            shaped((D // 2, FF + D), bf16),
            shaped((D // 2, FF + D), bf16),
            shaped((D // 2, FF), bf16),
            shaped((D // 2, FF), bf16),
            shaped((8, D), f32),
            shaped((8, D), f32),
        ),
        in_specs=[
            SMEM,
            whole((GH, GW, D)),
            whole((DENSE, D)),
            whole((DENSE, D)),
            whole((16, D)),
            pl.BlockSpec((D, CHUNK), lambda i: (0, at(i))),
            pl.BlockSpec((D, CHUNK), lambda i: (0, steps + at(i))),
        ]
        + [whole((WINDOWS // CALLS * WIN, LINE, D))] * CALLS
        + [whole((WINDOWS // CALLS * TOK, D))] * CALLS,
        out_specs=(
            whole((GH, GW, D)),
            whole((WINDOWS * WIN, LINE, D)),
            pl.BlockSpec((D // 2, CHUNK), lambda i: (0, i)),
            pl.BlockSpec((D // 2, CHUNK), lambda i: (0, i)),
            pl.BlockSpec((D // 2, CHUNK), lambda i: (0, at(i))),
            pl.BlockSpec((D // 2, CHUNK), lambda i: (0, at(i))),
            whole((8, D)),
            whole((8, D)),
        ),
        scratch_shapes=[
            pltpu.VMEM((DENSE, D), f32),
            pltpu.VMEM((DENSE, D), bf16),
            pltpu.VMEM((DENSE, D), f32),
            pltpu.VMEM((DENSE, D), f32),
            pltpu.VMEM((DENSE, CHUNK), bf16),
            pltpu.VMEM((DENSE, CHUNK), bf16),
        ],
        compiler_params=params(1),
        cost_estimate=pl.CostEstimate(flops=50_000_000_000, bytes_accessed=36_000_000, transcendentals=6_000_000),
        name="feed",
    )(core, images, cot, gupd, vec, weights, weights, *branches, *attended)


def backward(call, packed, soft, att, gbr, two, table, hot, before=()):
    per = lambda *shape: pl.BlockSpec(shape, lambda i: (i,) + (0,) * (len(shape) - 1))
    each = WINDOWS // CALLS
    return pl.pallas_call(
        backward_kernel,
        grid=(each,),
        out_shape=(
            shaped((each * TOK, 3 * D), bf16),
            shaped((8, D), f32),
            shaped((256, 128), f32),
            flag_shape,
        ),
        in_specs=[
            per(TOK, 3 * D),
            per(HEADS, TOK, TOK),
            per(TOK, D),
            pl.BlockSpec((TOK, D), lambda i: (call * each + i, 0)),
            whole((D, 2 * D)),
            whole((128, 256)),
            whole((2, TOK, 128)),
        ]
        + [ANY] * len(before),
        out_specs=(per(TOK, 3 * D), whole((8, D)), whole((256, 128)), FLAG),
        scratch_shapes=[pltpu.VMEM((TOK, D), bf16)],
        compiler_params=params(1),
        cost_estimate=pl.CostEstimate(flops=12_000_000_000, bytes_accessed=9_000_000, transcendentals=0),
        name="attend_back",
    )(packed, soft, att, gbr, two, table, hot, *before)


def attention_weights(core, parts, before=()):
    size = WINDOWS * TOK // CALLS
    operands = [array for part in parts for array in part]
    return pl.pallas_call(
        attention_weights_kernel,
        grid=(1,),
        out_shape=(shaped((D // 2, 3 * D), bf16),) * 2 + (flag_shape,),
        in_specs=[SMEM] + [whole((size, 3 * D)), whole((size, D))] * CALLS + [ANY] * len(before),
        out_specs=(whole((D // 2, 3 * D)),) * 2 + (FLAG,),
        scratch_shapes=[pltpu.VMEM((WINDOWS * TOK, 3 * D), bf16), pltpu.VMEM((WINDOWS * TOK, D), bf16)],
        compiler_params=params(1),
        cost_estimate=pl.CostEstimate(flops=25_000_000_000, bytes_accessed=18_000_000, transcendentals=0),
        name="attend_weights",
    )(core, *operands, *before)


def end(images, gbr, one, two, vec, gpacked, before=()):
    return pl.pallas_call(
        end_kernel,
        out_shape=(shaped((GH, GW, D), bf16), shaped((8, D), f32)),
        in_specs=[VMEM] * (5 + CALLS) + [ANY] * len(before),
        out_specs=(VMEM, VMEM),
        scratch_shapes=[pltpu.VMEM((WINDOWS * WIN, LINE, D), f32)],
        compiler_params=params(),
        cost_estimate=pl.CostEstimate(flops=8_000_000_000, bytes_accessed=17_000_000, transcendentals=0),
        name="end",
    )(images, gbr, one, two, vec, *gpacked, *before)


def pack(eight, up_bias, weight):
    return pl.pallas_call(
        pack_kernel,
        out_shape=shaped((weight.shape[0], 128 + 2 * D), bf16),
        in_specs=[VMEM] * 3,
        out_specs=VMEM,
        compiler_params=params(),
        name="pack",
    )(eight, up_bias, weight)


def one_hot_keys(flip):
    token = np.arange(TOK)
    row, col = token // LINE, token % LINE
    lane = np.arange(128)
    group, local = lane // 32, lane % 32
    hot = []
    for head in range(2):
        mine = (group % 2 == head)[None, :]
        value = ((local[None, :] == row[:, None]) & (local < WIN)[None, :]) | (
            (local[None, :] - 16 == (13 - col if flip else col)[:, None]) & (col < WIN)[:, None]
        )
        value = np.where(mine & value, 1.0, 0.0)
        value[:, 14] = np.where(col >= WIN, -1e30, 0.0)
        hot.append(value)
    return jnp.asarray(np.stack(hot), dtype=bf16)


def table_grads(total):
    rows = total[:128]
    cols = jnp.roll(total[128:], -16, axis=0)

    def pick(part):
        part = part.reshape(4, 32, 2, HD)
        value = part[0, :, 0] + part[1, :, 1] + part[2, :, 0] + part[3, :, 1]
        return value[:27]

    return pick(rows)[::-1], pick(cols)


AXES = ("dp", "fsdp")


class Exchange:
    def __init__(self, dp, fsdp):
        self.count = dp * fsdp
        self.bits = []
        bit = self.count // 2
        while bit:
            self.bits.append(bit)
            bit //= 2
        place = lax.axis_index(AXES).astype(jnp.int32)
        self.place = place
        self.mine = [(place >> (bit.bit_length() - 1)) & 1 for bit in self.bits]
        self.places = jnp.stack(self.mine)
        last = len(self.bits) - 1
        low = list(range(last - 1, 1, -1))
        self.orders = ([0, last] + low, [last, 0] + low)

    def swap(self, value, at):
        bit = self.bits[at]
        return lax.ppermute(value, AXES, [(i, i ^ bit) for i in range(self.count)])

    def spread(self, value):
        return value.reshape((1,) * len(self.bits) + value.shape)

    def join(self, value, at, flag=None):
        other = self.swap(value, at)
        mine = self.mine[at] if flag is None else self.mine[at] + flag[0]
        return jnp.where(
            mine == 0, jnp.concatenate([value, other], axis=at), jnp.concatenate([other, value], axis=at)
        )

    def total_round(self, value, ats, flag):
        value = value + flag[0].astype(f32)
        masks = [self.bits[at] for at in ats]
        move = lambda mask: lax.ppermute(value, AXES, [(i, i ^ mask) for i in range(self.count)])
        if len(masks) == 1:
            return value + move(masks[0])
        return (value + move(masks[0])) + (move(masks[1]) + move(masks[0] | masks[1]))

    def tie(self, values, before):
        count = len(values)

        def kernel(*refs):
            pass

        return pl.pallas_call(
            kernel,
            out_shape=tuple(shaped(v.shape, v.dtype) for v in values),
            in_specs=[ANY] * (count + len(before)),
            out_specs=(ANY,) * count,
            input_output_aliases={i: i for i in range(count)},
            name="tie",
        )(*values, *before)

    def flat(self, value):
        return value.reshape((self.count * value.shape[-2], value.shape[-1]))

    def cut(self, keep, send):
        rows, columns = keep.shape
        shape = (2, 1) + (2,) * (len(self.bits) - 2) + (2 * rows // self.count, columns)
        return keep.reshape(shape), self.swap(send, 1).reshape(shape)

    def narrow(self, parts, before=()):
        shapes, operands, specs, outs, out_specs = [], [], [], [], []
        for (stay, recv), at, half in parts:
            shape = stay.shape
            rows = int(np.prod(shape[at + 1 : -1]))
            lead = int(np.prod(shape[:at]))
            columns = shape[-1] if half is None else shape[-1] // 2
            block = (lead, 2, rows, columns)
            for array in (stay, recv):
                operands.append(array.reshape(lead, 2, rows, shape[-1]))
                specs.append(pl.BlockSpec(block, lambda i, c=half or 0: (0, 0, 0, c)))
            for kind in (f32, bf16):
                outs.append(shaped((lead, rows, columns), kind))
                out_specs.append(whole((lead, rows, columns)))
            shapes.append(shape[:at] + (1,) + shape[at + 1 : -1] + (columns,))
        count = len(parts)
        ats = [at for _, at, _ in parts]

        def kernel(mine_ref, *refs):
            results = refs[-2 * count - 1 : -1]
            refs[-1][0] = 0
            for i, at in enumerate(ats):
                mine = mine_ref[at]
                first, second = refs[2 * i], refs[2 * i + 1]
                for ref, place in ((results[2 * i], mine), (results[2 * i + 1], 1 - mine)):
                    total = first[:, place].astype(f32) + second[:, place].astype(f32)
                    ref[...] = total.astype(ref.dtype)

        size = sum(int(np.prod(o.shape)) for o in operands)
        got = pl.pallas_call(
            kernel,
            grid=(1,),
            out_shape=tuple(outs) + (flag_shape,),
            in_specs=[SMEM] + specs + [ANY] * len(before),
            out_specs=tuple(out_specs) + (FLAG,),
            compiler_params=params(1),
            cost_estimate=pl.CostEstimate(flops=size, bytes_accessed=4 * size, transcendentals=0),
            name="narrow",
        )(self.places, *operands, *before)
        results = []
        for i, at in enumerate(ats):
            stay, leave = got[2 * i].reshape(shapes[i]), got[2 * i + 1].reshape(shapes[i])
            results.append((stay, self.swap(leave, at)))
        return results, [got[-1]]

    def close(self, part):
        total = part[0].astype(f32) + part[1].astype(f32)
        return total.reshape(total.shape[-2:])

def local(
    dp,
    fsdp,
    images,
    grad_out,
    box_rows,
    box_cols,
    box_valid,
    box_count,
    in_weight,
    query_bias,
    value_bias,
    out_weight,
    out_bias,
    first_gain,
    first_shift,
    second_gain,
    second_shift,
    up_weight,
    up_bias,
    down_weight,
    down_bias,
    row_table,
    col_table,
):
    links = Exchange(dp, fsdp)
    image = images[0]
    core = (lax.axis_index("dp") & 1).astype(jnp.int32).reshape(1)
    hot = one_hot_keys(False)
    hot_back = one_hot_keys(True)
    eight = jnp.stack(
        [query_bias, value_bias, out_bias, first_gain, first_shift, second_gain, second_shift, down_bias]
    )
    first, second = links.orders[0][::-1], links.orders[1][::-1]
    last = len(first)
    two = links.spread(jnp.concatenate([in_weight[:, 2 * D :], out_weight], axis=1))
    one = links.spread(pack(eight, up_bias[None], in_weight))
    feed_weights = lax.all_gather(pack_feed(up_weight, down_weight), AXES, axis=0, tiled=True)
    for step in range(last - 2):
        two = links.join(two, second[step])
        one = links.join(one, first[step])
    cot, gupd, table, table_back, flag = weigh(
        box_count, grad_out[0], box_rows[0], box_cols[0], box_valid.reshape(NBOX, 1), row_table, col_table, [two, one]
    )
    two = links.join(two, second[last - 2], flag)
    one = links.join(one, first[last - 2], flag)
    unit, flag = begin(image, [two, one])
    unit = unit.reshape(WINDOWS * TOK, D)
    two = links.join(two, second[last - 1], flag)
    one = links.join(one, first[last - 1], flag)
    halves = [h.reshape(2, D // 4, -1) for h in (one, two, links.swap(one, 1), links.swap(two, 1))]

    ahead = [forward(0, unit, [links.places] + halves, table, hot)]
    weights = one, two = ahead[0][7:]
    ahead += [forward(call, unit, weights, table, hot) for call in range(1, CALLS)]
    vec = ahead[0][5]
    lines = (WINDOWS // CALLS * WIN, LINE, D)
    block_out, gbr, gup_k, gup_s, gdown_k, gdown_s, gupb, sums2 = middle(
        core, image, cot, gupd, vec, feed_weights, [a[4].reshape(lines) for a in ahead], [a[3] for a in ahead]
    )

    first, second = links.orders
    gbr_flat = gbr.reshape(WINDOWS * TOK, D)
    feed = [links.cut(gup_k, gup_s), links.cut(gdown_k, gdown_s)]
    back = []
    flag = []
    for call, (_, packed, soft, att) in enumerate([a[:4] for a in ahead]):
        back.append(backward(call, packed, soft, att, gbr_flat, two, table_back, hot_back, flag))
        flag = [back[-1][3]]
        if call == 0:
            feed, flag = links.narrow(list(zip(feed, (first[0], second[0]), (None, None))), flag)
    gin_k, gin_s, flag = attention_weights(core, [(b[0], a[0]) for a, b in zip(ahead, back)], flag)
    feed, flag = links.narrow(list(zip(feed, (first[1], second[1]), (None, None))), [flag])
    gin = links.cut(gin_k, links.tie([gin_s], flag)[0])
    image_grad, sums1 = end(image, gbr, one, two, vec, [b[0] for b in back], flag)
    gbias = sum(b[1] for b in back)
    row_grad, col_grad = table_grads(sum(b[2] for b in back))
    tables = jnp.concatenate([row_grad, col_grad, jnp.zeros((6, HD), f32)], axis=0).reshape(5, D)
    vectors = jnp.concatenate(
        [gbias[:2], sums2[2:3], sums1[:2], sums2[:2], sums2[3:4], gupb[:4], tables, jnp.zeros((7, D), f32)], axis=0
    )
    gin = [(gin, first[0], 0), (gin, second[0], 1)]
    before = [sums1]
    rounds = [first[0], 1] + first[1:]
    rounds = [rounds[i : i + 2] for i in range(0, len(rounds), 2)]
    for step in range(last):
        parts = list(gin)
        if step + 2 < last:
            parts += list(zip(feed, (first[step + 2], second[step + 2]), (None, None)))
        done, before = links.narrow(parts, before)
        if step + 1 < last:
            gin = list(zip(done[:2], (first[step + 1], second[step + 1]), (None, None)))
        feed = done[2:] or feed
        if step < len(rounds):
            vectors = links.total_round(vectors, rounds[step], before[0])
    gin = jnp.concatenate([links.close(g) for g in done[:2]], axis=1)
    gup, gout, gdown = unpack_feed(*feed)
    own = in_weight.shape[0]
    out = lax.dynamic_slice(vectors, (0, links.place * own), (12, own))
    tables = vectors[12:17].reshape(60, HD)
    row_grad, col_grad = tables[:27], tables[27:54]
    return (
        block_out[None],
        image_grad[None],
        gin,
        out[0],
        out[1],
        gout,
        out[2],
        out[3],
        out[4],
        out[5],
        out[6],
        gup,
        out[8:].reshape(-1),
        gdown,
        out[7],
        row_grad,
        col_grad,
    )


def solution(mesh):
    rows = P(AXES)
    dp, fsdp = mesh.shape["dp"], mesh.shape["fsdp"]
    return jax.shard_map(
        lambda *args: local(dp, fsdp, *args),
        mesh=mesh,
        in_specs=(rows,) * 19 + (P(), P()),
        out_specs=(rows,) * 15 + (P(), P()),
        check_vma=False,
    )
```

```python
import functools

import jax
import jax.numpy as jnp
import numpy as np
from jax import lax
from jax.experimental import pallas as pl
from jax.experimental.pallas import tpu as pltpu
from jax.sharding import PartitionSpec as P

D = 768
HEADS = 12
HD = 64
FF = 3072
WIN = 14
GH = 26
GW = 38
NBOX = 300
ACROSS = 3
WINDOWS = 6
LINE = 16
TOK = WIN * LINE
REAL = GH * GW
DENSE = 992
HALF = DENSE // 2
PAIRS = HEADS // 2
STARTS = (0, 14, 28)
WIDTHS = (14, 14, 10)
CHUNK = 768
CALLS = (2, 4)
SPLITS = ((0, 256), (256, 256), (512, 256), (768, 224))
epsilon = 1e-06
f32 = jnp.float32
bf16 = jnp.bfloat16
LIMIT = 60 * 1024 * 1024


def dot(a, b):
    return lax.dot_general(a, b, (((1,), (0,)), ((), ())), preferred_element_type=f32)


def dot_bt(a, b):
    return lax.dot_general(a, b, (((1,), (1,)), ((), ())), preferred_element_type=f32)


def dot_at(a, b):
    return lax.dot_general(a, b, (((0,), (0,)), ((), ())), preferred_element_type=f32)


def unit_of(x):
    center = x - jnp.mean(x, axis=-1, keepdims=True)
    inverse = lax.rsqrt(jnp.mean(center * center, axis=-1, keepdims=True) + epsilon)
    return center * inverse, inverse


def norm_back(grad, unit, inverse, gain):
    scaled = grad * gain
    return inverse * (
        scaled
        - jnp.mean(scaled, axis=-1, keepdims=True)
        - unit * jnp.mean(scaled * unit, axis=-1, keepdims=True)
    )


def place_of(row):
    return (row // WIN) * ACROSS, row % WIN


def spread_row(row, value, out_ref):
    first, place = place_of(row)
    for piece, (start, width) in enumerate(zip(STARTS, WIDTHS)):
        part = value[start : start + width]
        part = jnp.concatenate([part, jnp.zeros((LINE - width, part.shape[1]), part.dtype)], axis=0)
        out_ref[(first + piece) * WIN + place] = part.astype(out_ref.dtype)


def join_row(row, ref):
    first, place = place_of(row)
    return jnp.concatenate(
        [ref[(first + piece) * WIN + place].astype(f32)[:width] for piece, width in enumerate(WIDTHS)], axis=0
    )


def begin_kernel(img_ref, *refs):
    unit_ref, flag_ref = refs[-2:]
    flag_ref[0] = 0
    unit_ref[...] = jnp.zeros_like(unit_ref)
    for row in range(GH):
        unit, _ = unit_of(img_ref[row].astype(f32))
        spread_row(row, unit, unit_ref)


def pair_tables(row_table, col_table, entry_row, entry_col):
    parts = []
    for table, place in ((row_table, entry_row), (col_table, entry_col)):
        pieces = jnp.zeros((128, 128), f32)
        entries = lax.broadcasted_iota(jnp.int32, (2 * WIN - 1, 128), 0)
        lane = lane_iota((2 * WIN - 1, 128))
        row = lax.broadcasted_iota(jnp.int32, (128, 128), 0)
        for head in range(2):
            where = place(entries) + 32 * head
            pick = ((lane - where) % 64) == 0
            spread = dot_at(table, jnp.where(pick, 1.0, 0.0).astype(bf16))
            both = jnp.concatenate([spread, spread], axis=0)
            pieces = jnp.where((row < HD) == (head == 0), both, pieces)
        parts.append(pieces)
    return jnp.concatenate(parts, axis=1).astype(bf16)


def weight_kernel(count_ref, grad_ref, rows_ref, cols_ref, valid_ref, rowt_ref, colt_ref, *refs):
    cot_ref, upd_ref, table_ref, back_ref, flag_ref = refs[-5:]
    flag_ref[0] = 0
    table_ref[...] = pair_tables(rowt_ref[...], colt_ref[...], lambda e: 26 - e, lambda e: 29 - e)
    back_ref[...] = pair_tables(rowt_ref[...], colt_ref[...], lambda e: 26 - e, lambda e: 16 + e)
    slot = lax.broadcasted_iota(jnp.int32, (NBOX, 1), 0)
    live = (slot < count_ref[0]) & (valid_ref[...] == 1)
    rows = rows_ref[...]
    cols = cols_ref[...]
    top = jnp.minimum(rows[:, 0:1], rows[:, 1:2])
    low = jnp.maximum(rows[:, 0:1], rows[:, 1:2])
    left = jnp.minimum(cols[:, 0:1], cols[:, 1:2])
    right = jnp.maximum(cols[:, 0:1], cols[:, 1:2])
    grid_r = lax.broadcasted_iota(jnp.int32, (NBOX, GH), 1)
    grid_c = lax.broadcasted_iota(jnp.int32, (NBOX, GW), 1)
    in_rows = jnp.where((grid_r >= top) & (grid_r < low) & live, 1.0, 0.0)
    in_cols = jnp.where((grid_c >= left) & (grid_c < right), 1.0, 0.0)
    inside = dot_at(in_cols.astype(bf16), in_rows.astype(bf16))
    total = jnp.sum(jnp.where(live, 1.0, 0.0))
    weight = 1.0 + 2.0 * inside / jnp.maximum(total, 1.0)
    for row in range(GH):
        cot_ref[row * GW : (row + 1) * GW, :] = grad_ref[row].astype(f32) * weight[:, row : row + 1]
    cot_ref[REAL:, :] = jnp.zeros((DENSE - REAL, D), f32)
    upd_ref[...] = cot_ref[...].astype(bf16)


def lane_iota(shape):
    return lax.broadcasted_iota(jnp.int32, shape, len(shape) - 1)


def position_terms(queries, table):
    both = dot(queries, table)
    row_part = both[:, :128].reshape(WIN, LINE, 128)
    col_part = both[:, 128:].reshape(WIN, LINE, 128)
    lane = lane_iota((LINE, 128))
    local = lane % 32
    out = []
    for place in range(WIN):
        rolled_r = pltpu.roll(row_part[place], (place - 13) % 128, 1)
        rolled_c = pltpu.roll(col_part[place], 0, 1, stride=1, stride_axis=0)
        value = jnp.where(local < 16, rolled_r, rolled_c)
        high = value.astype(bf16).astype(f32)
        value = jnp.where(lane < 64, high, value - high)
        value = jnp.where(lane == 14, 1.0, value)
        out.append(value)
    return jnp.concatenate(out, axis=0).astype(bf16)


def keep_head(value, head):
    lane = lane_iota(value.shape)
    return jnp.where((lane < HD) == (head == 0), value, jnp.zeros_like(value))


def forward_kernel(places_ref, *refs):
    one_half, two_half, one_other, two_other, unit_ref, table_ref, hot_ref = refs[:7]
    tiles_ref, packed_ref, soft_ref, att_ref, branch_ref, vec_ref, one_ref, two_ref, sems = refs[7:]
    step = pl.program_id(0)

    @pl.when(step == 0)
    def _():
        core = places_ref[1]
        made = []
        for i, (half, whole_ref, place) in enumerate(
            [
                (one_half, one_ref, core),
                (two_half, two_ref, core),
                (one_other, one_ref, 1 - core),
                (two_other, two_ref, 1 - core),
            ]
        ):
            for y in range(2):
                here = pl.ds(pl.multiple_of((2 * y + place) * (D // 4), D // 4), D // 4)
                copy = pltpu.make_async_copy(half.at[y], whole_ref.at[here, :], sems.at[2 * i + y])
                copy.start()
                made.append(copy)
        for copy in made:
            copy.wait()
        vec_ref[...] = one_ref[:, :128].astype(f32).T[:16]

    window = step
    token = lax.broadcasted_iota(jnp.int32, (TOK, 1), 0)
    row_limit = jnp.where(window < ACROSS, WIN, GH - WIN)
    col_limit = jnp.where(window % ACROSS == ACROSS - 1, WIDTHS[2], WIN)
    valid = (token // LINE < row_limit) & (token % LINE < col_limit)
    tiles_ref[...] = (unit_ref[...] * vec_ref[3:4, :] + jnp.where(valid, vec_ref[4:5, :], 0.0)).astype(bf16)
    tiles = tiles_ref[...]
    packed_ref[:, :D] = (dot(tiles, one_ref[:, 128 : 128 + D]) + vec_ref[0:1, :]).astype(bf16)
    packed_ref[:, D : 2 * D] = dot(tiles, one_ref[:, 128 + D :]).astype(bf16)
    packed_ref[:, 2 * D :] = (dot(tiles, two_ref[:, :D]) + vec_ref[1:2, :]).astype(bf16)
    for pair in range(PAIRS):
        at = pair * 128
        queries = packed_ref[:, at : at + 128]
        keys = packed_ref[:, D + at : D + at + 128]
        values = packed_ref[:, 2 * D + at : 2 * D + at + 128]
        left = jnp.concatenate([queries, position_terms(queries, table_ref[...])], axis=1)
        parts = []
        for head in range(2):
            scaled = (keep_head(keys.astype(f32), head) * 0.125).astype(bf16)
            right = jnp.concatenate([scaled, hot_ref[head]], axis=1)
            scores = dot_bt(left, right)
            power = jnp.exp(scores - jnp.max(scores, axis=-1, keepdims=True))
            soft = (power * (1.0 / jnp.sum(power, axis=-1, keepdims=True))).astype(bf16)
            soft_ref[2 * pair + head] = soft
            parts.append(dot(soft, values))
        lane = lane_iota((TOK, 128))
        att_ref[:, at : at + 128] = jnp.where(lane < HD, parts[0], parts[1]).astype(bf16)
    branch_ref[...] = dot(att_ref[...], two_ref[:, D:]) + vec_ref[2:3, :]


def backward_kernel(packed_ref, soft_ref, att_ref, gbr_ref, two_ref, table_ref, hot_ref, *refs):
    gpacked_ref, gbias_ref, gtab_ref, flag_ref, gatt_ref = refs[-5:]

    @pl.when(pl.program_id(0) == 0)
    def _():
        flag_ref[0] = 0
        gbias_ref[...] = jnp.zeros_like(gbias_ref)
        gtab_ref[...] = jnp.zeros_like(gtab_ref)

    gatt_ref[...] = dot_bt(gbr_ref[...], two_ref[:, D:]).astype(bf16)
    lane = lane_iota((LINE, 128))
    local = lane % 32
    wide = lane_iota((TOK, 128))
    for pair in range(PAIRS):
        at = pair * 128
        queries = packed_ref[:, at : at + 128]
        keys = packed_ref[:, D + at : D + at + 128]
        values = packed_ref[:, 2 * D + at : 2 * D + at + 128]
        gatt = gatt_ref[:, at : at + 128]
        product = gatt.astype(f32) * att_ref[:, at : at + 128].astype(f32)
        left = []
        right = []
        gvalues = []
        gkeys = []
        for head in range(2):
            soft = soft_ref[2 * pair + head]
            delta = jnp.sum(keep_head(product, head), axis=-1, keepdims=True)
            gprobs = dot_bt(gatt, keep_head(values.astype(f32), head).astype(bf16))
            gscores = (soft.astype(f32) * (gprobs - delta)).astype(bf16)
            scaled = (keep_head(keys.astype(f32), head) * 0.125).astype(bf16)
            left.append(gscores)
            right.append(jnp.concatenate([scaled, hot_ref[head]], axis=1))
            gvalues.append(dot_at(soft, gatt))
            gkeys.append(dot_at(gscores, queries))
        both = dot(left[0], right[0]) + dot(left[1], right[1])
        terms = both[:, 128:].reshape(WIN, LINE, 128)
        rolled = []
        for place in range(WIN):
            value = terms[place]
            high = value.astype(bf16).astype(f32)
            value = jnp.where(lane < 64, high, value - high)
            row_part = jnp.where(local < WIN, value, 0.0)
            col_part = jnp.where((local >= 16) & (local < 16 + WIN), value, 0.0)
            row_part = pltpu.roll(row_part, 13 - place, 1)
            col_part = pltpu.roll(col_part, 0, 1, stride=1, stride_axis=0)
            rolled.append(jnp.concatenate([row_part, col_part], axis=1))
        rolled = jnp.concatenate(rolled, axis=0).astype(bf16)
        gqueries = both[:, :128] + dot_bt(rolled, table_ref[...])
        gtab_ref[...] += dot_at(rolled, queries)
        gq = gqueries.astype(bf16)
        gk = (jnp.where(wide < HD, gkeys[0], gkeys[1]) * 0.125).astype(bf16)
        gv = jnp.where(wide < HD, gvalues[0], gvalues[1]).astype(bf16)
        gpacked_ref[:, at : at + 128] = gq
        gpacked_ref[:, D + at : D + at + 128] = gk
        gpacked_ref[:, 2 * D + at : 2 * D + at + 128] = gv
        gbias_ref[0:1, at : at + 128] += jnp.sum(gq.astype(f32), axis=0, keepdims=True)
        gbias_ref[1:2, at : at + 128] += jnp.sum(gv.astype(f32), axis=0, keepdims=True)


def halve(core, value, keep_ref, send_ref, at):
    size = value.shape[0] // 4

    def put(first, second):
        for y in range(2):
            first[y * size : (y + 1) * size, at] = value[2 * y * size : (2 * y + 1) * size]
            second[y * size : (y + 1) * size, at] = value[(2 * y + 1) * size : (2 * y + 2) * size]

    @pl.when(core == 0)
    def _():
        put(keep_ref, send_ref)

    @pl.when(core == 1)
    def _():
        put(send_ref, keep_ref)


def attention_weights_kernel(core_ref, sums1_ref, sums2_ref, gupb_ref, tiles_ref, *refs):
    keep_ref, send_ref, flag_ref, gpacked, sems = refs[-5:]
    count = len(CALLS)
    gpacked_refs, gbias_refs = refs[:count], refs[count : 2 * count]
    flag_ref[0] = 0
    made = []
    for part in range(3):
        columns = slice(part * D, (part + 1) * D)
        at = 0
        for i, (windows, ref) in enumerate(zip(CALLS, gpacked_refs)):
            target = gpacked.at[at : at + windows * TOK, columns]
            copy = pltpu.make_async_copy(ref.at[:, columns], target, sems.at[part * count + i])
            copy.start()
            made.append(copy)
            at += windows * TOK
    gbias = gbias_refs[0][...]
    for ref in gbias_refs[1:]:
        gbias += ref[...]
    rows = [gbias[:2], sums2_ref[2:3, :], sums1_ref[:2, :], sums2_ref[:2, :], sums2_ref[3:4, :], gupb_ref[:4, :]]
    rows = jnp.concatenate(rows + [jnp.zeros((116, D), f32)], axis=0)
    value = jnp.concatenate([rows.T, jnp.zeros((D, 128), f32)], axis=1).astype(bf16)
    halve(core_ref[0], value, keep_ref, send_ref, slice(3 * D, 3 * D + 256))
    turned = tiles_ref[...].T
    for part in range(3):
        for copy in made[part * count : (part + 1) * count]:
            copy.wait()
        columns = slice(part * D, (part + 1) * D)
        halve(core_ref[0], dot(turned, gpacked[:, columns]).astype(bf16), keep_ref, send_ref, columns)


def gelu_parts(hidden):
    size = jnp.abs(hidden)
    power = jnp.exp(hidden * hidden * -0.5)
    denominator = 1.0 + (0.3275911 * 0.7071067811865476) * size
    near = pl.reciprocal(denominator, approx=True)
    near = near * (2.0 - denominator * near)
    series = near * (
        0.254829592
        + near * (-0.284496736 + near * (1.421413741 + near * (-1.453152027 + near * 1.061405429)))
    )
    tail = 0.5 * series * power
    normal = jnp.where(hidden >= 0, 1.0 - tail, tail)
    return hidden * normal, normal + hidden * power * 0.3989422804014327


def middle_kernel(
    core_ref,
    img_ref,
    cot_ref,
    gupd_ref,
    vec_ref,
    up_ref,
    down_ref,
    *refs,
):
    branch_ref, att_ref = refs[:2]
    out_ref, gbr_ref, gupk_ref, gups_ref, gdownk_ref, gdowns_ref, gupb_ref, sums_ref = refs[2:10]
    mid, normed, update, gnorm, active, ghidden = refs[10:]
    step = pl.program_id(0)
    gain = vec_ref[5:6, :]
    shift = vec_ref[6:7, :]

    @pl.when(step == 0)
    def _():
        for row in range(GH):
            mid[row * GW : (row + 1) * GW, :] = img_ref[row].astype(f32) + join_row(row, branch_ref)
        mid[REAL:, :] = jnp.zeros((DENSE - REAL, D), f32)
        update[...] = jnp.zeros_like(update)
        gnorm[...] = jnp.zeros_like(gnorm)

        def chunk(index, carry):
            here = pl.ds(pl.multiple_of(index * HALF, HALF), HALF)
            unit, _ = unit_of(mid[here, :])
            normed[here, :] = (unit * gain + shift).astype(bf16)
            return carry

        lax.fori_loop(0, DENSE // HALF, chunk, 0)

    @pl.when(step < FF // CHUNK)
    def _():
        up_bias = vec_ref[pl.ds(8 + step, 1), :]
        for start, size in SPLITS:
            here = slice(start, start + size)
            hidden = dot(normed[here, :], up_ref[...]) + up_bias
            gactive = dot_bt(gupd_ref[here, :], down_ref[...])
            act, slope = gelu_parts(hidden)
            act = act.astype(bf16)
            gh = (gactive * slope).astype(bf16)
            active[here, :] = act
            ghidden[here, :] = gh
            update[here, :] += dot(act, down_ref[...])
            gnorm[here, :] += dot_bt(gh, up_ref[...])
        gupb_ref[pl.ds(step, 1), :] = jnp.sum(ghidden[...].astype(f32), axis=0, keepdims=True)
        gdown = dot_at(active[...], gupd_ref[...]).astype(bf16)
        halve(core_ref[0], gdown, gdownk_ref, gdowns_ref, slice(None))
        gup = dot_at(normed[...], ghidden[...]).astype(bf16)
        halve(core_ref[0], gup, gupk_ref, gups_ref, slice(None))

    @pl.when(step == FF // CHUNK)
    def _():
        down_bias = vec_ref[7:8, :]
        for row in range(GH):
            here = slice(row * GW, (row + 1) * GW)
            out_ref[row] = (mid[here, :] + update[here, :] + down_bias).astype(bf16)

        def chunk(index, carry):
            here = pl.ds(pl.multiple_of(index * HALF, HALF), HALF)
            unit, inverse = unit_of(mid[here, :])
            grad = gnorm[here, :]
            cot = cot_ref[here, :]
            result = cot + norm_back(grad, unit, inverse, gain)
            rounded = result.astype(bf16).astype(f32)
            update[here, :] = rounded
            gain_sum, shift_sum, branch_sum, bias_sum = carry
            return (
                gain_sum + jnp.sum((grad * unit).reshape(HALF // 8, 8, D), axis=0),
                shift_sum + jnp.sum(grad.reshape(HALF // 8, 8, D), axis=0),
                branch_sum + jnp.sum(rounded.reshape(HALF // 8, 8, D), axis=0),
                bias_sum + jnp.sum(cot.astype(bf16).astype(f32).reshape(HALF // 8, 8, D), axis=0),
            )

        zero = jnp.zeros((8, D), f32)
        sums = lax.fori_loop(0, DENSE // HALF, chunk, (zero,) * 4)
        sums_ref[...] = jnp.concatenate(
            [jnp.sum(s, axis=0, keepdims=True) for s in sums] + [jnp.zeros((4, D), f32)], axis=0
        )
        gbr_ref[...] = jnp.zeros_like(gbr_ref)
        for row in range(GH):
            spread_row(row, update[row * GW : (row + 1) * GW, :], gbr_ref)
        gout = dot_at(att_ref[...], gbr_ref[...].reshape(WINDOWS * TOK, D))
        halve(core_ref[0], gout.astype(bf16), gupk_ref, gups_ref, slice(None))


def end_kernel(img_ref, gbr_ref, one_ref, two_ref, vec_ref, *refs):
    count = len(CALLS)
    gpacked_refs, gtab_refs = refs[:count], refs[count : 2 * count]
    out_ref, sums_ref, tables_ref, flag_ref, gtiles, gpacked, img, gbr, sems = refs[-9:]
    flag_ref[0] = 0
    made = []
    at = 0
    for i, (windows, ref) in enumerate(zip(CALLS, gpacked_refs)):
        made.append(pltpu.make_async_copy(ref, gpacked.at[at : at + windows * TOK, :], sems.at[i]))
        at += windows * TOK
    made.append(pltpu.make_async_copy(img_ref, img, sems.at[count]))
    made.append(pltpu.make_async_copy(gbr_ref, gbr, sems.at[count + 1]))
    for copy in made:
        copy.start()
    gain = vec_ref[3:4, :]
    at = 0
    for windows, copy in zip(CALLS, made):
        copy.wait()
        here = slice(at * TOK, (at + windows) * TOK)
        value = dot_bt(gpacked[here, : 2 * D], one_ref[:, 128:]) + dot_bt(gpacked[here, 2 * D :], two_ref[:, :D])
        gtiles[at * WIN : (at + windows) * WIN] = value.reshape(windows * WIN, LINE, D)
        at += windows
    for copy in made[count:]:
        copy.wait()
    gain_sum = jnp.zeros((1, D), f32)
    shift_sum = jnp.zeros((1, D), f32)
    for row in range(GH):
        unit, inverse = unit_of(img[row].astype(f32))
        grad = join_row(row, gtiles)
        gain_sum += jnp.sum(grad * unit, axis=0, keepdims=True)
        shift_sum += jnp.sum(grad, axis=0, keepdims=True)
        out_ref[row] = (join_row(row, gbr) + norm_back(grad, unit, inverse, gain)).astype(bf16)
    sums_ref[...] = jnp.concatenate([gain_sum, shift_sum, jnp.zeros((6, D), f32)], axis=0)
    total = gtab_refs[0][...]
    for ref in gtab_refs[1:]:
        total += ref[...]
    entries = 2 * WIN - 1
    rows = total[:128]
    cols = jnp.concatenate([total[128 + 16 :], total[128 : 128 + 16]], axis=0)
    tables = []
    for part in (rows, cols):
        whole_part = jnp.zeros((entries, HD), f32)
        for group in range(4):
            lines = part[32 * group : 32 * group + entries]
            whole_part += lines[:, HD:] if group % 2 else lines[:, :HD]
        tables.append(whole_part)
    flipped = [tables[0][entries - 1 - i : entries - i] for i in range(entries)]
    tables = jnp.concatenate(flipped + [tables[1], jnp.zeros((10, HD), f32)], axis=0)
    tables_ref[...] = jnp.concatenate([tables, jnp.zeros((64, HD), f32)], axis=1)


def pack_kernel(eight_ref, upb_ref, weight_ref, out_ref):
    own = weight_ref.shape[0]
    flat = upb_ref[...].astype(f32)
    rows = [eight_ref[...].astype(f32)] + [flat[:, own * i : own * (i + 1)] for i in range(4)]
    rows = jnp.concatenate(rows, axis=0)
    rows = jnp.concatenate([rows, jnp.zeros((12, 128 - own), f32)], axis=1)
    square = jnp.concatenate([rows, jnp.zeros((116, 128), f32)], axis=0)
    out_ref[:, :128] = square.T[:own].astype(bf16)
    out_ref[:, 128:] = weight_ref[:, : 2 * D]


def regroup(value, own, back=False):
    count = value.shape[1] // (4 * own)
    parts = []
    for i in range(count if back else 4):
        for j in range(4 if back else count):
            at = (j * count + i) * own if back else (4 * j + i) * own
            parts.append(value[:, at : at + own])
    return jnp.concatenate(parts, axis=1)


def pack_feed_kernel(up_ref, down_ref, out_ref):
    own = up_ref.shape[0]
    out_ref[:, :FF] = regroup(up_ref[...].astype(f32), own).astype(bf16)
    for k in range(4):
        part = down_ref[...].astype(f32)[k * own : (k + 1) * own]
        out_ref[:, FF + k * D : FF + (k + 1) * D] = part.astype(bf16)


def unpack_feed_kernel(first, second, up_ref, out_ref, down_ref):
    own = up_ref.shape[0]
    up_ref[...] = regroup(first[:, :FF], own, back=True)
    out_ref[...] = first[:, FF:]
    for k in range(4):
        down_ref[k * own : (k + 1) * own, :] = second[:, k * D : (k + 1) * D]


def unpack_in_kernel(first, second, tables_ref, in_ref, *refs):
    entries = 2 * WIN - 1
    tables = jnp.sum(tables_ref[...], axis=0)
    refs[-2][...] = tables[:entries, :HD]
    refs[-1][...] = tables[entries : 2 * entries, :HD]
    half = first.shape[1]
    in_ref[:, :half] = first
    in_ref[:, half:] = second[:, : 3 * D - half]
    own = first.shape[0]
    square = jnp.concatenate([second[:, 3 * D - half : 3 * D - half + 128], jnp.zeros((128 - own, 128), f32)], axis=0)
    rows = square.T
    for i in range(8):
        refs[i][...] = rows[i : i + 1, :own]
    refs[8][...] = jnp.concatenate([rows[i : i + 1, :own] for i in range(8, 12)], axis=1)


def params(steps=0):
    return pltpu.CompilerParams(
        vmem_limit_bytes=LIMIT, dimension_semantics=("arbitrary",) * steps if steps else None
    )


VMEM = pl.BlockSpec(memory_space=pltpu.VMEM)
SMEM = pl.BlockSpec(memory_space=pltpu.SMEM)


def whole(shape):
    return pl.BlockSpec(shape, lambda i: (0,) * len(shape))


def shaped(shape, dtype):
    return jax.ShapeDtypeStruct(shape, dtype)


def pack_feed(up, down):
    own = up.shape[0]
    return pl.pallas_call(
        pack_feed_kernel,
        out_shape=shaped((own, 2 * FF), bf16),
        in_specs=[VMEM] * 2,
        out_specs=VMEM,
        compiler_params=params(),
        name="pack_feed",
    )(up, down)


FLAG = pl.BlockSpec(memory_space=pltpu.SMEM)
ANY = pl.BlockSpec(memory_space=pl.ANY)
flag_shape = jax.ShapeDtypeStruct((1,), jnp.int32)


def begin(images, before):
    return pl.pallas_call(
        begin_kernel,
        out_shape=(shaped((WINDOWS * WIN, LINE, D), f32), flag_shape),
        in_specs=[VMEM] + [ANY] * len(before),
        out_specs=(VMEM, FLAG),
        compiler_params=params(),
        cost_estimate=pl.CostEstimate(flops=30_000_000, bytes_accessed=6_000_000, transcendentals=0),
        name="begin",
    )(images, *before)


def weigh(count, grad_out, rows, cols, valid, row_table, col_table, before):
    return pl.pallas_call(
        weight_kernel,
        out_shape=(
            shaped((DENSE, D), f32),
            shaped((DENSE, D), bf16),
            shaped((128, 256), bf16),
            shaped((128, 256), bf16),
            flag_shape,
        ),
        in_specs=[SMEM] + [VMEM] * 6 + [ANY] * len(before),
        out_specs=(VMEM,) * 4 + (FLAG,),
        compiler_params=params(),
        cost_estimate=pl.CostEstimate(flops=30_000_000, bytes_accessed=6_000_000, transcendentals=0),
        name="weigh",
    )(count, grad_out, rows, cols, valid, row_table, col_table, *before)


def forward(places, halves, unit, table, hot):
    per = lambda *shape: pl.BlockSpec(shape, lambda i: (i,) + (0,) * (len(shape) - 1))
    return pl.pallas_call(
        forward_kernel,
        grid=(WINDOWS,),
        out_shape=(
            shaped((WINDOWS * TOK, D), bf16),
            shaped((WINDOWS * TOK, 3 * D), bf16),
            shaped((WINDOWS * HEADS, TOK, TOK), bf16),
            shaped((WINDOWS * TOK, D), bf16),
            shaped((WINDOWS * TOK, D), f32),
            shaped((16, D), f32),
            shaped((D, 128 + 2 * D), bf16),
            shaped((D, 2 * D), bf16),
        ),
        in_specs=[SMEM] + [ANY] * 4 + [per(TOK, D), whole((128, 256)), whole((2, TOK, 128))],
        out_specs=(
            per(TOK, D),
            per(TOK, 3 * D),
            per(HEADS, TOK, TOK),
            per(TOK, D),
            per(TOK, D),
            whole((16, D)),
            whole((D, 128 + 2 * D)),
            whole((D, 2 * D)),
        ),
        scratch_shapes=[pltpu.SemaphoreType.DMA((8,))],
        compiler_params=params(1),
        cost_estimate=pl.CostEstimate(flops=30_000_000_000, bytes_accessed=28_000_000, transcendentals=4_000_000),
        name="attend",
    )(places, *halves, unit, table, hot)


def middle(core, images, cot, gupd, vec, weights, branch, attended):
    steps = FF // CHUNK
    at = lambda i: jnp.minimum(i, steps - 1)
    return pl.pallas_call(
        middle_kernel,
        grid=(steps + 1,),
        out_shape=(
            shaped((GH, GW, D), bf16),
            shaped((WINDOWS * WIN, LINE, D), bf16),
            shaped((D // 2, FF + D), bf16),
            shaped((D // 2, FF + D), bf16),
            shaped((D // 2, FF), bf16),
            shaped((D // 2, FF), bf16),
            shaped((8, D), f32),
            shaped((8, D), f32),
        ),
        in_specs=[
            SMEM,
            whole((GH, GW, D)),
            whole((DENSE, D)),
            whole((DENSE, D)),
            whole((16, D)),
            pl.BlockSpec((D, CHUNK), lambda i: (0, at(i))),
            pl.BlockSpec((D, CHUNK), lambda i: (0, steps + at(i))),
        ]
        + [whole((WINDOWS * WIN, LINE, D)), whole((WINDOWS * TOK, D))],
        out_specs=(
            whole((GH, GW, D)),
            whole((WINDOWS * WIN, LINE, D)),
            pl.BlockSpec((D // 2, CHUNK), lambda i: (0, i)),
            pl.BlockSpec((D // 2, CHUNK), lambda i: (0, i)),
            pl.BlockSpec((D // 2, CHUNK), lambda i: (0, at(i))),
            pl.BlockSpec((D // 2, CHUNK), lambda i: (0, at(i))),
            whole((8, D)),
            whole((8, D)),
        ),
        scratch_shapes=[
            pltpu.VMEM((DENSE, D), f32),
            pltpu.VMEM((DENSE, D), bf16),
            pltpu.VMEM((DENSE, D), f32),
            pltpu.VMEM((DENSE, D), f32),
            pltpu.VMEM((DENSE, CHUNK), bf16),
            pltpu.VMEM((DENSE, CHUNK), bf16),
        ],
        compiler_params=params(1),
        cost_estimate=pl.CostEstimate(flops=50_000_000_000, bytes_accessed=36_000_000, transcendentals=6_000_000),
        name="feed",
    )(core, images, cot, gupd, vec, weights, weights, branch, attended)


def backward(start, count, packed, soft, att, gbr, two, table, hot, before=()):
    per = lambda *shape: pl.BlockSpec(shape, lambda i: (start + i,) + (0,) * (len(shape) - 1))
    return pl.pallas_call(
        backward_kernel,
        grid=(count,),
        out_shape=(
            shaped((count * TOK, 3 * D), bf16),
            shaped((8, D), f32),
            shaped((256, 128), f32),
            flag_shape,
        ),
        in_specs=[
            per(TOK, 3 * D),
            per(HEADS, TOK, TOK),
            per(TOK, D),
            per(TOK, D),
            whole((D, 2 * D)),
            whole((128, 256)),
            whole((2, TOK, 128)),
        ]
        + [ANY] * len(before),
        out_specs=(pl.BlockSpec((TOK, 3 * D), lambda i: (i, 0)), whole((8, D)), whole((256, 128)), FLAG),
        scratch_shapes=[pltpu.VMEM((TOK, D), bf16)],
        compiler_params=params(1),
        cost_estimate=pl.CostEstimate(flops=6_000_000_000 * count, bytes_accessed=9_000_000, transcendentals=0),
        name="attend_back",
    )(packed, soft, att, gbr, two, table, hot, *before)


def attention_weights(core, sums, tiles, gpacked, gbias, before=()):
    return pl.pallas_call(
        attention_weights_kernel,
        grid=(1,),
        out_shape=(shaped((D // 2, 3 * D + 256), bf16),) * 2 + (flag_shape,),
        in_specs=[SMEM]
        + [whole((8, D))] * 3
        + [whole((WINDOWS * TOK, D))]
        + [ANY] * len(CALLS)
        + [whole((8, D))] * len(CALLS)
        + [ANY] * len(before),
        out_specs=(whole((D // 2, 3 * D + 256)),) * 2 + (FLAG,),
        scratch_shapes=[pltpu.VMEM((WINDOWS * TOK, 3 * D), bf16), pltpu.SemaphoreType.DMA((3 * len(CALLS),))],
        compiler_params=params(1),
        cost_estimate=pl.CostEstimate(flops=25_000_000_000, bytes_accessed=18_000_000, transcendentals=0),
        name="attend_weights",
    )(core, *sums, tiles, *gpacked, *gbias, *before)


def end(images, gbr, one, two, vec, gpacked, gtab, before=()):
    return pl.pallas_call(
        end_kernel,
        out_shape=(shaped((GH, GW, D), bf16), shaped((8, D), f32), shaped((64, 128), f32), flag_shape),
        in_specs=[ANY] * 2 + [VMEM] * 3 + [ANY] * len(CALLS) + [VMEM] * len(CALLS) + [ANY] * len(before),
        out_specs=(VMEM, VMEM, VMEM, FLAG),
        scratch_shapes=[
            pltpu.VMEM((WINDOWS * WIN, LINE, D), f32),
            pltpu.VMEM((WINDOWS * TOK, 3 * D), bf16),
            pltpu.VMEM((GH, GW, D), bf16),
            pltpu.VMEM((WINDOWS * WIN, LINE, D), bf16),
            pltpu.SemaphoreType.DMA((len(CALLS) + 2,)),
        ],
        compiler_params=params(),
        cost_estimate=pl.CostEstimate(flops=12_000_000_000, bytes_accessed=17_000_000, transcendentals=0),
        name="end",
    )(images, gbr, one, two, vec, *gpacked, *gtab, *before)


def pack(eight, up_bias, weight):
    return pl.pallas_call(
        pack_kernel,
        out_shape=shaped((weight.shape[0], 128 + 2 * D), bf16),
        in_specs=[VMEM] * 3,
        out_specs=VMEM,
        compiler_params=params(),
        name="pack",
    )(eight, up_bias, weight)


def one_hot_keys(flip):
    token = np.arange(TOK)
    row, col = token // LINE, token % LINE
    lane = np.arange(128)
    group, local = lane // 32, lane % 32
    hot = []
    for head in range(2):
        mine = (group % 2 == head)[None, :]
        value = ((local[None, :] == row[:, None]) & (local < WIN)[None, :]) | (
            (local[None, :] - 16 == (13 - col if flip else col)[:, None]) & (col < WIN)[:, None]
        )
        value = np.where(mine & value, 1.0, 0.0)
        value[:, 14] = np.where(col >= WIN, -1e30, 0.0)
        hot.append(value)
    return jnp.asarray(np.stack(hot), dtype=bf16)


AXES = ("dp", "fsdp")


class Exchange:
    def __init__(self, dp, fsdp):
        self.count = dp * fsdp
        self.bits = []
        bit = self.count // 2
        while bit:
            self.bits.append(bit)
            bit //= 2
        place = lax.axis_index(AXES).astype(jnp.int32)
        self.place = place
        self.mine = [(place >> (bit.bit_length() - 1)) & 1 for bit in self.bits]
        self.places = jnp.stack(self.mine)
        last = len(self.bits) - 1
        low = list(range(last - 1, 1, -1))
        self.orders = ([0, last] + low, [last, 0] + low)

    def swap(self, value, at):
        bit = self.bits[at]
        return lax.ppermute(value, AXES, [(i, i ^ bit) for i in range(self.count)])

    def spread(self, value):
        return value.reshape((1,) * len(self.bits) + value.shape)

    def join(self, value, at, flag=None):
        other = self.swap(value, at)
        mine = self.mine[at] if flag is None else self.mine[at] + flag[0]
        return jnp.where(
            mine == 0, jnp.concatenate([value, other], axis=at), jnp.concatenate([other, value], axis=at)
        )

    def own_part(self, piece, flag=None):
        terms, done, half = piece
        total = None
        for term in terms:
            for at in done:
                if term.shape[at] == 2:
                    mine = self.mine[at] if flag is None else self.mine[at] + flag[0]
                    term = lax.dynamic_index_in_dim(term, mine, at, keepdims=True)
            if half is not None:
                columns = term.shape[-1] // 2
                term = term[..., half * columns : (half + 1) * columns]
            term = term.astype(f32)
            total = term if total is None else total + term
        return total

    def halve(self, value, at):
        leave = lax.dynamic_index_in_dim(value, 1 - self.mine[at], at, keepdims=True).astype(bf16)
        stay = lax.dynamic_index_in_dim(value, self.mine[at], at, keepdims=True)
        return stay, self.swap(leave, at), leave

    def tie(self, values, before):
        count = len(values)

        def kernel(*refs):
            pass

        return pl.pallas_call(
            kernel,
            out_shape=tuple(shaped(v.shape, v.dtype) for v in values),
            in_specs=[ANY] * (count + len(before)),
            out_specs=(ANY,) * count,
            input_output_aliases={i: i for i in range(count)},
            name="tie",
        )(*values, *before)

    def flat(self, value):
        return value.reshape((self.count * value.shape[-2], value.shape[-1]))

    def cut(self, keep, send):
        rows, columns = keep.shape
        shape = (2, 1) + (2,) * (len(self.bits) - 2) + (2 * rows // self.count, columns)
        return [keep.reshape(shape), self.swap(send, 1).reshape(shape)]

    def blocks(self, piece, width, steps, leave=None):
        terms, done, half = piece
        specs = []
        for term in terms:
            shape = term.shape
            block, pick = [], []
            for at in range(len(self.bits)):
                cut = at in done or at == leave
                block.append(1 if cut else shape[at])
                pick.append((at, shape[at] == 2 and cut, at == leave))
            block += [shape[-2], width]
            first = half * steps if half and shape[-1] > width * steps else 0

            def index(i, places, pick=pick, first=first):
                where = [jnp.where(other, 1 - places[at], places[at]) if use else 0 for at, use, other in pick]
                return (*where, 0, first + jnp.minimum(i, steps - 1))

            specs.append(pl.BlockSpec(tuple(block), index))
        return specs

    def narrow(self, pieces, ats, widths, before=()):
        operands, specs, outs, out_specs, counts = [], [], [], [], []
        grid = 1
        for piece, at, width in zip(pieces, ats, widths):
            terms, done, half = piece
            columns = terms[-1].shape[-1] // (2 if half is not None and len(terms) == 2 else 1)
            steps = columns // width
            grid = max(grid, steps)
            specs += self.blocks(piece, width, steps, at)
            operands += terms
            counts.append(len(terms))
            shape = tuple(1 if i in done or i == at else n for i, n in enumerate(terms[0].shape[:-1]))
            outs.append(shaped(shape + (columns,), bf16))
            out_specs.append(
                pl.BlockSpec(
                    shape + (width,),
                    lambda i, places, n=len(shape), steps=steps: (0,) * n + (jnp.minimum(i, steps - 1),),
                )
            )
        count = len(pieces)

        def kernel(places, *refs):
            results = refs[-count - 1 : -1]
            refs[-1][0] = 0
            at = 0
            for i, terms in enumerate(counts):
                total = refs[at][...].astype(f32)
                for ref in refs[at + 1 : at + terms]:
                    total += ref[...].astype(f32)
                results[i][...] = total.astype(bf16)
                at += terms

        size = sum(int(np.prod(o.shape)) for o in outs)
        got = pl.pallas_call(
            kernel,
            grid_spec=pltpu.PrefetchScalarGridSpec(
                num_scalar_prefetch=1,
                grid=(grid,),
                in_specs=specs + [ANY] * len(before),
                out_specs=tuple(out_specs) + (FLAG,),
            ),
            out_shape=tuple(outs) + (flag_shape,),
            compiler_params=params(1),
            cost_estimate=pl.CostEstimate(flops=4 * size, bytes_accessed=8 * size, transcendentals=0),
            name="narrow",
        )(self.places, *operands, *before)
        results = []
        for (terms, done, half), at, leave in zip(pieces, ats, got):
            results.append((terms + [self.swap(leave, at)], done + [at], half))
        return results, [got[-1]]

    def close(self, pieces, kernel, out_shape, name, more=()):
        operands = [part.reshape(part.shape[-2:]) for piece in pieces for part in piece]

        def body(*refs):
            sums = [refs[2 * i][...] + refs[2 * i + 1][...].astype(f32) for i in range(len(pieces))]
            kernel(*sums, *refs[2 * len(pieces) :])

        return pl.pallas_call(
            body,
            out_shape=out_shape,
            in_specs=[VMEM] * (len(operands) + len(more)),
            out_specs=(VMEM,) * len(out_shape),
            compiler_params=params(),
            name=name,
        )(*operands, *more)


def local(
    dp,
    fsdp,
    images,
    grad_out,
    box_rows,
    box_cols,
    box_valid,
    box_count,
    in_weight,
    query_bias,
    value_bias,
    out_weight,
    out_bias,
    first_gain,
    first_shift,
    second_gain,
    second_shift,
    up_weight,
    up_bias,
    down_weight,
    down_bias,
    row_table,
    col_table,
):
    links = Exchange(dp, fsdp)
    image = images[0]
    core = (lax.axis_index("dp") & 1).astype(jnp.int32).reshape(1)
    hot = one_hot_keys(False)
    hot_back = one_hot_keys(True)
    eight = jnp.stack(
        [query_bias, value_bias, out_bias, first_gain, first_shift, second_gain, second_shift, down_bias]
    )
    first, second = links.orders[0][::-1], links.orders[1][::-1]
    last = len(first)
    two = links.spread(jnp.concatenate([in_weight[:, 2 * D :], out_weight], axis=1))
    one = links.spread(pack(eight, up_bias[None], in_weight))
    feed_weights = lax.all_gather(pack_feed(up_weight, down_weight), AXES, axis=0, tiled=True)
    for step in range(last - 2):
        two = links.join(two, second[step])
        one = links.join(one, first[step])
    cot, gupd, table, table_back, flag = weigh(
        box_count, grad_out[0], box_rows[0], box_cols[0], box_valid.reshape(NBOX, 1), row_table, col_table, [two, one]
    )
    two = links.join(two, second[last - 2], flag)
    one = links.join(one, first[last - 2], flag)
    unit, flag = begin(image, [two, one])
    unit = unit.reshape(WINDOWS * TOK, D)
    two = links.join(two, second[last - 1], flag)
    one = links.join(one, first[last - 1], flag)
    halves = [h.reshape(2, D // 4, -1) for h in (one, two, links.swap(one, 1), links.swap(two, 1))]

    tiles, packed, soft, att, branch, vec, one, two = forward(links.places, halves, unit, table, hot)
    block_out, gbr, gup_k, gup_s, gdown_k, gdown_s, gupb, sums2 = middle(
        core, image, cot, gupd, vec, feed_weights, branch.reshape(WINDOWS * WIN, LINE, D), att
    )

    first, second = links.orders
    gbr_flat = gbr.reshape(WINDOWS * TOK, D)
    feed = [(links.cut(gup_k, gup_s), [], None), (links.cut(gdown_k, gdown_s), [], None)]
    back = []
    flag = []
    start = 0
    for windows in CALLS:
        back.append(backward(start, windows, packed, soft, att, gbr_flat, two, table_back, hot_back, flag))
        flag = [back[-1][3]]
        if start == 0:
            feed, flag = links.narrow(feed, (first[0], second[0]), (FF + D, FF), flag)
        start += windows
    gpacked = [b[0] for b in back]
    image_grad, sums1, tables, flag = end(image, gbr, one, two, vec, gpacked, [b[2] for b in back], flag)
    feed, flag = links.narrow(feed, (first[1], second[1]), (FF + D, FF), [flag])
    all_tables = lax.all_gather(tables, AXES, axis=0, tiled=False)
    gin_k, gin_s, flag = attention_weights(core, (sums1, sums2, gupb), tiles, gpacked, [b[1] for b in back], flag)
    *recv, gin_s = links.tie([f[0][-1] for f in feed] + [gin_s], [flag])
    feed = [(f[0][:-1] + [r], f[1], f[2]) for f, r in zip(feed, recv)]
    gin = links.cut(gin_k, gin_s)
    feed = [links.halve(links.own_part(f), at) for f, at in zip(feed, (first[2], second[2]))]
    gin = [(links.own_part((gin, [], half)),) for half in range(2)]
    for step in range(last):
        gin = [links.halve(sum(g), at) for g, at in zip([(g[0],) if len(g) == 1 else g[:2] for g in gin], (first[step], second[step]))]
        if 1 <= step < last - 2 or step == last - 1:
            late = links.tie([f[1] for f in feed], [g[2] for g in gin])
            feed = [(f[0], r) for f, r in zip(feed, late)]
        if 1 <= step < last - 2:
            ats = (first[step + 2], second[step + 2])
            feed = [links.halve(f[0] + f[1].astype(f32), at) for f, at in zip(feed, ats)]
    gin = [g[:2] for g in gin]
    feed = [f[:2] for f in feed]
    own = in_weight.shape[0]
    gup, gout, gdown = links.close(
        feed, unpack_feed_kernel, (shaped((own, FF), f32), shaped((own, D), f32), shaped((4 * own, D), f32)), "unpack_feed"
    )
    entries = 2 * WIN - 1
    gin, *out = links.close(
        gin,
        unpack_in_kernel,
        (shaped((own, 3 * D), f32),)
        + (shaped((1, own), f32),) * 8
        + (shaped((1, 4 * own), f32),)
        + (shaped((entries, HD), f32),) * 2,
        "unpack_in",
        [all_tables],
    )
    qb, vb, ob, g1, s1, g2, s2, db, ub = [o.reshape(-1) for o in out[:9]]
    row_grad, col_grad = out[9:]
    return (
        block_out[None],
        image_grad[None],
        gin,
        qb,
        vb,
        gout,
        ob,
        g1,
        s1,
        g2,
        s2,
        gup,
        ub,
        gdown,
        db,
        row_grad,
        col_grad,
    )


def solution(mesh):
    rows = P(AXES)
    dp, fsdp = mesh.shape["dp"], mesh.shape["fsdp"]
    return jax.shard_map(
        lambda *args: local(dp, fsdp, *args),
        mesh=mesh,
        in_specs=(rows,) * 19 + (P(), P()),
        out_specs=(rows,) * 15 + (P(), P()),
        check_vma=False,
    )
```

```python
import functools

import jax
import jax.numpy as jnp
import numpy as np
from jax import lax
from jax.experimental import pallas as pl
from jax.experimental.pallas import tpu as pltpu
from jax.sharding import PartitionSpec as P

D = 768
HEADS = 12
HD = 64
FF = 3072
WIN = 14
GH = 26
GW = 38
NBOX = 300
ACROSS = 3
WINDOWS = 6
LINE = 16
TOK = WIN * LINE
REAL = GH * GW
DENSE = 992
HALF = DENSE // 2
PAIRS = HEADS // 2
STARTS = (0, 14, 28)
WIDTHS = (14, 14, 10)
CHUNK = 768
CALLS = (2, 4)
SPLITS = ((0, 256), (256, 256), (512, 256), (768, 224))
epsilon = 1e-06
f32 = jnp.float32
bf16 = jnp.bfloat16
LIMIT = 60 * 1024 * 1024


def dot(a, b):
    return lax.dot_general(a, b, (((1,), (0,)), ((), ())), preferred_element_type=f32)


def dot_bt(a, b):
    return lax.dot_general(a, b, (((1,), (1,)), ((), ())), preferred_element_type=f32)


def dot_at(a, b):
    return lax.dot_general(a, b, (((0,), (0,)), ((), ())), preferred_element_type=f32)


def unit_of(x):
    center = x - jnp.mean(x, axis=-1, keepdims=True)
    inverse = lax.rsqrt(jnp.mean(center * center, axis=-1, keepdims=True) + epsilon)
    return center * inverse, inverse


def norm_back(grad, unit, inverse, gain):
    scaled = grad * gain
    return inverse * (
        scaled
        - jnp.mean(scaled, axis=-1, keepdims=True)
        - unit * jnp.mean(scaled * unit, axis=-1, keepdims=True)
    )


def place_of(row):
    return (row // WIN) * ACROSS, row % WIN


def spread_row(row, value, out_ref):
    first, place = place_of(row)
    for piece, (start, width) in enumerate(zip(STARTS, WIDTHS)):
        part = value[start : start + width]
        part = jnp.concatenate([part, jnp.zeros((LINE - width, part.shape[1]), part.dtype)], axis=0)
        out_ref[(first + piece) * WIN + place] = part.astype(out_ref.dtype)


def join_row(row, ref):
    first, place = place_of(row)
    return jnp.concatenate(
        [ref[(first + piece) * WIN + place].astype(f32)[:width] for piece, width in enumerate(WIDTHS)], axis=0
    )


def begin_kernel(img_ref, *refs):
    unit_ref, flag_ref = refs[-2:]
    flag_ref[0] = 0
    unit_ref[...] = jnp.zeros_like(unit_ref)
    for row in range(GH):
        unit, _ = unit_of(img_ref[row].astype(f32))
        spread_row(row, unit, unit_ref)


def pair_tables(row_table, col_table, entry_row, entry_col):
    parts = []
    for table, place in ((row_table, entry_row), (col_table, entry_col)):
        pieces = jnp.zeros((128, 128), f32)
        entries = lax.broadcasted_iota(jnp.int32, (2 * WIN - 1, 128), 0)
        lane = lane_iota((2 * WIN - 1, 128))
        row = lax.broadcasted_iota(jnp.int32, (128, 128), 0)
        for head in range(2):
            where = place(entries) + 32 * head
            pick = ((lane - where) % 64) == 0
            spread = dot_at(table, jnp.where(pick, 1.0, 0.0).astype(bf16))
            both = jnp.concatenate([spread, spread], axis=0)
            pieces = jnp.where((row < HD) == (head == 0), both, pieces)
        parts.append(pieces)
    return jnp.concatenate(parts, axis=1).astype(bf16)


def weight_kernel(count_ref, grad_ref, rows_ref, cols_ref, valid_ref, rowt_ref, colt_ref, *refs):
    cot_ref, upd_ref, table_ref, back_ref, flag_ref = refs[-5:]
    flag_ref[0] = 0
    table_ref[...] = pair_tables(rowt_ref[...], colt_ref[...], lambda e: 26 - e, lambda e: 29 - e)
    back_ref[...] = pair_tables(rowt_ref[...], colt_ref[...], lambda e: 26 - e, lambda e: 16 + e)
    slot = lax.broadcasted_iota(jnp.int32, (NBOX, 1), 0)
    live = (slot < count_ref[0]) & (valid_ref[...] == 1)
    rows = rows_ref[...]
    cols = cols_ref[...]
    top = jnp.minimum(rows[:, 0:1], rows[:, 1:2])
    low = jnp.maximum(rows[:, 0:1], rows[:, 1:2])
    left = jnp.minimum(cols[:, 0:1], cols[:, 1:2])
    right = jnp.maximum(cols[:, 0:1], cols[:, 1:2])
    grid_r = lax.broadcasted_iota(jnp.int32, (NBOX, GH), 1)
    grid_c = lax.broadcasted_iota(jnp.int32, (NBOX, GW), 1)
    in_rows = jnp.where((grid_r >= top) & (grid_r < low) & live, 1.0, 0.0)
    in_cols = jnp.where((grid_c >= left) & (grid_c < right), 1.0, 0.0)
    inside = dot_at(in_cols.astype(bf16), in_rows.astype(bf16))
    total = jnp.sum(jnp.where(live, 1.0, 0.0))
    weight = 1.0 + 2.0 * inside / jnp.maximum(total, 1.0)
    for row in range(GH):
        cot_ref[row * GW : (row + 1) * GW, :] = grad_ref[row].astype(f32) * weight[:, row : row + 1]
    cot_ref[REAL:, :] = jnp.zeros((DENSE - REAL, D), f32)
    upd_ref[...] = cot_ref[...].astype(bf16)


def lane_iota(shape):
    return lax.broadcasted_iota(jnp.int32, shape, len(shape) - 1)


def position_terms(queries, table):
    both = dot(queries, table)
    row_part = both[:, :128].reshape(WIN, LINE, 128)
    col_part = both[:, 128:].reshape(WIN, LINE, 128)
    lane = lane_iota((LINE, 128))
    local = lane % 32
    out = []
    for place in range(WIN):
        rolled_r = pltpu.roll(row_part[place], (place - 13) % 128, 1)
        rolled_c = pltpu.roll(col_part[place], 0, 1, stride=1, stride_axis=0)
        value = jnp.where(local < 16, rolled_r, rolled_c)
        high = value.astype(bf16).astype(f32)
        value = jnp.where(lane < 64, high, value - high)
        value = jnp.where(lane == 14, 1.0, value)
        out.append(value)
    return jnp.concatenate(out, axis=0).astype(bf16)


def keep_head(value, head):
    lane = lane_iota(value.shape)
    return jnp.where((lane < HD) == (head == 0), value, jnp.zeros_like(value))


def forward_kernel(places_ref, *refs):
    one_half, two_half, one_other, two_other, unit_ref, table_ref, hot_ref = refs[:7]
    tiles_ref, packed_ref, soft_ref, att_ref, branch_ref, vec_ref, one_ref, two_ref, sems = refs[7:]
    step = pl.program_id(0)

    @pl.when(step == 0)
    def _():
        core = places_ref[1]
        made = []
        for i, (half, whole_ref, place) in enumerate(
            [
                (one_half, one_ref, core),
                (two_half, two_ref, core),
                (one_other, one_ref, 1 - core),
                (two_other, two_ref, 1 - core),
            ]
        ):
            for y in range(2):
                here = pl.ds(pl.multiple_of((2 * y + place) * (D // 4), D // 4), D // 4)
                copy = pltpu.make_async_copy(half.at[y], whole_ref.at[here, :], sems.at[2 * i + y])
                copy.start()
                made.append(copy)
        for copy in made:
            copy.wait()
        vec_ref[...] = one_ref[:, :128].astype(f32).T[:16]

    window = step
    token = lax.broadcasted_iota(jnp.int32, (TOK, 1), 0)
    row_limit = jnp.where(window < ACROSS, WIN, GH - WIN)
    col_limit = jnp.where(window % ACROSS == ACROSS - 1, WIDTHS[2], WIN)
    valid = (token // LINE < row_limit) & (token % LINE < col_limit)
    tiles_ref[...] = (unit_ref[...] * vec_ref[3:4, :] + jnp.where(valid, vec_ref[4:5, :], 0.0)).astype(bf16)
    tiles = tiles_ref[...]
    packed_ref[:, :D] = (dot(tiles, one_ref[:, 128 : 128 + D]) + vec_ref[0:1, :]).astype(bf16)
    packed_ref[:, D : 2 * D] = dot(tiles, one_ref[:, 128 + D :]).astype(bf16)
    packed_ref[:, 2 * D :] = (dot(tiles, two_ref[:, :D]) + vec_ref[1:2, :]).astype(bf16)
    for pair in range(PAIRS):
        at = pair * 128
        queries = packed_ref[:, at : at + 128]
        keys = packed_ref[:, D + at : D + at + 128]
        values = packed_ref[:, 2 * D + at : 2 * D + at + 128]
        left = jnp.concatenate([queries, position_terms(queries, table_ref[...])], axis=1)
        parts = []
        for head in range(2):
            scaled = (keep_head(keys.astype(f32), head) * 0.125).astype(bf16)
            right = jnp.concatenate([scaled, hot_ref[head]], axis=1)
            scores = dot_bt(left, right)
            power = jnp.exp(scores - jnp.max(scores, axis=-1, keepdims=True))
            soft = (power * (1.0 / jnp.sum(power, axis=-1, keepdims=True))).astype(bf16)
            soft_ref[2 * pair + head] = soft
            parts.append(dot(soft, values))
        lane = lane_iota((TOK, 128))
        att_ref[:, at : at + 128] = jnp.where(lane < HD, parts[0], parts[1]).astype(bf16)
    branch_ref[...] = dot(att_ref[...], two_ref[:, D:]) + vec_ref[2:3, :]


def backward_kernel(packed_ref, soft_ref, att_ref, gbr_ref, two_ref, table_ref, hot_ref, *refs):
    gpacked_ref, gbias_ref, gtab_ref, flag_ref, gatt_ref = refs[-5:]

    @pl.when(pl.program_id(0) == 0)
    def _():
        flag_ref[0] = 0
        gbias_ref[...] = jnp.zeros_like(gbias_ref)
        gtab_ref[...] = jnp.zeros_like(gtab_ref)

    gatt_ref[...] = dot_bt(gbr_ref[...], two_ref[:, D:]).astype(bf16)
    lane = lane_iota((LINE, 128))
    local = lane % 32
    wide = lane_iota((TOK, 128))
    for pair in range(PAIRS):
        at = pair * 128
        queries = packed_ref[:, at : at + 128]
        keys = packed_ref[:, D + at : D + at + 128]
        values = packed_ref[:, 2 * D + at : 2 * D + at + 128]
        gatt = gatt_ref[:, at : at + 128]
        product = gatt.astype(f32) * att_ref[:, at : at + 128].astype(f32)
        left = []
        right = []
        gvalues = []
        gkeys = []
        turned_g = gatt.T
        turned_q = queries.T
        for head in range(2):
            soft = soft_ref[2 * pair + head]
            delta = jnp.sum(keep_head(product, head), axis=-1, keepdims=True)
            gprobs = dot_bt(gatt, keep_head(values.astype(f32), head).astype(bf16))
            gscores = (soft.astype(f32) * (gprobs - delta)).astype(bf16)
            scaled = (keep_head(keys.astype(f32), head) * 0.125).astype(bf16)
            left.append(gscores)
            right.append(jnp.concatenate([scaled, hot_ref[head]], axis=1))
            rows = slice(head * HD, (head + 1) * HD)
            gvalues.append(dot(turned_g[rows], soft))
            gkeys.append(dot(turned_q[rows], gscores))
        both = dot(left[0], right[0]) + dot(left[1], right[1])
        terms = both[:, 128:].reshape(WIN, LINE, 128)
        rolled = []
        for place in range(WIN):
            value = terms[place]
            high = value.astype(bf16).astype(f32)
            value = jnp.where(lane < 64, high, value - high)
            row_part = jnp.where(local < WIN, value, 0.0)
            col_part = jnp.where((local >= 16) & (local < 16 + WIN), value, 0.0)
            row_part = pltpu.roll(row_part, 13 - place, 1)
            col_part = pltpu.roll(col_part, 0, 1, stride=1, stride_axis=0)
            rolled.append(jnp.concatenate([row_part, col_part], axis=1))
        rolled = jnp.concatenate(rolled, axis=0).astype(bf16)
        gqueries = both[:, :128] + dot_bt(rolled, table_ref[...])
        gtab_ref[...] += dot_at(rolled, queries)
        gq = gqueries.astype(bf16)
        gk = (jnp.concatenate(gkeys, axis=0) * 0.125).astype(bf16).T
        gv = jnp.concatenate(gvalues, axis=0).astype(bf16).T
        gpacked_ref[:, at : at + 128] = gq
        gpacked_ref[:, D + at : D + at + 128] = gk
        gpacked_ref[:, 2 * D + at : 2 * D + at + 128] = gv
        gbias_ref[0:1, at : at + 128] += jnp.sum(gq.astype(f32), axis=0, keepdims=True)
        gbias_ref[1:2, at : at + 128] += jnp.sum(gv.astype(f32), axis=0, keepdims=True)


def halve(core, value, keep_ref, send_ref, at):
    size = value.shape[0] // 4

    def put(first, second):
        for y in range(2):
            first[y * size : (y + 1) * size, at] = value[2 * y * size : (2 * y + 1) * size]
            second[y * size : (y + 1) * size, at] = value[(2 * y + 1) * size : (2 * y + 2) * size]

    @pl.when(core == 0)
    def _():
        put(keep_ref, send_ref)

    @pl.when(core == 1)
    def _():
        put(send_ref, keep_ref)


def attention_weights_kernel(core_ref, sums1_ref, sums2_ref, gupb_ref, tiles_ref, *refs):
    keep_ref, send_ref, flag_ref, gpacked, sems = refs[-5:]
    count = len(CALLS)
    gpacked_refs, gbias_refs = refs[:count], refs[count : 2 * count]
    flag_ref[0] = 0
    made = []
    for part in range(3):
        columns = slice(part * D, (part + 1) * D)
        at = 0
        for i, (windows, ref) in enumerate(zip(CALLS, gpacked_refs)):
            target = gpacked.at[at : at + windows * TOK, columns]
            copy = pltpu.make_async_copy(ref.at[:, columns], target, sems.at[part * count + i])
            copy.start()
            made.append(copy)
            at += windows * TOK
    gbias = gbias_refs[0][...]
    for ref in gbias_refs[1:]:
        gbias += ref[...]
    rows = [gbias[:2], sums2_ref[2:3, :], sums1_ref[:2, :], sums2_ref[:2, :], sums2_ref[3:4, :], gupb_ref[:4, :]]
    rows = jnp.concatenate(rows + [jnp.zeros((116, D), f32)], axis=0)
    value = jnp.concatenate([rows.T, jnp.zeros((D, 128), f32)], axis=1).astype(bf16)
    halve(core_ref[0], value, keep_ref, send_ref, slice(3 * D, 3 * D + 256))
    turned = tiles_ref[...].T
    for part in range(3):
        for copy in made[part * count : (part + 1) * count]:
            copy.wait()
        columns = slice(part * D, (part + 1) * D)
        halve(core_ref[0], dot(turned, gpacked[:, columns]).astype(bf16), keep_ref, send_ref, columns)


def gelu_parts(hidden):
    size = jnp.abs(hidden)
    power = jnp.exp(hidden * hidden * -0.5)
    denominator = 1.0 + (0.3275911 * 0.7071067811865476) * size
    near = pl.reciprocal(denominator, approx=True)
    near = near * (2.0 - denominator * near)
    series = near * (
        0.254829592
        + near * (-0.284496736 + near * (1.421413741 + near * (-1.453152027 + near * 1.061405429)))
    )
    tail = 0.5 * series * power
    normal = jnp.where(hidden >= 0, 1.0 - tail, tail)
    return hidden * normal, normal + hidden * power * 0.3989422804014327


def middle_kernel(
    core_ref,
    img_ref,
    cot_any,
    gupd_any,
    vec_ref,
    up_ref,
    down_ref,
    *refs,
):
    branch_ref, att_any = refs[:2]
    out_ref, gbr_ref, gupk_ref, gups_ref, gdownk_ref, gdowns_ref, gupb_ref, sums_ref = refs[2:10]
    mid, normed, update, gnorm, active, ghidden, cot_ref, gupd_ref, att_ref, sems = refs[10:]
    step = pl.program_id(0)

    def copies():
        pairs = ((gupd_any, gupd_ref), (cot_any, cot_ref), (att_any, att_ref))
        return [pltpu.make_async_copy(*pair, sems.at[i]) for i, pair in enumerate(pairs)]

    gain = vec_ref[5:6, :]
    shift = vec_ref[6:7, :]

    @pl.when(step == 0)
    def _():
        for copy in copies():
            copy.start()
        for row in range(GH):
            mid[row * GW : (row + 1) * GW, :] = img_ref[row].astype(f32) + join_row(row, branch_ref)
        mid[REAL:, :] = jnp.zeros((DENSE - REAL, D), f32)
        update[...] = jnp.zeros_like(update)
        gnorm[...] = jnp.zeros_like(gnorm)

        def chunk(index, carry):
            here = pl.ds(pl.multiple_of(index * HALF, HALF), HALF)
            unit, _ = unit_of(mid[here, :])
            normed[here, :] = (unit * gain + shift).astype(bf16)
            return carry

        lax.fori_loop(0, DENSE // HALF, chunk, 0)
        copies()[0].wait()

    @pl.when(step < FF // CHUNK)
    def _():
        up_bias = vec_ref[pl.ds(8 + step, 1), :]
        for start, size in SPLITS:
            here = slice(start, start + size)
            hidden = dot(normed[here, :], up_ref[...]) + up_bias
            gactive = dot_bt(gupd_ref[here, :], down_ref[...])
            act, slope = gelu_parts(hidden)
            act = act.astype(bf16)
            gh = (gactive * slope).astype(bf16)
            active[here, :] = act
            ghidden[here, :] = gh
            update[here, :] += dot(act, down_ref[...])
            gnorm[here, :] += dot_bt(gh, up_ref[...])
        gupb_ref[pl.ds(step, 1), :] = jnp.sum(ghidden[...].astype(f32), axis=0, keepdims=True)
        gdown = dot_at(active[...], gupd_ref[...]).astype(bf16)
        halve(core_ref[0], gdown, gdownk_ref, gdowns_ref, slice(None))
        gup = dot_at(normed[...], ghidden[...]).astype(bf16)
        halve(core_ref[0], gup, gupk_ref, gups_ref, slice(None))

    @pl.when(step == FF // CHUNK)
    def _():
        for copy in copies()[1:]:
            copy.wait()
        down_bias = vec_ref[7:8, :]
        for row in range(GH):
            here = slice(row * GW, (row + 1) * GW)
            out_ref[row] = (mid[here, :] + update[here, :] + down_bias).astype(bf16)

        def chunk(index, carry):
            here = pl.ds(pl.multiple_of(index * HALF, HALF), HALF)
            unit, inverse = unit_of(mid[here, :])
            grad = gnorm[here, :]
            cot = cot_ref[here, :]
            result = cot + norm_back(grad, unit, inverse, gain)
            rounded = result.astype(bf16).astype(f32)
            update[here, :] = rounded
            gain_sum, shift_sum, branch_sum, bias_sum = carry
            return (
                gain_sum + jnp.sum((grad * unit).reshape(HALF // 8, 8, D), axis=0),
                shift_sum + jnp.sum(grad.reshape(HALF // 8, 8, D), axis=0),
                branch_sum + jnp.sum(rounded.reshape(HALF // 8, 8, D), axis=0),
                bias_sum + jnp.sum(cot.astype(bf16).astype(f32).reshape(HALF // 8, 8, D), axis=0),
            )

        zero = jnp.zeros((8, D), f32)
        sums = lax.fori_loop(0, DENSE // HALF, chunk, (zero,) * 4)
        sums_ref[...] = jnp.concatenate(
            [jnp.sum(s, axis=0, keepdims=True) for s in sums] + [jnp.zeros((4, D), f32)], axis=0
        )
        gbr_ref[...] = jnp.zeros_like(gbr_ref)
        for row in range(GH):
            spread_row(row, update[row * GW : (row + 1) * GW, :], gbr_ref)
        gout = dot_at(att_ref[...], gbr_ref[...].reshape(WINDOWS * TOK, D))
        halve(core_ref[0], gout.astype(bf16), gupk_ref, gups_ref, slice(None))


def end_kernel(img_ref, gbr_ref, one_ref, two_ref, vec_ref, *refs):
    count = len(CALLS)
    gpacked_refs, gtab_refs = refs[:count], refs[count : 2 * count]
    out_ref, sums_ref, tables_ref, flag_ref, gtiles, gpacked, img, gbr, sems = refs[-9:]
    flag_ref[0] = 0
    made = []
    at = 0
    for i, (windows, ref) in enumerate(zip(CALLS, gpacked_refs)):
        made.append(pltpu.make_async_copy(ref, gpacked.at[at : at + windows * TOK, :], sems.at[i]))
        at += windows * TOK
    made.append(pltpu.make_async_copy(img_ref, img, sems.at[count]))
    made.append(pltpu.make_async_copy(gbr_ref, gbr, sems.at[count + 1]))
    for copy in made:
        copy.start()
    gain = vec_ref[3:4, :]
    at = 0
    for windows, copy in zip(CALLS, made):
        copy.wait()
        here = slice(at * TOK, (at + windows) * TOK)
        value = dot_bt(gpacked[here, : 2 * D], one_ref[:, 128:]) + dot_bt(gpacked[here, 2 * D :], two_ref[:, :D])
        gtiles[at * WIN : (at + windows) * WIN] = value.reshape(windows * WIN, LINE, D)
        at += windows
    for copy in made[count:]:
        copy.wait()
    gain_sum = jnp.zeros((1, D), f32)
    shift_sum = jnp.zeros((1, D), f32)
    for row in range(GH):
        unit, inverse = unit_of(img[row].astype(f32))
        grad = join_row(row, gtiles)
        gain_sum += jnp.sum(grad * unit, axis=0, keepdims=True)
        shift_sum += jnp.sum(grad, axis=0, keepdims=True)
        out_ref[row] = (join_row(row, gbr) + norm_back(grad, unit, inverse, gain)).astype(bf16)
    sums_ref[...] = jnp.concatenate([gain_sum, shift_sum, jnp.zeros((6, D), f32)], axis=0)
    total = gtab_refs[0][...]
    for ref in gtab_refs[1:]:
        total += ref[...]
    entries = 2 * WIN - 1
    rows = total[:128]
    cols = jnp.concatenate([total[128 + 16 :], total[128 : 128 + 16]], axis=0)
    tables = []
    for part in (rows, cols):
        whole_part = jnp.zeros((entries, HD), f32)
        for group in range(4):
            lines = part[32 * group : 32 * group + entries]
            whole_part += lines[:, HD:] if group % 2 else lines[:, :HD]
        tables.append(whole_part)
    flipped = [tables[0][entries - 1 - i : entries - i] for i in range(entries)]
    tables = jnp.concatenate(flipped + [tables[1], jnp.zeros((10, HD), f32)], axis=0)
    tables_ref[...] = jnp.concatenate([tables, jnp.zeros((64, HD), f32)], axis=1)


def pack_kernel(eight_ref, upb_ref, weight_ref, out_ref):
    own = weight_ref.shape[0]
    flat = upb_ref[...].astype(f32)
    rows = [eight_ref[...].astype(f32)] + [flat[:, own * i : own * (i + 1)] for i in range(4)]
    rows = jnp.concatenate(rows, axis=0)
    rows = jnp.concatenate([rows, jnp.zeros((12, 128 - own), f32)], axis=1)
    square = jnp.concatenate([rows, jnp.zeros((116, 128), f32)], axis=0)
    out_ref[:, :128] = square.T[:own].astype(bf16)
    out_ref[:, 128:] = weight_ref[:, : 2 * D]


def regroup(value, own, back=False):
    count = value.shape[1] // (4 * own)
    parts = []
    for i in range(count if back else 4):
        for j in range(4 if back else count):
            at = (j * count + i) * own if back else (4 * j + i) * own
            parts.append(value[:, at : at + own])
    return jnp.concatenate(parts, axis=1)


def pack_feed_kernel(up_ref, down_ref, out_ref):
    own = up_ref.shape[0]
    out_ref[:, :FF] = regroup(up_ref[...].astype(f32), own).astype(bf16)
    for k in range(4):
        part = down_ref[...].astype(f32)[k * own : (k + 1) * own]
        out_ref[:, FF + k * D : FF + (k + 1) * D] = part.astype(bf16)


def unpack_feed_kernel(first, second, up_ref, out_ref, down_ref):
    own = up_ref.shape[0]
    up_ref[...] = regroup(first[:, :FF], own, back=True)
    out_ref[...] = first[:, FF:]
    for k in range(4):
        down_ref[k * own : (k + 1) * own, :] = second[:, k * D : (k + 1) * D]


def unpack_in_kernel(first, second, tables_ref, in_ref, *refs):
    entries = 2 * WIN - 1
    tables = jnp.sum(tables_ref[...], axis=0)
    refs[-2][...] = tables[:entries, :HD]
    refs[-1][...] = tables[entries : 2 * entries, :HD]
    half = first.shape[1]
    in_ref[:, :half] = first
    in_ref[:, half:] = second[:, : 3 * D - half]
    own = first.shape[0]
    square = jnp.concatenate([second[:, 3 * D - half : 3 * D - half + 128], jnp.zeros((128 - own, 128), f32)], axis=0)
    rows = square.T
    for i in range(8):
        refs[i][...] = rows[i : i + 1, :own]
    refs[8][...] = jnp.concatenate([rows[i : i + 1, :own] for i in range(8, 12)], axis=1)


def params(steps=0):
    return pltpu.CompilerParams(
        vmem_limit_bytes=LIMIT, dimension_semantics=("arbitrary",) * steps if steps else None
    )


VMEM = pl.BlockSpec(memory_space=pltpu.VMEM)
SMEM = pl.BlockSpec(memory_space=pltpu.SMEM)


def whole(shape):
    return pl.BlockSpec(shape, lambda i: (0,) * len(shape))


def shaped(shape, dtype):
    return jax.ShapeDtypeStruct(shape, dtype)


def pack_feed(up, down):
    own = up.shape[0]
    return pl.pallas_call(
        pack_feed_kernel,
        out_shape=shaped((own, 2 * FF), bf16),
        in_specs=[VMEM] * 2,
        out_specs=VMEM,
        compiler_params=params(),
        name="pack_feed",
    )(up, down)


FLAG = pl.BlockSpec(memory_space=pltpu.SMEM)
ANY = pl.BlockSpec(memory_space=pl.ANY)
flag_shape = jax.ShapeDtypeStruct((1,), jnp.int32)


def begin(images, before):
    return pl.pallas_call(
        begin_kernel,
        out_shape=(shaped((WINDOWS * WIN, LINE, D), f32), flag_shape),
        in_specs=[VMEM] + [ANY] * len(before),
        out_specs=(VMEM, FLAG),
        compiler_params=params(),
        cost_estimate=pl.CostEstimate(flops=30_000_000, bytes_accessed=6_000_000, transcendentals=0),
        name="begin",
    )(images, *before)


def weigh(count, grad_out, rows, cols, valid, row_table, col_table, before):
    return pl.pallas_call(
        weight_kernel,
        out_shape=(
            shaped((DENSE, D), f32),
            shaped((DENSE, D), bf16),
            shaped((128, 256), bf16),
            shaped((128, 256), bf16),
            flag_shape,
        ),
        in_specs=[SMEM] + [VMEM] * 6 + [ANY] * len(before),
        out_specs=(VMEM,) * 4 + (FLAG,),
        compiler_params=params(),
        cost_estimate=pl.CostEstimate(flops=30_000_000, bytes_accessed=6_000_000, transcendentals=0),
        name="weigh",
    )(count, grad_out, rows, cols, valid, row_table, col_table, *before)


def forward(places, halves, unit, table, hot):
    per = lambda *shape: pl.BlockSpec(shape, lambda i: (i,) + (0,) * (len(shape) - 1))
    return pl.pallas_call(
        forward_kernel,
        grid=(WINDOWS,),
        out_shape=(
            shaped((WINDOWS * TOK, D), bf16),
            shaped((WINDOWS * TOK, 3 * D), bf16),
            shaped((WINDOWS * HEADS, TOK, TOK), bf16),
            shaped((WINDOWS * TOK, D), bf16),
            shaped((WINDOWS * TOK, D), f32),
            shaped((16, D), f32),
            shaped((D, 128 + 2 * D), bf16),
            shaped((D, 2 * D), bf16),
        ),
        in_specs=[SMEM] + [ANY] * 4 + [per(TOK, D), whole((128, 256)), whole((2, TOK, 128))],
        out_specs=(
            per(TOK, D),
            per(TOK, 3 * D),
            per(HEADS, TOK, TOK),
            per(TOK, D),
            per(TOK, D),
            whole((16, D)),
            whole((D, 128 + 2 * D)),
            whole((D, 2 * D)),
        ),
        scratch_shapes=[pltpu.SemaphoreType.DMA((8,))],
        compiler_params=params(1),
        cost_estimate=pl.CostEstimate(flops=30_000_000_000, bytes_accessed=28_000_000, transcendentals=4_000_000),
        name="attend",
    )(places, *halves, unit, table, hot)


def middle(core, images, cot, gupd, vec, weights, branch, attended):
    steps = FF // CHUNK
    at = lambda i: jnp.minimum(i, steps - 1)
    return pl.pallas_call(
        middle_kernel,
        grid=(steps + 1,),
        out_shape=(
            shaped((GH, GW, D), bf16),
            shaped((WINDOWS * WIN, LINE, D), bf16),
            shaped((D // 2, FF + D), bf16),
            shaped((D // 2, FF + D), bf16),
            shaped((D // 2, FF), bf16),
            shaped((D // 2, FF), bf16),
            shaped((8, D), f32),
            shaped((8, D), f32),
        ),
        in_specs=[
            SMEM,
            whole((GH, GW, D)),
            ANY,
            ANY,
            whole((16, D)),
            pl.BlockSpec((D, CHUNK), lambda i: (0, at(i))),
            pl.BlockSpec((D, CHUNK), lambda i: (0, steps + at(i))),
        ]
        + [whole((WINDOWS * WIN, LINE, D)), ANY],
        out_specs=(
            whole((GH, GW, D)),
            whole((WINDOWS * WIN, LINE, D)),
            pl.BlockSpec((D // 2, CHUNK), lambda i: (0, i)),
            pl.BlockSpec((D // 2, CHUNK), lambda i: (0, i)),
            pl.BlockSpec((D // 2, CHUNK), lambda i: (0, at(i))),
            pl.BlockSpec((D // 2, CHUNK), lambda i: (0, at(i))),
            whole((8, D)),
            whole((8, D)),
        ),
        scratch_shapes=[
            pltpu.VMEM((DENSE, D), f32),
            pltpu.VMEM((DENSE, D), bf16),
            pltpu.VMEM((DENSE, D), f32),
            pltpu.VMEM((DENSE, D), f32),
            pltpu.VMEM((DENSE, CHUNK), bf16),
            pltpu.VMEM((DENSE, CHUNK), bf16),
            pltpu.VMEM((DENSE, D), f32),
            pltpu.VMEM((DENSE, D), bf16),
            pltpu.VMEM((WINDOWS * TOK, D), bf16),
            pltpu.SemaphoreType.DMA((3,)),
        ],
        compiler_params=params(1),
        cost_estimate=pl.CostEstimate(flops=50_000_000_000, bytes_accessed=36_000_000, transcendentals=6_000_000),
        name="feed",
    )(core, images, cot, gupd, vec, weights, weights, branch, attended)


def backward(start, count, packed, soft, att, gbr, two, table, hot, before=()):
    per = lambda *shape: pl.BlockSpec(shape, lambda i: (start + i,) + (0,) * (len(shape) - 1))
    return pl.pallas_call(
        backward_kernel,
        grid=(count,),
        out_shape=(
            shaped((count * TOK, 3 * D), bf16),
            shaped((8, D), f32),
            shaped((256, 128), f32),
            flag_shape,
        ),
        in_specs=[
            per(TOK, 3 * D),
            per(HEADS, TOK, TOK),
            per(TOK, D),
            per(TOK, D),
            whole((D, 2 * D)),
            whole((128, 256)),
            whole((2, TOK, 128)),
        ]
        + [ANY] * len(before),
        out_specs=(pl.BlockSpec((TOK, 3 * D), lambda i: (i, 0)), whole((8, D)), whole((256, 128)), FLAG),
        scratch_shapes=[pltpu.VMEM((TOK, D), bf16)],
        compiler_params=params(1),
        cost_estimate=pl.CostEstimate(flops=6_000_000_000 * count, bytes_accessed=9_000_000, transcendentals=0),
        name="attend_back",
    )(packed, soft, att, gbr, two, table, hot, *before)


def attention_weights(core, sums, tiles, gpacked, gbias, before=()):
    return pl.pallas_call(
        attention_weights_kernel,
        grid=(1,),
        out_shape=(shaped((D // 2, 3 * D + 256), bf16),) * 2 + (flag_shape,),
        in_specs=[SMEM]
        + [whole((8, D))] * 3
        + [whole((WINDOWS * TOK, D))]
        + [ANY] * len(CALLS)
        + [whole((8, D))] * len(CALLS)
        + [ANY] * len(before),
        out_specs=(whole((D // 2, 3 * D + 256)),) * 2 + (FLAG,),
        scratch_shapes=[pltpu.VMEM((WINDOWS * TOK, 3 * D), bf16), pltpu.SemaphoreType.DMA((3 * len(CALLS),))],
        compiler_params=params(1),
        cost_estimate=pl.CostEstimate(flops=25_000_000_000, bytes_accessed=18_000_000, transcendentals=0),
        name="attend_weights",
    )(core, *sums, tiles, *gpacked, *gbias, *before)


def end(images, gbr, one, two, vec, gpacked, gtab, before=()):
    return pl.pallas_call(
        end_kernel,
        out_shape=(shaped((GH, GW, D), bf16), shaped((8, D), f32), shaped((64, 128), f32), flag_shape),
        in_specs=[ANY] * 2 + [VMEM] * 3 + [ANY] * len(CALLS) + [VMEM] * len(CALLS) + [ANY] * len(before),
        out_specs=(VMEM, VMEM, VMEM, FLAG),
        scratch_shapes=[
            pltpu.VMEM((WINDOWS * WIN, LINE, D), f32),
            pltpu.VMEM((WINDOWS * TOK, 3 * D), bf16),
            pltpu.VMEM((GH, GW, D), bf16),
            pltpu.VMEM((WINDOWS * WIN, LINE, D), bf16),
            pltpu.SemaphoreType.DMA((len(CALLS) + 2,)),
        ],
        compiler_params=params(),
        cost_estimate=pl.CostEstimate(flops=12_000_000_000, bytes_accessed=17_000_000, transcendentals=0),
        name="end",
    )(images, gbr, one, two, vec, *gpacked, *gtab, *before)


def pack(eight, up_bias, weight):
    return pl.pallas_call(
        pack_kernel,
        out_shape=shaped((weight.shape[0], 128 + 2 * D), bf16),
        in_specs=[VMEM] * 3,
        out_specs=VMEM,
        compiler_params=params(),
        name="pack",
    )(eight, up_bias, weight)


def one_hot_keys(flip):
    token = np.arange(TOK)
    row, col = token // LINE, token % LINE
    lane = np.arange(128)
    group, local = lane // 32, lane % 32
    hot = []
    for head in range(2):
        mine = (group % 2 == head)[None, :]
        value = ((local[None, :] == row[:, None]) & (local < WIN)[None, :]) | (
            (local[None, :] - 16 == (13 - col if flip else col)[:, None]) & (col < WIN)[:, None]
        )
        value = np.where(mine & value, 1.0, 0.0)
        value[:, 14] = np.where(col >= WIN, -1e30, 0.0)
        hot.append(value)
    return jnp.asarray(np.stack(hot), dtype=bf16)


AXES = ("dp", "fsdp")


class Exchange:
    def __init__(self, dp, fsdp):
        self.count = dp * fsdp
        self.bits = []
        bit = self.count // 2
        while bit:
            self.bits.append(bit)
            bit //= 2
        place = lax.axis_index(AXES).astype(jnp.int32)
        self.place = place
        self.mine = [(place >> (bit.bit_length() - 1)) & 1 for bit in self.bits]
        self.places = jnp.stack(self.mine)
        last = len(self.bits) - 1
        low = list(range(last - 1, 1, -1))
        self.orders = ([0, last] + low, [last, 0] + low)

    def swap(self, value, at):
        bit = self.bits[at]
        return lax.ppermute(value, AXES, [(i, i ^ bit) for i in range(self.count)])

    def spread(self, value):
        return value.reshape((1,) * len(self.bits) + value.shape)

    def join(self, value, at, flag=None):
        other = self.swap(value, at)
        mine = self.mine[at] if flag is None else self.mine[at] + flag[0]
        return jnp.where(
            mine == 0, jnp.concatenate([value, other], axis=at), jnp.concatenate([other, value], axis=at)
        )

    def own_part(self, piece, flag=None):
        terms, done, half = piece
        total = None
        for term in terms:
            for at in done:
                if term.shape[at] == 2:
                    mine = self.mine[at] if flag is None else self.mine[at] + flag[0]
                    term = lax.dynamic_index_in_dim(term, mine, at, keepdims=True)
            if half is not None:
                columns = term.shape[-1] // 2
                term = term[..., half * columns : (half + 1) * columns]
            term = term.astype(f32)
            total = term if total is None else total + term
        return total

    def halve(self, value, at):
        leave = lax.dynamic_index_in_dim(value, 1 - self.mine[at], at, keepdims=True).astype(bf16)
        stay = lax.dynamic_index_in_dim(value, self.mine[at], at, keepdims=True)
        return stay, self.swap(leave, at), leave

    def tie(self, values, before):
        count = len(values)

        def kernel(*refs):
            pass

        return pl.pallas_call(
            kernel,
            out_shape=tuple(shaped(v.shape, v.dtype) for v in values),
            in_specs=[ANY] * (count + len(before)),
            out_specs=(ANY,) * count,
            input_output_aliases={i: i for i in range(count)},
            name="tie",
        )(*values, *before)

    def flat(self, value):
        return value.reshape((self.count * value.shape[-2], value.shape[-1]))

    def cut(self, keep, send):
        rows, columns = keep.shape
        shape = (2, 1) + (2,) * (len(self.bits) - 2) + (2 * rows // self.count, columns)
        return [keep.reshape(shape), self.swap(send, 1).reshape(shape)]

    def blocks(self, piece, width, steps, leave=None):
        terms, done, half = piece
        specs = []
        for term in terms:
            shape = term.shape
            block, pick = [], []
            for at in range(len(self.bits)):
                cut = at in done or at == leave
                block.append(1 if cut else shape[at])
                pick.append((at, shape[at] == 2 and cut, at == leave))
            block += [shape[-2], width]
            first = half * steps if half and shape[-1] > width * steps else 0

            def index(i, places, pick=pick, first=first):
                where = [jnp.where(other, 1 - places[at], places[at]) if use else 0 for at, use, other in pick]
                return (*where, 0, first + jnp.minimum(i, steps - 1))

            specs.append(pl.BlockSpec(tuple(block), index))
        return specs

    def narrow(self, pieces, ats, widths, before=()):
        operands, specs, outs, out_specs, counts = [], [], [], [], []
        grid = 1
        for piece, at, width in zip(pieces, ats, widths):
            terms, done, half = piece
            columns = terms[-1].shape[-1] // (2 if half is not None and len(terms) == 2 else 1)
            steps = columns // width
            grid = max(grid, steps)
            specs += self.blocks(piece, width, steps, at)
            operands += terms
            counts.append(len(terms))
            shape = tuple(1 if i in done or i == at else n for i, n in enumerate(terms[0].shape[:-1]))
            outs.append(shaped(shape + (columns,), bf16))
            out_specs.append(
                pl.BlockSpec(
                    shape + (width,),
                    lambda i, places, n=len(shape), steps=steps: (0,) * n + (jnp.minimum(i, steps - 1),),
                )
            )
        count = len(pieces)

        def kernel(places, *refs):
            results = refs[-count - 1 : -1]
            refs[-1][0] = 0
            at = 0
            for i, terms in enumerate(counts):
                total = refs[at][...].astype(f32)
                for ref in refs[at + 1 : at + terms]:
                    total += ref[...].astype(f32)
                results[i][...] = total.astype(bf16)
                at += terms

        size = sum(int(np.prod(o.shape)) for o in outs)
        got = pl.pallas_call(
            kernel,
            grid_spec=pltpu.PrefetchScalarGridSpec(
                num_scalar_prefetch=1,
                grid=(grid,),
                in_specs=specs + [ANY] * len(before),
                out_specs=tuple(out_specs) + (FLAG,),
            ),
            out_shape=tuple(outs) + (flag_shape,),
            compiler_params=params(1),
            cost_estimate=pl.CostEstimate(flops=4 * size, bytes_accessed=8 * size, transcendentals=0),
            name="narrow",
        )(self.places, *operands, *before)
        results = []
        for (terms, done, half), at, leave in zip(pieces, ats, got):
            results.append((terms + [self.swap(leave, at)], done + [at], half))
        return results, [got[-1]]

    def close(self, pieces, kernel, out_shape, name, more=()):
        operands = [part.reshape(part.shape[-2:]) for piece in pieces for part in piece]

        def body(*refs):
            sums = [refs[2 * i][...] + refs[2 * i + 1][...].astype(f32) for i in range(len(pieces))]
            kernel(*sums, *refs[2 * len(pieces) :])

        return pl.pallas_call(
            body,
            out_shape=out_shape,
            in_specs=[VMEM] * (len(operands) + len(more)),
            out_specs=(VMEM,) * len(out_shape),
            compiler_params=params(),
            name=name,
        )(*operands, *more)


def local(
    dp,
    fsdp,
    images,
    grad_out,
    box_rows,
    box_cols,
    box_valid,
    box_count,
    in_weight,
    query_bias,
    value_bias,
    out_weight,
    out_bias,
    first_gain,
    first_shift,
    second_gain,
    second_shift,
    up_weight,
    up_bias,
    down_weight,
    down_bias,
    row_table,
    col_table,
):
    links = Exchange(dp, fsdp)
    image = images[0]
    core = (lax.axis_index("dp") & 1).astype(jnp.int32).reshape(1)
    hot = one_hot_keys(False)
    hot_back = one_hot_keys(True)
    eight = jnp.stack(
        [query_bias, value_bias, out_bias, first_gain, first_shift, second_gain, second_shift, down_bias]
    )
    first, second = links.orders[0][::-1], links.orders[1][::-1]
    last = len(first)
    two = links.spread(jnp.concatenate([in_weight[:, 2 * D :], out_weight], axis=1))
    one = links.spread(pack(eight, up_bias[None], in_weight))
    feed_weights = lax.all_gather(pack_feed(up_weight, down_weight), AXES, axis=0, tiled=True)
    for step in range(last - 2):
        two = links.join(two, second[step])
        one = links.join(one, first[step])
    cot, gupd, table, table_back, flag = weigh(
        box_count, grad_out[0], box_rows[0], box_cols[0], box_valid.reshape(NBOX, 1), row_table, col_table, [two, one]
    )
    two = links.join(two, second[last - 2], flag)
    one = links.join(one, first[last - 2], flag)
    unit, flag = begin(image, [two, one])
    unit = unit.reshape(WINDOWS * TOK, D)
    two = links.join(two, second[last - 1], flag)
    one = links.join(one, first[last - 1], flag)
    halves = [h.reshape(2, D // 4, -1) for h in (one, two, links.swap(one, 1), links.swap(two, 1))]

    tiles, packed, soft, att, branch, vec, one, two = forward(links.places, halves, unit, table, hot)
    block_out, gbr, gup_k, gup_s, gdown_k, gdown_s, gupb, sums2 = middle(
        core, image, cot, gupd, vec, feed_weights, branch.reshape(WINDOWS * WIN, LINE, D), att
    )

    first, second = links.orders
    gbr_flat = gbr.reshape(WINDOWS * TOK, D)
    feed = [(links.cut(gup_k, gup_s), [], None), (links.cut(gdown_k, gdown_s), [], None)]
    back = []
    flag = []
    start = 0
    for windows in CALLS:
        back.append(backward(start, windows, packed, soft, att, gbr_flat, two, table_back, hot_back, flag))
        flag = [back[-1][3]]
        if start == 0:
            feed, flag = links.narrow(feed, (first[0], second[0]), ((FF + D) // 2, FF // 2), flag)
        start += windows
    gpacked = [b[0] for b in back]
    image_grad, sums1, tables, flag = end(image, gbr, one, two, vec, gpacked, [b[2] for b in back], flag)
    feed, flag = links.narrow(feed, (first[1], second[1]), (FF + D, FF), [flag])
    all_tables = lax.all_gather(tables, AXES, axis=0, tiled=False)
    gin_k, gin_s, flag = attention_weights(core, (sums1, sums2, gupb), tiles, gpacked, [b[1] for b in back], flag)
    *recv, gin_s = links.tie([f[0][-1] for f in feed] + [gin_s], [flag])
    feed = [(f[0][:-1] + [r], f[1], f[2]) for f, r in zip(feed, recv)]
    gin = links.cut(gin_k, gin_s)
    feed = [links.halve(links.own_part(f), at) for f, at in zip(feed, (first[2], second[2]))]
    gin = [(links.own_part((gin, [], half)),) for half in range(2)]
    for step in range(last):
        gin = [links.halve(sum(g), at) for g, at in zip([(g[0],) if len(g) == 1 else g[:2] for g in gin], (first[step], second[step]))]
        if 1 <= step < last - 2 or step == last - 1:
            late = links.tie([f[1] for f in feed], [g[2] for g in gin])
            feed = [(f[0], r) for f, r in zip(feed, late)]
        if 1 <= step < last - 2:
            ats = (first[step + 2], second[step + 2])
            feed = [links.halve(f[0] + f[1].astype(f32), at) for f, at in zip(feed, ats)]
    gin = [g[:2] for g in gin]
    feed = [f[:2] for f in feed]
    own = in_weight.shape[0]
    gup, gout, gdown = links.close(
        feed, unpack_feed_kernel, (shaped((own, FF), f32), shaped((own, D), f32), shaped((4 * own, D), f32)), "unpack_feed"
    )
    entries = 2 * WIN - 1
    gin, *out = links.close(
        gin,
        unpack_in_kernel,
        (shaped((own, 3 * D), f32),)
        + (shaped((1, own), f32),) * 8
        + (shaped((1, 4 * own), f32),)
        + (shaped((entries, HD), f32),) * 2,
        "unpack_in",
        [all_tables],
    )
    qb, vb, ob, g1, s1, g2, s2, db, ub = [o.reshape(-1) for o in out[:9]]
    row_grad, col_grad = out[9:]
    return (
        block_out[None],
        image_grad[None],
        gin,
        qb,
        vb,
        gout,
        ob,
        g1,
        s1,
        g2,
        s2,
        gup,
        ub,
        gdown,
        db,
        row_grad,
        col_grad,
    )


def solution(mesh):
    rows = P(AXES)
    dp, fsdp = mesh.shape["dp"], mesh.shape["fsdp"]
    return jax.shard_map(
        lambda *args: local(dp, fsdp, *args),
        mesh=mesh,
        in_specs=(rows,) * 19 + (P(), P()),
        out_specs=(rows,) * 15 + (P(), P()),
        check_vma=False,
    )
```

```python
import functools

import jax
import jax.numpy as jnp
import numpy as np
from jax import lax
from jax.experimental import pallas as pl
from jax.experimental.pallas import tpu as pltpu
from jax.sharding import PartitionSpec as P

D = 768
HEADS = 12
HD = 64
FF = 3072
WIN = 14
GH = 26
GW = 38
NBOX = 300
ACROSS = 3
WINDOWS = 6
LINE = 16
TOK = WIN * LINE
REAL = GH * GW
DENSE = 992
HALF = DENSE // 2
PAIRS = HEADS // 2
STARTS = (0, 14, 28)
WIDTHS = (14, 14, 10)
CHUNK = 768
CALLS = (2, 4)
SPLITS = ((0, 256), (256, 256), (512, 256), (768, 224))
epsilon = 1e-06
f32 = jnp.float32
bf16 = jnp.bfloat16
LIMIT = 60 * 1024 * 1024


def dot(a, b):
    return lax.dot_general(a, b, (((1,), (0,)), ((), ())), preferred_element_type=f32)


def dot_bt(a, b):
    return lax.dot_general(a, b, (((1,), (1,)), ((), ())), preferred_element_type=f32)


def dot_at(a, b):
    return lax.dot_general(a, b, (((0,), (0,)), ((), ())), preferred_element_type=f32)


def unit_of(x):
    center = x - jnp.mean(x, axis=-1, keepdims=True)
    inverse = lax.rsqrt(jnp.mean(center * center, axis=-1, keepdims=True) + epsilon)
    return center * inverse, inverse


def norm_back(grad, unit, inverse, gain):
    scaled = grad * gain
    return inverse * (
        scaled
        - jnp.mean(scaled, axis=-1, keepdims=True)
        - unit * jnp.mean(scaled * unit, axis=-1, keepdims=True)
    )


def place_of(row):
    return (row // WIN) * ACROSS, row % WIN


def spread_row(row, value, out_ref):
    first, place = place_of(row)
    for piece, (start, width) in enumerate(zip(STARTS, WIDTHS)):
        part = value[start : start + width]
        part = jnp.concatenate([part, jnp.zeros((LINE - width, part.shape[1]), part.dtype)], axis=0)
        out_ref[(first + piece) * WIN + place] = part.astype(out_ref.dtype)


def join_row(row, ref):
    first, place = place_of(row)
    return jnp.concatenate(
        [ref[(first + piece) * WIN + place].astype(f32)[:width] for piece, width in enumerate(WIDTHS)], axis=0
    )


def begin_kernel(img_ref, *refs):
    unit_ref, flag_ref = refs[-2:]
    flag_ref[0] = 0
    unit_ref[...] = jnp.zeros_like(unit_ref)
    for row in range(GH):
        unit, _ = unit_of(img_ref[row].astype(f32))
        spread_row(row, unit, unit_ref)


def pair_tables(row_table, col_table, entry_row, entry_col):
    parts = []
    for table, place in ((row_table, entry_row), (col_table, entry_col)):
        pieces = jnp.zeros((128, 128), f32)
        entries = lax.broadcasted_iota(jnp.int32, (2 * WIN - 1, 128), 0)
        lane = lane_iota((2 * WIN - 1, 128))
        row = lax.broadcasted_iota(jnp.int32, (128, 128), 0)
        for head in range(2):
            where = place(entries) + 32 * head
            pick = ((lane - where) % 64) == 0
            spread = dot_at(table, jnp.where(pick, 1.0, 0.0).astype(bf16))
            both = jnp.concatenate([spread, spread], axis=0)
            pieces = jnp.where((row < HD) == (head == 0), both, pieces)
        parts.append(pieces)
    return jnp.concatenate(parts, axis=1).astype(bf16)


def weight_kernel(count_ref, grad_ref, rows_ref, cols_ref, valid_ref, rowt_ref, colt_ref, *refs):
    cot_ref, upd_ref, table_ref, back_ref, flag_ref = refs[-5:]
    flag_ref[0] = 0
    table_ref[...] = pair_tables(rowt_ref[...], colt_ref[...], lambda e: 26 - e, lambda e: 29 - e)
    back_ref[...] = pair_tables(rowt_ref[...], colt_ref[...], lambda e: 26 - e, lambda e: 16 + e)
    slot = lax.broadcasted_iota(jnp.int32, (NBOX, 1), 0)
    live = (slot < count_ref[0]) & (valid_ref[...] == 1)
    rows = rows_ref[...]
    cols = cols_ref[...]
    top = jnp.minimum(rows[:, 0:1], rows[:, 1:2])
    low = jnp.maximum(rows[:, 0:1], rows[:, 1:2])
    left = jnp.minimum(cols[:, 0:1], cols[:, 1:2])
    right = jnp.maximum(cols[:, 0:1], cols[:, 1:2])
    grid_r = lax.broadcasted_iota(jnp.int32, (NBOX, GH), 1)
    grid_c = lax.broadcasted_iota(jnp.int32, (NBOX, GW), 1)
    in_rows = jnp.where((grid_r >= top) & (grid_r < low) & live, 1.0, 0.0)
    in_cols = jnp.where((grid_c >= left) & (grid_c < right), 1.0, 0.0)
    inside = dot_at(in_cols.astype(bf16), in_rows.astype(bf16))
    total = jnp.sum(jnp.where(live, 1.0, 0.0))
    weight = 1.0 + 2.0 * inside / jnp.maximum(total, 1.0)
    for row in range(GH):
        cot_ref[row * GW : (row + 1) * GW, :] = grad_ref[row].astype(f32) * weight[:, row : row + 1]
    cot_ref[REAL:, :] = jnp.zeros((DENSE - REAL, D), f32)
    upd_ref[...] = cot_ref[...].astype(bf16)


def lane_iota(shape):
    return lax.broadcasted_iota(jnp.int32, shape, len(shape) - 1)


def position_terms(queries, table):
    both = dot(queries, table)
    row_part = both[:, :128].reshape(WIN, LINE, 128)
    col_part = both[:, 128:].reshape(WIN, LINE, 128)
    lane = lane_iota((LINE, 128))
    local = lane % 32
    out = []
    for place in range(WIN):
        rolled_r = pltpu.roll(row_part[place], (place - 13) % 128, 1)
        rolled_c = pltpu.roll(col_part[place], 0, 1, stride=1, stride_axis=0)
        value = jnp.where(local < 16, rolled_r, rolled_c)
        high = value.astype(bf16).astype(f32)
        value = jnp.where(lane < 64, high, value - high)
        value = jnp.where(lane == 14, 1.0, value)
        out.append(value)
    return jnp.concatenate(out, axis=0).astype(bf16)


def keep_head(value, head):
    lane = lane_iota(value.shape)
    return jnp.where((lane < HD) == (head == 0), value, jnp.zeros_like(value))


def forward_kernel(places_ref, *refs):
    one_half, two_half, one_other, two_other, unit_ref, table_ref, hot_ref = refs[:7]
    tiles_ref, packed_ref, soft_ref, att_ref, branch_ref, vec_ref, one_ref, two_ref, sems = refs[7:]
    step = pl.program_id(0)

    @pl.when(step == 0)
    def _():
        core = places_ref[1]
        made = []
        for i, (half, whole_ref, place) in enumerate(
            [
                (one_half, one_ref, core),
                (two_half, two_ref, core),
                (one_other, one_ref, 1 - core),
                (two_other, two_ref, 1 - core),
            ]
        ):
            for y in range(2):
                here = pl.ds(pl.multiple_of((2 * y + place) * (D // 4), D // 4), D // 4)
                copy = pltpu.make_async_copy(half.at[y], whole_ref.at[here, :], sems.at[2 * i + y])
                copy.start()
                made.append(copy)
        for copy in made:
            copy.wait()
        vec_ref[...] = one_ref[:, :128].astype(f32).T[:16]

    window = step
    token = lax.broadcasted_iota(jnp.int32, (TOK, 1), 0)
    row_limit = jnp.where(window < ACROSS, WIN, GH - WIN)
    col_limit = jnp.where(window % ACROSS == ACROSS - 1, WIDTHS[2], WIN)
    valid = (token // LINE < row_limit) & (token % LINE < col_limit)
    tiles_ref[...] = (unit_ref[...] * vec_ref[3:4, :] + jnp.where(valid, vec_ref[4:5, :], 0.0)).astype(bf16)
    tiles = tiles_ref[...]
    packed_ref[:, :D] = (dot(tiles, one_ref[:, 128 : 128 + D]) + vec_ref[0:1, :]).astype(bf16)
    packed_ref[:, D : 2 * D] = dot(tiles, one_ref[:, 128 + D :]).astype(bf16)
    packed_ref[:, 2 * D :] = (dot(tiles, two_ref[:, :D]) + vec_ref[1:2, :]).astype(bf16)
    for pair in range(PAIRS):
        at = pair * 128
        queries = packed_ref[:, at : at + 128]
        keys = packed_ref[:, D + at : D + at + 128]
        values = packed_ref[:, 2 * D + at : 2 * D + at + 128]
        left = jnp.concatenate([queries, position_terms(queries, table_ref[...])], axis=1)
        parts = []
        for head in range(2):
            scaled = (keep_head(keys.astype(f32), head) * 0.125).astype(bf16)
            right = jnp.concatenate([scaled, hot_ref[head]], axis=1)
            scores = dot_bt(left, right)
            power = jnp.exp(scores - jnp.max(scores, axis=-1, keepdims=True))
            soft = (power * (1.0 / jnp.sum(power, axis=-1, keepdims=True))).astype(bf16)
            soft_ref[2 * pair + head] = soft
            parts.append(dot(soft, values))
        lane = lane_iota((TOK, 128))
        att_ref[:, at : at + 128] = jnp.where(lane < HD, parts[0], parts[1]).astype(bf16)
    branch_ref[...] = dot(att_ref[...], two_ref[:, D:]) + vec_ref[2:3, :]


def backward_kernel(packed_ref, soft_ref, att_ref, gbr_ref, two_ref, table_ref, hot_ref, *refs):
    gpacked_ref, gbias_ref, gtab_ref, flag_ref, gatt_ref = refs[-5:]

    @pl.when(pl.program_id(0) == 0)
    def _():
        flag_ref[0] = 0
        gbias_ref[...] = jnp.zeros_like(gbias_ref)
        gtab_ref[...] = jnp.zeros_like(gtab_ref)

    gatt_ref[...] = dot_bt(gbr_ref[...], two_ref[:, D:]).astype(bf16)
    lane = lane_iota((LINE, 128))
    local = lane % 32
    wide = lane_iota((TOK, 128))
    for pair in range(PAIRS):
        at = pair * 128
        queries = packed_ref[:, at : at + 128]
        keys = packed_ref[:, D + at : D + at + 128]
        values = packed_ref[:, 2 * D + at : 2 * D + at + 128]
        gatt = gatt_ref[:, at : at + 128]
        product = gatt.astype(f32) * att_ref[:, at : at + 128].astype(f32)
        left = []
        right = []
        gvalues = []
        gkeys = []
        turned_g = gatt.T
        turned_q = queries.T
        for head in range(2):
            soft = soft_ref[2 * pair + head]
            delta = jnp.sum(keep_head(product, head), axis=-1, keepdims=True)
            gprobs = dot_bt(gatt, keep_head(values.astype(f32), head).astype(bf16))
            gscores = (soft.astype(f32) * (gprobs - delta)).astype(bf16)
            scaled = (keep_head(keys.astype(f32), head) * 0.125).astype(bf16)
            left.append(gscores)
            right.append(jnp.concatenate([scaled, hot_ref[head]], axis=1))
            rows = slice(head * HD, (head + 1) * HD)
            gvalues.append(dot(turned_g[rows], soft))
            gkeys.append(dot(turned_q[rows], gscores))
        both = dot(left[0], right[0]) + dot(left[1], right[1])
        terms = both[:, 128:].reshape(WIN, LINE, 128)
        rolled = []
        for place in range(WIN):
            value = terms[place]
            high = value.astype(bf16).astype(f32)
            value = jnp.where(lane < 64, high, value - high)
            row_part = jnp.where(local < WIN, value, 0.0)
            col_part = jnp.where((local >= 16) & (local < 16 + WIN), value, 0.0)
            row_part = pltpu.roll(row_part, 13 - place, 1)
            col_part = pltpu.roll(col_part, 0, 1, stride=1, stride_axis=0)
            rolled.append(jnp.concatenate([row_part, col_part], axis=1))
        rolled = jnp.concatenate(rolled, axis=0).astype(bf16)
        gqueries = both[:, :128] + dot_bt(rolled, table_ref[...])
        gtab_ref[...] += dot_at(rolled, queries)
        gq = gqueries.astype(bf16)
        gk = (jnp.concatenate(gkeys, axis=0) * 0.125).astype(bf16).T
        gv = jnp.concatenate(gvalues, axis=0).astype(bf16).T
        gpacked_ref[:, at : at + 128] = gq
        gpacked_ref[:, D + at : D + at + 128] = gk
        gpacked_ref[:, 2 * D + at : 2 * D + at + 128] = gv
        gbias_ref[0:1, at : at + 128] += jnp.sum(gq.astype(f32), axis=0, keepdims=True)
        gbias_ref[1:2, at : at + 128] += jnp.sum(gv.astype(f32), axis=0, keepdims=True)


def halve(core, value, keep_ref, send_ref, at):
    size = value.shape[0] // 4

    def put(first, second):
        for y in range(2):
            first[y * size : (y + 1) * size, at] = value[2 * y * size : (2 * y + 1) * size]
            second[y * size : (y + 1) * size, at] = value[(2 * y + 1) * size : (2 * y + 2) * size]

    @pl.when(core == 0)
    def _():
        put(keep_ref, send_ref)

    @pl.when(core == 1)
    def _():
        put(send_ref, keep_ref)


def attention_weights_kernel(core_ref, sums1_ref, sums2_ref, gupb_ref, tiles_ref, *refs):
    keep_ref, send_ref, flag_ref, gpacked, sems = refs[-5:]
    count = len(CALLS)
    gpacked_refs, gbias_refs = refs[:count], refs[count : 2 * count]
    flag_ref[0] = 0
    made = []
    for part in range(3):
        columns = slice(part * D, (part + 1) * D)
        at = 0
        for i, (windows, ref) in enumerate(zip(CALLS, gpacked_refs)):
            target = gpacked.at[at : at + windows * TOK, columns]
            copy = pltpu.make_async_copy(ref.at[:, columns], target, sems.at[part * count + i])
            copy.start()
            made.append(copy)
            at += windows * TOK
    gbias = gbias_refs[0][...]
    for ref in gbias_refs[1:]:
        gbias += ref[...]
    rows = [gbias[:2], sums2_ref[2:3, :], sums1_ref[:2, :], sums2_ref[:2, :], sums2_ref[3:4, :], gupb_ref[:4, :]]
    rows = jnp.concatenate(rows + [jnp.zeros((116, D), f32)], axis=0)
    value = jnp.concatenate([rows.T, jnp.zeros((D, 128), f32)], axis=1).astype(bf16)
    halve(core_ref[0], value, keep_ref, send_ref, slice(3 * D, 3 * D + 256))
    turned = tiles_ref[...].T
    for part in range(3):
        for copy in made[part * count : (part + 1) * count]:
            copy.wait()
        columns = slice(part * D, (part + 1) * D)
        halve(core_ref[0], dot(turned, gpacked[:, columns]).astype(bf16), keep_ref, send_ref, columns)


def gelu_parts(hidden):
    size = jnp.abs(hidden)
    power = jnp.exp(hidden * hidden * -0.5)
    denominator = 1.0 + (0.3275911 * 0.7071067811865476) * size
    near = pl.reciprocal(denominator, approx=True)
    near = near * (2.0 - denominator * near)
    series = near * (
        0.254829592
        + near * (-0.284496736 + near * (1.421413741 + near * (-1.453152027 + near * 1.061405429)))
    )
    tail = 0.5 * series * power
    normal = jnp.where(hidden >= 0, 1.0 - tail, tail)
    return hidden * normal, normal + hidden * power * 0.3989422804014327


def middle_kernel(
    core_ref,
    img_ref,
    cot_any,
    gupd_any,
    vec_ref,
    up_ref,
    down_ref,
    *refs,
):
    branch_ref, att_any = refs[:2]
    out_ref, gbr_ref, gupk_ref, gups_ref, gdownk_ref, gdowns_ref, gupb_ref, sums_ref = refs[2:10]
    mid, normed, update, gnorm, active, ghidden, cot_ref, gupd_ref, att_ref, sems = refs[10:]
    step = pl.program_id(0)

    def copies():
        pairs = ((gupd_any, gupd_ref), (cot_any, cot_ref), (att_any, att_ref))
        return [pltpu.make_async_copy(*pair, sems.at[i]) for i, pair in enumerate(pairs)]

    gain = vec_ref[5:6, :]
    shift = vec_ref[6:7, :]

    @pl.when(step == 0)
    def _():
        for copy in copies():
            copy.start()
        for row in range(GH):
            mid[row * GW : (row + 1) * GW, :] = img_ref[row].astype(f32) + join_row(row, branch_ref)
        mid[REAL:, :] = jnp.zeros((DENSE - REAL, D), f32)
        update[...] = jnp.zeros_like(update)
        gnorm[...] = jnp.zeros_like(gnorm)

        def chunk(index, carry):
            here = pl.ds(pl.multiple_of(index * HALF, HALF), HALF)
            unit, _ = unit_of(mid[here, :])
            normed[here, :] = (unit * gain + shift).astype(bf16)
            return carry

        lax.fori_loop(0, DENSE // HALF, chunk, 0)
        copies()[0].wait()

    @pl.when(step < FF // CHUNK)
    def _():
        up_bias = vec_ref[pl.ds(8 + step, 1), :]
        for start, size in SPLITS:
            here = slice(start, start + size)
            hidden = dot(normed[here, :], up_ref[...]) + up_bias
            gactive = dot_bt(gupd_ref[here, :], down_ref[...])
            act, slope = gelu_parts(hidden)
            act = act.astype(bf16)
            gh = (gactive * slope).astype(bf16)
            active[here, :] = act
            ghidden[here, :] = gh
            update[here, :] += dot(act, down_ref[...])
            gnorm[here, :] += dot_bt(gh, up_ref[...])
        gupb_ref[pl.ds(step, 1), :] = jnp.sum(ghidden[...].astype(f32), axis=0, keepdims=True)
        gdown = dot_at(active[...], gupd_ref[...]).astype(bf16)
        halve(core_ref[0], gdown, gdownk_ref, gdowns_ref, slice(None))
        gup = dot_at(normed[...], ghidden[...]).astype(bf16)
        halve(core_ref[0], gup, gupk_ref, gups_ref, slice(None))

    @pl.when(step == FF // CHUNK)
    def _():
        for copy in copies()[1:]:
            copy.wait()
        down_bias = vec_ref[7:8, :]
        for row in range(GH):
            here = slice(row * GW, (row + 1) * GW)
            out_ref[row] = (mid[here, :] + update[here, :] + down_bias).astype(bf16)

        def chunk(index, carry):
            here = pl.ds(pl.multiple_of(index * HALF, HALF), HALF)
            unit, inverse = unit_of(mid[here, :])
            grad = gnorm[here, :]
            cot = cot_ref[here, :]
            result = cot + norm_back(grad, unit, inverse, gain)
            rounded = result.astype(bf16).astype(f32)
            update[here, :] = rounded
            gain_sum, shift_sum, branch_sum, bias_sum = carry
            return (
                gain_sum + jnp.sum((grad * unit).reshape(HALF // 8, 8, D), axis=0),
                shift_sum + jnp.sum(grad.reshape(HALF // 8, 8, D), axis=0),
                branch_sum + jnp.sum(rounded.reshape(HALF // 8, 8, D), axis=0),
                bias_sum + jnp.sum(cot.astype(bf16).astype(f32).reshape(HALF // 8, 8, D), axis=0),
            )

        zero = jnp.zeros((8, D), f32)
        sums = lax.fori_loop(0, DENSE // HALF, chunk, (zero,) * 4)
        sums_ref[...] = jnp.concatenate(
            [jnp.sum(s, axis=0, keepdims=True) for s in sums] + [jnp.zeros((4, D), f32)], axis=0
        )
        gbr_ref[...] = jnp.zeros_like(gbr_ref)
        for row in range(GH):
            spread_row(row, update[row * GW : (row + 1) * GW, :], gbr_ref)
        gout = dot_at(att_ref[...], gbr_ref[...].reshape(WINDOWS * TOK, D))
        halve(core_ref[0], gout.astype(bf16), gupk_ref, gups_ref, slice(None))


def end_kernel(img_ref, gbr_ref, one_ref, two_ref, vec_ref, *refs):
    count = len(CALLS)
    gpacked_refs, gtab_refs = refs[:count], refs[count : 2 * count]
    out_ref, sums_ref, tables_ref, flag_ref, gtiles, gpacked, img, gbr, sems = refs[-9:]
    flag_ref[0] = 0
    made = []
    at = 0
    for i, (windows, ref) in enumerate(zip(CALLS, gpacked_refs)):
        made.append(pltpu.make_async_copy(ref, gpacked.at[at : at + windows * TOK, :], sems.at[i]))
        at += windows * TOK
    made.append(pltpu.make_async_copy(img_ref, img, sems.at[count]))
    made.append(pltpu.make_async_copy(gbr_ref, gbr, sems.at[count + 1]))
    for copy in made:
        copy.start()
    gain = vec_ref[3:4, :]
    at = 0
    for windows, copy in zip(CALLS, made):
        copy.wait()
        here = slice(at * TOK, (at + windows) * TOK)
        value = dot_bt(gpacked[here, : 2 * D], one_ref[:, 128:]) + dot_bt(gpacked[here, 2 * D :], two_ref[:, :D])
        gtiles[at * WIN : (at + windows) * WIN] = value.reshape(windows * WIN, LINE, D)
        at += windows
    for copy in made[count:]:
        copy.wait()
    gain_sum = jnp.zeros((1, D), f32)
    shift_sum = jnp.zeros((1, D), f32)
    for row in range(GH):
        unit, inverse = unit_of(img[row].astype(f32))
        grad = join_row(row, gtiles)
        gain_sum += jnp.sum(grad * unit, axis=0, keepdims=True)
        shift_sum += jnp.sum(grad, axis=0, keepdims=True)
        out_ref[row] = (join_row(row, gbr) + norm_back(grad, unit, inverse, gain)).astype(bf16)
    sums_ref[...] = jnp.concatenate([gain_sum, shift_sum, jnp.zeros((6, D), f32)], axis=0)
    total = gtab_refs[0][...]
    for ref in gtab_refs[1:]:
        total += ref[...]
    entries = 2 * WIN - 1
    rows = total[:128]
    cols = jnp.concatenate([total[128 + 16 :], total[128 : 128 + 16]], axis=0)
    tables = []
    for part in (rows, cols):
        whole_part = jnp.zeros((entries, HD), f32)
        for group in range(4):
            lines = part[32 * group : 32 * group + entries]
            whole_part += lines[:, HD:] if group % 2 else lines[:, :HD]
        tables.append(whole_part)
    flipped = [tables[0][entries - 1 - i : entries - i] for i in range(entries)]
    tables = jnp.concatenate(flipped + [tables[1], jnp.zeros((10, HD), f32)], axis=0)
    tables_ref[...] = jnp.concatenate([tables, jnp.zeros((64, HD), f32)], axis=1)


def pack_kernel(eight_ref, upb_ref, weight_ref, out_ref):
    own = weight_ref.shape[0]
    flat = upb_ref[...].astype(f32)
    rows = [eight_ref[...].astype(f32)] + [flat[:, own * i : own * (i + 1)] for i in range(4)]
    rows = jnp.concatenate(rows, axis=0)
    rows = jnp.concatenate([rows, jnp.zeros((12, 128 - own), f32)], axis=1)
    square = jnp.concatenate([rows, jnp.zeros((116, 128), f32)], axis=0)
    out_ref[:, :128] = square.T[:own].astype(bf16)
    out_ref[:, 128:] = weight_ref[:, : 2 * D]


def regroup(value, own, back=False):
    count = value.shape[1] // (4 * own)
    parts = []
    for i in range(count if back else 4):
        for j in range(4 if back else count):
            at = (j * count + i) * own if back else (4 * j + i) * own
            parts.append(value[:, at : at + own])
    return jnp.concatenate(parts, axis=1)


def pack_feed_kernel(up_ref, down_ref, out_ref):
    own = up_ref.shape[0]
    out_ref[:, :FF] = regroup(up_ref[...].astype(f32), own).astype(bf16)
    for k in range(4):
        part = down_ref[...].astype(f32)[k * own : (k + 1) * own]
        out_ref[:, FF + k * D : FF + (k + 1) * D] = part.astype(bf16)


def unpack_feed_kernel(first, second, up_ref, out_ref, down_ref):
    own = up_ref.shape[0]
    up_ref[...] = regroup(first[:, :FF], own, back=True)
    out_ref[...] = first[:, FF:]
    for k in range(4):
        down_ref[k * own : (k + 1) * own, :] = second[:, k * D : (k + 1) * D]


def unpack_in_kernel(first, second, tables_ref, in_ref, *refs):
    entries = 2 * WIN - 1
    tables = jnp.sum(tables_ref[...], axis=0)
    refs[-2][...] = tables[:entries, :HD]
    refs[-1][...] = tables[entries : 2 * entries, :HD]
    half = first.shape[1]
    in_ref[:, :half] = first
    in_ref[:, half:] = second[:, : 3 * D - half]
    own = first.shape[0]
    square = jnp.concatenate([second[:, 3 * D - half : 3 * D - half + 128], jnp.zeros((128 - own, 128), f32)], axis=0)
    rows = square.T
    for i in range(8):
        refs[i][...] = rows[i : i + 1, :own]
    refs[8][...] = jnp.concatenate([rows[i : i + 1, :own] for i in range(8, 12)], axis=1)


def params(steps=0):
    return pltpu.CompilerParams(
        vmem_limit_bytes=LIMIT, dimension_semantics=("arbitrary",) * steps if steps else None
    )


VMEM = pl.BlockSpec(memory_space=pltpu.VMEM)
SMEM = pl.BlockSpec(memory_space=pltpu.SMEM)


def whole(shape):
    return pl.BlockSpec(shape, lambda i: (0,) * len(shape))


def shaped(shape, dtype):
    return jax.ShapeDtypeStruct(shape, dtype)


def pack_feed(up, down):
    own = up.shape[0]
    return pl.pallas_call(
        pack_feed_kernel,
        out_shape=shaped((own, 2 * FF), bf16),
        in_specs=[VMEM] * 2,
        out_specs=VMEM,
        compiler_params=params(),
        name="pack_feed",
    )(up, down)


FLAG = pl.BlockSpec(memory_space=pltpu.SMEM)
ANY = pl.BlockSpec(memory_space=pl.ANY)
flag_shape = jax.ShapeDtypeStruct((1,), jnp.int32)


def begin(images, before):
    return pl.pallas_call(
        begin_kernel,
        out_shape=(shaped((WINDOWS * WIN, LINE, D), f32), flag_shape),
        in_specs=[VMEM] + [ANY] * len(before),
        out_specs=(VMEM, FLAG),
        compiler_params=params(),
        cost_estimate=pl.CostEstimate(flops=30_000_000, bytes_accessed=6_000_000, transcendentals=0),
        name="begin",
    )(images, *before)


def weigh(count, grad_out, rows, cols, valid, row_table, col_table, before):
    return pl.pallas_call(
        weight_kernel,
        out_shape=(
            shaped((DENSE, D), f32),
            shaped((DENSE, D), bf16),
            shaped((128, 256), bf16),
            shaped((128, 256), bf16),
            flag_shape,
        ),
        in_specs=[SMEM] + [VMEM] * 6 + [ANY] * len(before),
        out_specs=(VMEM,) * 4 + (FLAG,),
        compiler_params=params(),
        cost_estimate=pl.CostEstimate(flops=30_000_000, bytes_accessed=6_000_000, transcendentals=0),
        name="weigh",
    )(count, grad_out, rows, cols, valid, row_table, col_table, *before)


def forward(places, halves, unit, table, hot):
    per = lambda *shape: pl.BlockSpec(shape, lambda i: (i,) + (0,) * (len(shape) - 1))
    return pl.pallas_call(
        forward_kernel,
        grid=(WINDOWS,),
        out_shape=(
            shaped((WINDOWS * TOK, D), bf16),
            shaped((WINDOWS * TOK, 3 * D), bf16),
            shaped((WINDOWS * HEADS, TOK, TOK), bf16),
            shaped((WINDOWS * TOK, D), bf16),
            shaped((WINDOWS * TOK, D), f32),
            shaped((16, D), f32),
            shaped((D, 128 + 2 * D), bf16),
            shaped((D, 2 * D), bf16),
        ),
        in_specs=[SMEM] + [ANY] * 4 + [per(TOK, D), whole((128, 256)), whole((2, TOK, 128))],
        out_specs=(
            per(TOK, D),
            per(TOK, 3 * D),
            per(HEADS, TOK, TOK),
            per(TOK, D),
            per(TOK, D),
            whole((16, D)),
            whole((D, 128 + 2 * D)),
            whole((D, 2 * D)),
        ),
        scratch_shapes=[pltpu.SemaphoreType.DMA((8,))],
        compiler_params=params(1),
        cost_estimate=pl.CostEstimate(flops=30_000_000_000, bytes_accessed=28_000_000, transcendentals=4_000_000),
        name="attend",
    )(places, *halves, unit, table, hot)


def middle(core, images, cot, gupd, vec, weights, branch, attended):
    steps = FF // CHUNK
    at = lambda i: jnp.minimum(i, steps - 1)
    return pl.pallas_call(
        middle_kernel,
        grid=(steps + 1,),
        out_shape=(
            shaped((GH, GW, D), bf16),
            shaped((WINDOWS * WIN, LINE, D), bf16),
            shaped((D // 2, FF + D), bf16),
            shaped((D // 2, FF + D), bf16),
            shaped((D // 2, FF), bf16),
            shaped((D // 2, FF), bf16),
            shaped((8, D), f32),
            shaped((8, D), f32),
        ),
        in_specs=[
            SMEM,
            whole((GH, GW, D)),
            ANY,
            ANY,
            whole((16, D)),
            pl.BlockSpec((D, CHUNK), lambda i: (0, at(i))),
            pl.BlockSpec((D, CHUNK), lambda i: (0, steps + at(i))),
        ]
        + [whole((WINDOWS * WIN, LINE, D)), ANY],
        out_specs=(
            whole((GH, GW, D)),
            whole((WINDOWS * WIN, LINE, D)),
            pl.BlockSpec((D // 2, CHUNK), lambda i: (0, i)),
            pl.BlockSpec((D // 2, CHUNK), lambda i: (0, i)),
            pl.BlockSpec((D // 2, CHUNK), lambda i: (0, at(i))),
            pl.BlockSpec((D // 2, CHUNK), lambda i: (0, at(i))),
            whole((8, D)),
            whole((8, D)),
        ),
        scratch_shapes=[
            pltpu.VMEM((DENSE, D), f32),
            pltpu.VMEM((DENSE, D), bf16),
            pltpu.VMEM((DENSE, D), f32),
            pltpu.VMEM((DENSE, D), f32),
            pltpu.VMEM((DENSE, CHUNK), bf16),
            pltpu.VMEM((DENSE, CHUNK), bf16),
            pltpu.VMEM((DENSE, D), f32),
            pltpu.VMEM((DENSE, D), bf16),
            pltpu.VMEM((WINDOWS * TOK, D), bf16),
            pltpu.SemaphoreType.DMA((3,)),
        ],
        compiler_params=params(1),
        cost_estimate=pl.CostEstimate(flops=50_000_000_000, bytes_accessed=36_000_000, transcendentals=6_000_000),
        name="feed",
    )(core, images, cot, gupd, vec, weights, weights, branch, attended)


def backward(start, count, packed, soft, att, gbr, two, table, hot, before=()):
    per = lambda *shape: pl.BlockSpec(shape, lambda i: (start + i,) + (0,) * (len(shape) - 1))
    return pl.pallas_call(
        backward_kernel,
        grid=(count,),
        out_shape=(
            shaped((count * TOK, 3 * D), bf16),
            shaped((8, D), f32),
            shaped((256, 128), f32),
            flag_shape,
        ),
        in_specs=[
            per(TOK, 3 * D),
            per(HEADS, TOK, TOK),
            per(TOK, D),
            per(TOK, D),
            whole((D, 2 * D)),
            whole((128, 256)),
            whole((2, TOK, 128)),
        ]
        + [ANY] * len(before),
        out_specs=(pl.BlockSpec((TOK, 3 * D), lambda i: (i, 0)), whole((8, D)), whole((256, 128)), FLAG),
        scratch_shapes=[pltpu.VMEM((TOK, D), bf16)],
        compiler_params=params(1),
        cost_estimate=pl.CostEstimate(flops=1_000_000_000, bytes_accessed=2_000_000, transcendentals=0),
        name="attend_back",
    )(packed, soft, att, gbr, two, table, hot, *before)


def attention_weights(core, sums, tiles, gpacked, gbias, before=()):
    return pl.pallas_call(
        attention_weights_kernel,
        grid=(1,),
        out_shape=(shaped((D // 2, 3 * D + 256), bf16),) * 2 + (flag_shape,),
        in_specs=[SMEM]
        + [whole((8, D))] * 3
        + [whole((WINDOWS * TOK, D))]
        + [ANY] * len(CALLS)
        + [whole((8, D))] * len(CALLS)
        + [ANY] * len(before),
        out_specs=(whole((D // 2, 3 * D + 256)),) * 2 + (FLAG,),
        scratch_shapes=[pltpu.VMEM((WINDOWS * TOK, 3 * D), bf16), pltpu.SemaphoreType.DMA((3 * len(CALLS),))],
        compiler_params=params(1),
        cost_estimate=pl.CostEstimate(flops=1_000_000_000, bytes_accessed=2_000_000, transcendentals=0),
        name="attend_weights",
    )(core, *sums, tiles, *gpacked, *gbias, *before)


def end(images, gbr, one, two, vec, gpacked, gtab, before=()):
    return pl.pallas_call(
        end_kernel,
        out_shape=(shaped((GH, GW, D), bf16), shaped((8, D), f32), shaped((64, 128), f32), flag_shape),
        in_specs=[ANY] * 2 + [VMEM] * 3 + [ANY] * len(CALLS) + [VMEM] * len(CALLS) + [ANY] * len(before),
        out_specs=(VMEM, VMEM, VMEM, FLAG),
        scratch_shapes=[
            pltpu.VMEM((WINDOWS * WIN, LINE, D), f32),
            pltpu.VMEM((WINDOWS * TOK, 3 * D), bf16),
            pltpu.VMEM((GH, GW, D), bf16),
            pltpu.VMEM((WINDOWS * WIN, LINE, D), bf16),
            pltpu.SemaphoreType.DMA((len(CALLS) + 2,)),
        ],
        compiler_params=params(),
        cost_estimate=pl.CostEstimate(flops=1_000_000_000, bytes_accessed=2_000_000, transcendentals=0),
        name="end",
    )(images, gbr, one, two, vec, *gpacked, *gtab, *before)


def pack(eight, up_bias, weight):
    return pl.pallas_call(
        pack_kernel,
        out_shape=shaped((weight.shape[0], 128 + 2 * D), bf16),
        in_specs=[VMEM] * 3,
        out_specs=VMEM,
        compiler_params=params(),
        name="pack",
    )(eight, up_bias, weight)


def one_hot_keys(flip):
    token = np.arange(TOK)
    row, col = token // LINE, token % LINE
    lane = np.arange(128)
    group, local = lane // 32, lane % 32
    hot = []
    for head in range(2):
        mine = (group % 2 == head)[None, :]
        value = ((local[None, :] == row[:, None]) & (local < WIN)[None, :]) | (
            (local[None, :] - 16 == (13 - col if flip else col)[:, None]) & (col < WIN)[:, None]
        )
        value = np.where(mine & value, 1.0, 0.0)
        value[:, 14] = np.where(col >= WIN, -1e30, 0.0)
        hot.append(value)
    return jnp.asarray(np.stack(hot), dtype=bf16)


AXES = ("dp", "fsdp")


class Exchange:
    def __init__(self, dp, fsdp):
        self.count = dp * fsdp
        self.bits = []
        bit = self.count // 2
        while bit:
            self.bits.append(bit)
            bit //= 2
        place = lax.axis_index(AXES).astype(jnp.int32)
        self.place = place
        self.mine = [(place >> (bit.bit_length() - 1)) & 1 for bit in self.bits]
        self.places = jnp.stack(self.mine)
        last = len(self.bits) - 1
        low = list(range(last - 1, 1, -1))
        self.orders = ([0, last] + low, [last, 0] + low)

    def swap(self, value, at):
        bit = self.bits[at]
        return lax.ppermute(value, AXES, [(i, i ^ bit) for i in range(self.count)])

    def spread(self, value):
        return value.reshape((1,) * len(self.bits) + value.shape)

    def join(self, value, at, flag=None):
        other = self.swap(value, at)
        mine = self.mine[at] if flag is None else self.mine[at] + flag[0]
        return jnp.where(
            mine == 0, jnp.concatenate([value, other], axis=at), jnp.concatenate([other, value], axis=at)
        )

    def own_part(self, piece, flag=None):
        terms, done, half = piece
        total = None
        for term in terms:
            for at in done:
                if term.shape[at] == 2:
                    mine = self.mine[at] if flag is None else self.mine[at] + flag[0]
                    term = lax.dynamic_index_in_dim(term, mine, at, keepdims=True)
            if half is not None:
                columns = term.shape[-1] // 2
                term = term[..., half * columns : (half + 1) * columns]
            term = term.astype(f32)
            total = term if total is None else total + term
        return total

    def halve(self, value, at):
        leave = lax.dynamic_index_in_dim(value, 1 - self.mine[at], at, keepdims=True).astype(bf16)
        stay = lax.dynamic_index_in_dim(value, self.mine[at], at, keepdims=True)
        return stay, self.swap(leave, at), leave

    def tie(self, values, before):
        count = len(values)

        def kernel(*refs):
            pass

        return pl.pallas_call(
            kernel,
            out_shape=tuple(shaped(v.shape, v.dtype) for v in values),
            in_specs=[ANY] * (count + len(before)),
            out_specs=(ANY,) * count,
            input_output_aliases={i: i for i in range(count)},
            name="tie",
        )(*values, *before)

    def flat(self, value):
        return value.reshape((self.count * value.shape[-2], value.shape[-1]))

    def cut(self, keep, send):
        rows, columns = keep.shape
        shape = (2, 1) + (2,) * (len(self.bits) - 2) + (2 * rows // self.count, columns)
        return [keep.reshape(shape), self.swap(send, 1).reshape(shape)]

    def blocks(self, piece, width, steps, leave=None):
        terms, done, half = piece
        specs = []
        for term in terms:
            shape = term.shape
            block, pick = [], []
            for at in range(len(self.bits)):
                cut = at in done or at == leave
                block.append(1 if cut else shape[at])
                pick.append((at, shape[at] == 2 and cut, at == leave))
            block += [shape[-2], width]
            first = half * steps if half and shape[-1] > width * steps else 0

            def index(i, places, pick=pick, first=first):
                where = [jnp.where(other, 1 - places[at], places[at]) if use else 0 for at, use, other in pick]
                return (*where, 0, first + jnp.minimum(i, steps - 1))

            specs.append(pl.BlockSpec(tuple(block), index))
        return specs

    def narrow(self, pieces, ats, widths, before=()):
        operands, specs, outs, out_specs, counts = [], [], [], [], []
        grid = 1
        for piece, at, width in zip(pieces, ats, widths):
            terms, done, half = piece
            columns = terms[-1].shape[-1] // (2 if half is not None and len(terms) == 2 else 1)
            steps = columns // width
            grid = max(grid, steps)
            specs += self.blocks(piece, width, steps, at)
            operands += terms
            counts.append(len(terms))
            shape = tuple(1 if i in done or i == at else n for i, n in enumerate(terms[0].shape[:-1]))
            outs.append(shaped(shape + (columns,), bf16))
            out_specs.append(
                pl.BlockSpec(
                    shape + (width,),
                    lambda i, places, n=len(shape), steps=steps: (0,) * n + (jnp.minimum(i, steps - 1),),
                )
            )
        count = len(pieces)

        def kernel(places, *refs):
            results = refs[-count - 1 : -1]
            refs[-1][0] = 0
            at = 0
            for i, terms in enumerate(counts):
                total = refs[at][...].astype(f32)
                for ref in refs[at + 1 : at + terms]:
                    total += ref[...].astype(f32)
                results[i][...] = total.astype(bf16)
                at += terms

        size = sum(int(np.prod(o.shape)) for o in outs)
        got = pl.pallas_call(
            kernel,
            grid_spec=pltpu.PrefetchScalarGridSpec(
                num_scalar_prefetch=1,
                grid=(grid,),
                in_specs=specs + [ANY] * len(before),
                out_specs=tuple(out_specs) + (FLAG,),
            ),
            out_shape=tuple(outs) + (flag_shape,),
            compiler_params=params(1),
            cost_estimate=pl.CostEstimate(flops=4 * size, bytes_accessed=8 * size, transcendentals=0),
            name="narrow",
        )(self.places, *operands, *before)
        results = []
        for (terms, done, half), at, leave in zip(pieces, ats, got):
            results.append((terms + [self.swap(leave, at)], done + [at], half))
        return results, [got[-1]]

    def close(self, pieces, kernel, out_shape, name, more=()):
        operands = [part.reshape(part.shape[-2:]) for piece in pieces for part in piece]

        def body(*refs):
            sums = [refs[2 * i][...] + refs[2 * i + 1][...].astype(f32) for i in range(len(pieces))]
            kernel(*sums, *refs[2 * len(pieces) :])

        return pl.pallas_call(
            body,
            out_shape=out_shape,
            in_specs=[VMEM] * (len(operands) + len(more)),
            out_specs=(VMEM,) * len(out_shape),
            compiler_params=params(),
            name=name,
        )(*operands, *more)


def local(
    dp,
    fsdp,
    images,
    grad_out,
    box_rows,
    box_cols,
    box_valid,
    box_count,
    in_weight,
    query_bias,
    value_bias,
    out_weight,
    out_bias,
    first_gain,
    first_shift,
    second_gain,
    second_shift,
    up_weight,
    up_bias,
    down_weight,
    down_bias,
    row_table,
    col_table,
):
    links = Exchange(dp, fsdp)
    image = images[0]
    core = (lax.axis_index("dp") & 1).astype(jnp.int32).reshape(1)
    hot = one_hot_keys(False)
    hot_back = one_hot_keys(True)
    eight = jnp.stack(
        [query_bias, value_bias, out_bias, first_gain, first_shift, second_gain, second_shift, down_bias]
    )
    first, second = links.orders[0][::-1], links.orders[1][::-1]
    last = len(first)
    two = links.spread(jnp.concatenate([in_weight[:, 2 * D :], out_weight], axis=1))
    one = links.spread(pack(eight, up_bias[None], in_weight))
    feed_weights = lax.all_gather(pack_feed(up_weight, down_weight), AXES, axis=0, tiled=True)
    for step in range(last - 2):
        two = links.join(two, second[step])
        one = links.join(one, first[step])
    cot, gupd, table, table_back, flag = weigh(
        box_count, grad_out[0], box_rows[0], box_cols[0], box_valid.reshape(NBOX, 1), row_table, col_table, [two, one]
    )
    two = links.join(two, second[last - 2], flag)
    one = links.join(one, first[last - 2], flag)
    unit, flag = begin(image, [two, one])
    unit = unit.reshape(WINDOWS * TOK, D)
    two = links.join(two, second[last - 1], flag)
    one = links.join(one, first[last - 1], flag)
    halves = [h.reshape(2, D // 4, -1) for h in (one, two, links.swap(one, 1), links.swap(two, 1))]

    tiles, packed, soft, att, branch, vec, one, two = forward(links.places, halves, unit, table, hot)
    block_out, gbr, gup_k, gup_s, gdown_k, gdown_s, gupb, sums2 = middle(
        core, image, cot, gupd, vec, feed_weights, branch.reshape(WINDOWS * WIN, LINE, D), att
    )

    first, second = links.orders
    gbr_flat = gbr.reshape(WINDOWS * TOK, D)
    feed = [(links.cut(gup_k, gup_s), [], None), (links.cut(gdown_k, gdown_s), [], None)]
    back = []
    flag = []
    start = 0
    for windows in CALLS:
        back.append(backward(start, windows, packed, soft, att, gbr_flat, two, table_back, hot_back, flag))
        flag = [back[-1][3]]
        if start == 0:
            feed, flag = links.narrow(feed, (first[0], second[0]), ((FF + D) // 2, FF // 2), flag)
        start += windows
    gpacked = [b[0] for b in back]
    image_grad, sums1, tables, flag = end(image, gbr, one, two, vec, gpacked, [b[2] for b in back], flag)
    feed, flag = links.narrow(feed, (first[1], second[1]), (FF + D, FF), [flag])
    all_tables = lax.all_gather(tables, AXES, axis=0, tiled=False)
    gin_k, gin_s, flag = attention_weights(core, (sums1, sums2, gupb), tiles, gpacked, [b[1] for b in back], flag)
    recv = links.tie([f[0][-1] for f in feed], [flag])
    feed = [(f[0][:-1] + [r], f[1], f[2]) for f, r in zip(feed, recv)]
    gin = links.cut(gin_k, gin_s)
    feed = [links.halve(links.own_part(f), at) for f, at in zip(feed, (first[2], second[2]))]
    gin = [(links.own_part((gin, [], half)),) for half in range(2)]
    for step in range(last):
        gin = [links.halve(sum(g), at) for g, at in zip([(g[0],) if len(g) == 1 else g[:2] for g in gin], (first[step], second[step]))]
        if 1 <= step < last - 2 or step == last - 1:
            late = links.tie([f[1] for f in feed], [g[2] for g in gin])
            feed = [(f[0], r) for f, r in zip(feed, late)]
        if 1 <= step < last - 2:
            ats = (first[step + 2], second[step + 2])
            feed = [links.halve(f[0] + f[1].astype(f32), at) for f, at in zip(feed, ats)]
    gin = [g[:2] for g in gin]
    feed = [f[:2] for f in feed]
    own = in_weight.shape[0]
    gup, gout, gdown = links.close(
        feed, unpack_feed_kernel, (shaped((own, FF), f32), shaped((own, D), f32), shaped((4 * own, D), f32)), "unpack_feed"
    )
    entries = 2 * WIN - 1
    gin, *out = links.close(
        gin,
        unpack_in_kernel,
        (shaped((own, 3 * D), f32),)
        + (shaped((1, own), f32),) * 8
        + (shaped((1, 4 * own), f32),)
        + (shaped((entries, HD), f32),) * 2,
        "unpack_in",
        [all_tables],
    )
    qb, vb, ob, g1, s1, g2, s2, db, ub = [o.reshape(-1) for o in out[:9]]
    row_grad, col_grad = out[9:]
    return (
        block_out[None],
        image_grad[None],
        gin,
        qb,
        vb,
        gout,
        ob,
        g1,
        s1,
        g2,
        s2,
        gup,
        ub,
        gdown,
        db,
        row_grad,
        col_grad,
    )


def solution(mesh):
    rows = P(AXES)
    dp, fsdp = mesh.shape["dp"], mesh.shape["fsdp"]
    return jax.shard_map(
        lambda *args: local(dp, fsdp, *args),
        mesh=mesh,
        in_specs=(rows,) * 19 + (P(), P()),
        out_specs=(rows,) * 15 + (P(), P()),
        check_vma=False,
    )
```

```python
import functools

import jax
import jax.numpy as jnp
import numpy as np
from jax import lax
from jax.experimental import pallas as pl
from jax.experimental.pallas import tpu as pltpu
from jax.sharding import PartitionSpec as P

D = 768
HEADS = 12
HD = 64
FF = 3072
WIN = 14
GH = 26
GW = 38
NBOX = 300
ACROSS = 3
WINDOWS = 6
LINE = 16
TOK = WIN * LINE
REAL = GH * GW
DENSE = 992
HALF = DENSE // 2
PAIRS = HEADS // 2
STARTS = (0, 14, 28)
WIDTHS = (14, 14, 10)
CHUNK = 768
CALLS = (2, 4)
SPLITS = ((0, 256), (256, 256), (512, 256), (768, 224))
epsilon = 1e-06
f32 = jnp.float32
bf16 = jnp.bfloat16
LIMIT = 60 * 1024 * 1024


def dot(a, b):
    return lax.dot_general(a, b, (((1,), (0,)), ((), ())), preferred_element_type=f32)


def dot_bt(a, b):
    return lax.dot_general(a, b, (((1,), (1,)), ((), ())), preferred_element_type=f32)


def dot_at(a, b):
    return lax.dot_general(a, b, (((0,), (0,)), ((), ())), preferred_element_type=f32)


def unit_of(x):
    center = x - jnp.mean(x, axis=-1, keepdims=True)
    inverse = lax.rsqrt(jnp.mean(center * center, axis=-1, keepdims=True) + epsilon)
    return center * inverse, inverse


def norm_back(grad, unit, inverse, gain):
    scaled = grad * gain
    return inverse * (
        scaled
        - jnp.mean(scaled, axis=-1, keepdims=True)
        - unit * jnp.mean(scaled * unit, axis=-1, keepdims=True)
    )


def place_of(row):
    return (row // WIN) * ACROSS, row % WIN


def spread_row(row, value, out_ref):
    first, place = place_of(row)
    for piece, (start, width) in enumerate(zip(STARTS, WIDTHS)):
        part = value[start : start + width]
        part = jnp.concatenate([part, jnp.zeros((LINE - width, part.shape[1]), part.dtype)], axis=0)
        out_ref[(first + piece) * WIN + place] = part.astype(out_ref.dtype)


def join_row(row, ref):
    first, place = place_of(row)
    return jnp.concatenate(
        [ref[(first + piece) * WIN + place].astype(f32)[:width] for piece, width in enumerate(WIDTHS)], axis=0
    )


def begin_kernel(img_ref, *refs):
    unit_ref, flag_ref = refs[-2:]
    flag_ref[0] = 0
    unit_ref[...] = jnp.zeros_like(unit_ref)
    for row in range(GH):
        unit, _ = unit_of(img_ref[row].astype(f32))
        spread_row(row, unit, unit_ref)


def pair_tables(row_table, col_table, entry_row, entry_col):
    parts = []
    for table, place in ((row_table, entry_row), (col_table, entry_col)):
        pieces = jnp.zeros((128, 128), f32)
        entries = lax.broadcasted_iota(jnp.int32, (2 * WIN - 1, 128), 0)
        lane = lane_iota((2 * WIN - 1, 128))
        row = lax.broadcasted_iota(jnp.int32, (128, 128), 0)
        for head in range(2):
            where = place(entries) + 32 * head
            pick = ((lane - where) % 64) == 0
            spread = dot_at(table, jnp.where(pick, 1.0, 0.0).astype(bf16))
            both = jnp.concatenate([spread, spread], axis=0)
            pieces = jnp.where((row < HD) == (head == 0), both, pieces)
        parts.append(pieces)
    return jnp.concatenate(parts, axis=1).astype(bf16)


def weight_kernel(count_ref, grad_ref, rows_ref, cols_ref, valid_ref, rowt_ref, colt_ref, *refs):
    cot_ref, upd_ref, table_ref, back_ref, flag_ref = refs[-5:]
    flag_ref[0] = 0
    table_ref[...] = pair_tables(rowt_ref[...], colt_ref[...], lambda e: 26 - e, lambda e: 29 - e)
    back_ref[...] = pair_tables(rowt_ref[...], colt_ref[...], lambda e: 26 - e, lambda e: 16 + e)
    slot = lax.broadcasted_iota(jnp.int32, (NBOX, 1), 0)
    live = (slot < count_ref[0]) & (valid_ref[...] == 1)
    rows = rows_ref[...]
    cols = cols_ref[...]
    top = jnp.minimum(rows[:, 0:1], rows[:, 1:2])
    low = jnp.maximum(rows[:, 0:1], rows[:, 1:2])
    left = jnp.minimum(cols[:, 0:1], cols[:, 1:2])
    right = jnp.maximum(cols[:, 0:1], cols[:, 1:2])
    grid_r = lax.broadcasted_iota(jnp.int32, (NBOX, GH), 1)
    grid_c = lax.broadcasted_iota(jnp.int32, (NBOX, GW), 1)
    in_rows = jnp.where((grid_r >= top) & (grid_r < low) & live, 1.0, 0.0)
    in_cols = jnp.where((grid_c >= left) & (grid_c < right), 1.0, 0.0)
    inside = dot_at(in_cols.astype(bf16), in_rows.astype(bf16))
    total = jnp.sum(jnp.where(live, 1.0, 0.0))
    weight = 1.0 + 2.0 * inside / jnp.maximum(total, 1.0)
    for row in range(GH):
        cot_ref[row * GW : (row + 1) * GW, :] = grad_ref[row].astype(f32) * weight[:, row : row + 1]
    cot_ref[REAL:, :] = jnp.zeros((DENSE - REAL, D), f32)
    upd_ref[...] = cot_ref[...].astype(bf16)


def lane_iota(shape):
    return lax.broadcasted_iota(jnp.int32, shape, len(shape) - 1)


def position_terms(queries, table):
    both = dot(queries, table)
    row_part = both[:, :128].reshape(WIN, LINE, 128)
    col_part = both[:, 128:].reshape(WIN, LINE, 128)
    lane = lane_iota((LINE, 128))
    local = lane % 32
    out = []
    for place in range(WIN):
        rolled_r = pltpu.roll(row_part[place], (place - 13) % 128, 1)
        rolled_c = pltpu.roll(col_part[place], 0, 1, stride=1, stride_axis=0)
        value = jnp.where(local < 16, rolled_r, rolled_c)
        high = value.astype(bf16).astype(f32)
        value = jnp.where(lane < 64, high, value - high)
        value = jnp.where(lane == 14, 1.0, value)
        out.append(value)
    return jnp.concatenate(out, axis=0).astype(bf16)


def keep_head(value, head):
    lane = lane_iota(value.shape)
    return jnp.where((lane < HD) == (head == 0), value, jnp.zeros_like(value))


def forward_kernel(places_ref, *refs):
    one_half, two_half, one_other, two_other, unit_ref, table_ref, hot_ref = refs[:7]
    tiles_ref, packed_ref, soft_ref, att_ref, branch_ref, vec_ref, one_ref, two_ref, sems = refs[7:]
    step = pl.program_id(0)

    @pl.when(step == 0)
    def _():
        core = places_ref[1]
        made = []
        for i, (half, whole_ref, place) in enumerate(
            [
                (one_half, one_ref, core),
                (two_half, two_ref, core),
                (one_other, one_ref, 1 - core),
                (two_other, two_ref, 1 - core),
            ]
        ):
            for y in range(2):
                here = pl.ds(pl.multiple_of((2 * y + place) * (D // 4), D // 4), D // 4)
                copy = pltpu.make_async_copy(half.at[y], whole_ref.at[here, :], sems.at[2 * i + y])
                copy.start()
                made.append(copy)
        for copy in made:
            copy.wait()
        vec_ref[...] = one_ref[:, :128].astype(f32).T[:16]

    window = step
    token = lax.broadcasted_iota(jnp.int32, (TOK, 1), 0)
    row_limit = jnp.where(window < ACROSS, WIN, GH - WIN)
    col_limit = jnp.where(window % ACROSS == ACROSS - 1, WIDTHS[2], WIN)
    valid = (token // LINE < row_limit) & (token % LINE < col_limit)
    tiles_ref[...] = (unit_ref[...] * vec_ref[3:4, :] + jnp.where(valid, vec_ref[4:5, :], 0.0)).astype(bf16)
    tiles = tiles_ref[...]
    packed_ref[:, :D] = (dot(tiles, one_ref[:, 128 : 128 + D]) + vec_ref[0:1, :]).astype(bf16)
    packed_ref[:, D : 2 * D] = dot(tiles, one_ref[:, 128 + D :]).astype(bf16)
    packed_ref[:, 2 * D :] = (dot(tiles, two_ref[:, :D]) + vec_ref[1:2, :]).astype(bf16)
    for pair in range(PAIRS):
        at = pair * 128
        queries = packed_ref[:, at : at + 128]
        keys = packed_ref[:, D + at : D + at + 128]
        values = packed_ref[:, 2 * D + at : 2 * D + at + 128]
        left = jnp.concatenate([queries, position_terms(queries, table_ref[...])], axis=1)
        parts = []
        for head in range(2):
            scaled = (keep_head(keys.astype(f32), head) * 0.125).astype(bf16)
            right = jnp.concatenate([scaled, hot_ref[head]], axis=1)
            scores = dot_bt(left, right)
            power = jnp.exp(scores - jnp.max(scores, axis=-1, keepdims=True))
            soft = (power * (1.0 / jnp.sum(power, axis=-1, keepdims=True))).astype(bf16)
            soft_ref[2 * pair + head] = soft
            parts.append(dot(soft, values))
        lane = lane_iota((TOK, 128))
        att_ref[:, at : at + 128] = jnp.where(lane < HD, parts[0], parts[1]).astype(bf16)
    branch_ref[...] = (dot(att_ref[...], two_ref[:, D:]) + vec_ref[2:3, :]).astype(bf16)


def backward_kernel(packed_ref, soft_ref, att_ref, gbr_ref, two_ref, table_ref, hot_ref, *refs):
    gpacked_ref, gbias_ref, gtab_ref, flag_ref, gatt_ref = refs[-5:]

    @pl.when(pl.program_id(0) == 0)
    def _():
        flag_ref[0] = 0
        gbias_ref[...] = jnp.zeros_like(gbias_ref)
        gtab_ref[...] = jnp.zeros_like(gtab_ref)

    gatt_ref[...] = dot_bt(gbr_ref[...], two_ref[:, D:]).astype(bf16)
    lane = lane_iota((LINE, 128))
    local = lane % 32
    wide = lane_iota((TOK, 128))
    for pair in range(PAIRS):
        at = pair * 128
        queries = packed_ref[:, at : at + 128]
        keys = packed_ref[:, D + at : D + at + 128]
        values = packed_ref[:, 2 * D + at : 2 * D + at + 128]
        gatt = gatt_ref[:, at : at + 128]
        product = gatt.astype(f32) * att_ref[:, at : at + 128].astype(f32)
        left = []
        right = []
        gvalues = []
        gkeys = []
        turned_g = gatt.T
        turned_q = queries.T
        for head in range(2):
            soft = soft_ref[2 * pair + head]
            delta = jnp.sum(keep_head(product, head), axis=-1, keepdims=True)
            gprobs = dot_bt(gatt, keep_head(values.astype(f32), head).astype(bf16))
            gscores = (soft.astype(f32) * (gprobs - delta)).astype(bf16)
            scaled = (keep_head(keys.astype(f32), head) * 0.125).astype(bf16)
            left.append(gscores)
            right.append(jnp.concatenate([scaled, hot_ref[head]], axis=1))
            rows = slice(head * HD, (head + 1) * HD)
            gvalues.append(dot(turned_g[rows], soft))
            gkeys.append(dot(turned_q[rows], gscores))
        both = dot(left[0], right[0]) + dot(left[1], right[1])
        terms = both[:, 128:].reshape(WIN, LINE, 128)
        rolled = []
        for place in range(WIN):
            value = terms[place]
            high = value.astype(bf16).astype(f32)
            value = jnp.where(lane < 64, high, value - high)
            row_part = jnp.where(local < WIN, value, 0.0)
            col_part = jnp.where((local >= 16) & (local < 16 + WIN), value, 0.0)
            row_part = pltpu.roll(row_part, 13 - place, 1)
            col_part = pltpu.roll(col_part, 0, 1, stride=1, stride_axis=0)
            rolled.append(jnp.concatenate([row_part, col_part], axis=1))
        rolled = jnp.concatenate(rolled, axis=0).astype(bf16)
        gqueries = both[:, :128] + dot_bt(rolled, table_ref[...])
        gtab_ref[...] += dot_at(rolled, queries)
        gq = gqueries.astype(bf16)
        gk = (jnp.concatenate(gkeys, axis=0) * 0.125).astype(bf16).T
        gv = jnp.concatenate(gvalues, axis=0).astype(bf16).T
        gpacked_ref[:, at : at + 128] = gq
        gpacked_ref[:, D + at : D + at + 128] = gk
        gpacked_ref[:, 2 * D + at : 2 * D + at + 128] = gv
        gbias_ref[0:1, at : at + 128] += jnp.sum(gq.astype(f32), axis=0, keepdims=True)
        gbias_ref[1:2, at : at + 128] += jnp.sum(gv.astype(f32), axis=0, keepdims=True)


def halve(core, value, keep_ref, send_ref, at):
    size = value.shape[0] // 4

    def put(first, second):
        for y in range(2):
            first[y * size : (y + 1) * size, at] = value[2 * y * size : (2 * y + 1) * size]
            second[y * size : (y + 1) * size, at] = value[(2 * y + 1) * size : (2 * y + 2) * size]

    @pl.when(core == 0)
    def _():
        put(keep_ref, send_ref)

    @pl.when(core == 1)
    def _():
        put(send_ref, keep_ref)


def attention_weights_kernel(core_ref, sums1_ref, sums2_ref, gupb_ref, tiles_ref, *refs):
    keep_ref, send_ref, flag_ref, gpacked, sems = refs[-5:]
    count = len(CALLS)
    gpacked_refs, gbias_refs = refs[:count], refs[count : 2 * count]
    flag_ref[0] = 0
    made = []
    for part in range(3):
        columns = slice(part * D, (part + 1) * D)
        at = 0
        for i, (windows, ref) in enumerate(zip(CALLS, gpacked_refs)):
            target = gpacked.at[at : at + windows * TOK, columns]
            copy = pltpu.make_async_copy(ref.at[:, columns], target, sems.at[part * count + i])
            copy.start()
            made.append(copy)
            at += windows * TOK
    gbias = gbias_refs[0][...]
    for ref in gbias_refs[1:]:
        gbias += ref[...]
    rows = [gbias[:2], sums2_ref[2:3, :], sums1_ref[:2, :], sums2_ref[:2, :], sums2_ref[3:4, :], gupb_ref[:4, :]]
    rows = jnp.concatenate(rows + [jnp.zeros((116, D), f32)], axis=0)
    value = jnp.concatenate([rows.T, jnp.zeros((D, 128), f32)], axis=1).astype(bf16)
    halve(core_ref[0], value, keep_ref, send_ref, slice(3 * D, 3 * D + 256))
    turned = tiles_ref[...].T
    for part in range(3):
        for copy in made[part * count : (part + 1) * count]:
            copy.wait()
        columns = slice(part * D, (part + 1) * D)
        halve(core_ref[0], dot(turned, gpacked[:, columns]).astype(bf16), keep_ref, send_ref, columns)


def gelu_parts(hidden):
    size = jnp.abs(hidden)
    power = jnp.exp(hidden * hidden * -0.5)
    denominator = 1.0 + (0.3275911 * 0.7071067811865476) * size
    near = pl.reciprocal(denominator, approx=True)
    near = near * (2.0 - denominator * near)
    series = near * (
        0.254829592
        + near * (-0.284496736 + near * (1.421413741 + near * (-1.453152027 + near * 1.061405429)))
    )
    tail = 0.5 * series * power
    normal = jnp.where(hidden >= 0, 1.0 - tail, tail)
    return hidden * normal, normal + hidden * power * 0.3989422804014327


def middle_kernel(
    core_ref,
    img_ref,
    cot_any,
    gupd_any,
    vec_ref,
    up_ref,
    down_ref,
    *refs,
):
    branch_ref, att_any = refs[:2]
    out_ref, gbr_ref, gupk_ref, gups_ref, gdownk_ref, gdowns_ref, gupb_ref, sums_ref = refs[2:10]
    mid, normed, update, gnorm, active, ghidden, cot_ref, gupd_ref, att_ref, sems = refs[10:]
    step = pl.program_id(0)

    def copies():
        pairs = ((gupd_any, gupd_ref), (cot_any, cot_ref), (att_any, att_ref))
        return [pltpu.make_async_copy(*pair, sems.at[i]) for i, pair in enumerate(pairs)]

    gain = vec_ref[5:6, :]
    shift = vec_ref[6:7, :]

    @pl.when(step == 0)
    def _():
        for copy in copies():
            copy.start()
        for row in range(GH):
            mid[row * GW : (row + 1) * GW, :] = img_ref[row].astype(f32) + join_row(row, branch_ref)
        mid[REAL:, :] = jnp.zeros((DENSE - REAL, D), f32)
        update[...] = jnp.zeros_like(update)
        gnorm[...] = jnp.zeros_like(gnorm)

        def chunk(index, carry):
            here = pl.ds(pl.multiple_of(index * HALF, HALF), HALF)
            unit, _ = unit_of(mid[here, :])
            normed[here, :] = (unit * gain + shift).astype(bf16)
            return carry

        lax.fori_loop(0, DENSE // HALF, chunk, 0)
        copies()[0].wait()

    @pl.when(step < FF // CHUNK)
    def _():
        up_bias = vec_ref[pl.ds(8 + step, 1), :]
        for start, size in SPLITS:
            here = slice(start, start + size)
            hidden = dot(normed[here, :], up_ref[...]) + up_bias
            gactive = dot_bt(gupd_ref[here, :], down_ref[...])
            act, slope = gelu_parts(hidden)
            act = act.astype(bf16)
            gh = (gactive * slope).astype(bf16)
            active[here, :] = act
            ghidden[here, :] = gh
            update[here, :] += dot(act, down_ref[...])
            gnorm[here, :] += dot_bt(gh, up_ref[...])
        gupb_ref[pl.ds(step, 1), :] = jnp.sum(ghidden[...].astype(f32), axis=0, keepdims=True)
        gdown = dot_at(active[...], gupd_ref[...]).astype(bf16)
        halve(core_ref[0], gdown, gdownk_ref, gdowns_ref, slice(None))
        gup = dot_at(normed[...], ghidden[...]).astype(bf16)
        halve(core_ref[0], gup, gupk_ref, gups_ref, slice(None))

    @pl.when(step == FF // CHUNK)
    def _():
        for copy in copies()[1:]:
            copy.wait()
        down_bias = vec_ref[7:8, :]
        for row in range(GH):
            here = slice(row * GW, (row + 1) * GW)
            out_ref[row] = (mid[here, :] + update[here, :] + down_bias).astype(bf16)

        def chunk(index, carry):
            here = pl.ds(pl.multiple_of(index * HALF, HALF), HALF)
            unit, inverse = unit_of(mid[here, :])
            grad = gnorm[here, :]
            cot = cot_ref[here, :]
            result = cot + norm_back(grad, unit, inverse, gain)
            rounded = result.astype(bf16).astype(f32)
            update[here, :] = rounded
            gain_sum, shift_sum, branch_sum, bias_sum = carry
            return (
                gain_sum + jnp.sum((grad * unit).reshape(HALF // 8, 8, D), axis=0),
                shift_sum + jnp.sum(grad.reshape(HALF // 8, 8, D), axis=0),
                branch_sum + jnp.sum(rounded.reshape(HALF // 8, 8, D), axis=0),
                bias_sum + jnp.sum(cot.astype(bf16).astype(f32).reshape(HALF // 8, 8, D), axis=0),
            )

        zero = jnp.zeros((8, D), f32)
        sums = lax.fori_loop(0, DENSE // HALF, chunk, (zero,) * 4)
        sums_ref[...] = jnp.concatenate(
            [jnp.sum(s, axis=0, keepdims=True) for s in sums] + [jnp.zeros((4, D), f32)], axis=0
        )
        gbr_ref[...] = jnp.zeros_like(gbr_ref)
        for row in range(GH):
            spread_row(row, update[row * GW : (row + 1) * GW, :], gbr_ref)
        gout = dot_at(att_ref[...], gbr_ref[...].reshape(WINDOWS * TOK, D))
        halve(core_ref[0], gout.astype(bf16), gupk_ref, gups_ref, slice(None))


def end_kernel(img_ref, gbr_ref, one_ref, two_ref, vec_ref, *refs):
    count = len(CALLS)
    gpacked_refs, gtab_refs = refs[:count], refs[count : 2 * count]
    out_ref, sums_ref, tables_ref, flag_ref, gtiles, gpacked, img, gbr, sems = refs[-9:]
    flag_ref[0] = 0
    made = []
    at = 0
    for i, (windows, ref) in enumerate(zip(CALLS, gpacked_refs)):
        made.append(pltpu.make_async_copy(ref, gpacked.at[at : at + windows * TOK, :], sems.at[i]))
        at += windows * TOK
    made.append(pltpu.make_async_copy(img_ref, img, sems.at[count]))
    made.append(pltpu.make_async_copy(gbr_ref, gbr, sems.at[count + 1]))
    for copy in made:
        copy.start()
    gain = vec_ref[3:4, :]
    at = 0
    for windows, copy in zip(CALLS, made):
        copy.wait()
        here = slice(at * TOK, (at + windows) * TOK)
        value = dot_bt(gpacked[here, : 2 * D], one_ref[:, 128:]) + dot_bt(gpacked[here, 2 * D :], two_ref[:, :D])
        gtiles[at * WIN : (at + windows) * WIN] = value.reshape(windows * WIN, LINE, D)
        at += windows
    for copy in made[count:]:
        copy.wait()
    gain_sum = jnp.zeros((1, D), f32)
    shift_sum = jnp.zeros((1, D), f32)
    for row in range(GH):
        unit, inverse = unit_of(img[row].astype(f32))
        grad = join_row(row, gtiles)
        gain_sum += jnp.sum(grad * unit, axis=0, keepdims=True)
        shift_sum += jnp.sum(grad, axis=0, keepdims=True)
        out_ref[row] = (join_row(row, gbr) + norm_back(grad, unit, inverse, gain)).astype(bf16)
    sums_ref[...] = jnp.concatenate([gain_sum, shift_sum, jnp.zeros((6, D), f32)], axis=0)
    total = gtab_refs[0][...]
    for ref in gtab_refs[1:]:
        total += ref[...]
    entries = 2 * WIN - 1
    rows = total[:128]
    cols = jnp.concatenate([total[128 + 16 :], total[128 : 128 + 16]], axis=0)
    tables = []
    for part in (rows, cols):
        whole_part = jnp.zeros((entries, HD), f32)
        for group in range(4):
            lines = part[32 * group : 32 * group + entries]
            whole_part += lines[:, HD:] if group % 2 else lines[:, :HD]
        tables.append(whole_part)
    flipped = [tables[0][entries - 1 - i : entries - i] for i in range(entries)]
    tables = jnp.concatenate(flipped + [tables[1], jnp.zeros((10, HD), f32)], axis=0)
    tables_ref[...] = jnp.concatenate([tables, jnp.zeros((64, HD), f32)], axis=1)


def pack_kernel(eight_ref, upb_ref, weight_ref, out_ref):
    own = weight_ref.shape[0]
    flat = upb_ref[...].astype(f32)
    rows = [eight_ref[...].astype(f32)] + [flat[:, own * i : own * (i + 1)] for i in range(4)]
    rows = jnp.concatenate(rows, axis=0)
    rows = jnp.concatenate([rows, jnp.zeros((12, 128 - own), f32)], axis=1)
    square = jnp.concatenate([rows, jnp.zeros((116, 128), f32)], axis=0)
    out_ref[:, :128] = square.T[:own].astype(bf16)
    out_ref[:, 128:] = weight_ref[:, : 2 * D]


def regroup(value, own, back=False):
    count = value.shape[1] // (4 * own)
    parts = []
    for i in range(count if back else 4):
        for j in range(4 if back else count):
            at = (j * count + i) * own if back else (4 * j + i) * own
            parts.append(value[:, at : at + own])
    return jnp.concatenate(parts, axis=1)


def pack_feed_kernel(up_ref, down_ref, out_ref):
    own = up_ref.shape[0]
    out_ref[:, :FF] = regroup(up_ref[...].astype(f32), own).astype(bf16)
    for k in range(4):
        part = down_ref[...].astype(f32)[k * own : (k + 1) * own]
        out_ref[:, FF + k * D : FF + (k + 1) * D] = part.astype(bf16)


def unpack_feed_kernel(first, second, up_ref, out_ref, down_ref):
    own = up_ref.shape[0]
    up_ref[...] = regroup(first[:, :FF], own, back=True)
    out_ref[...] = first[:, FF:]
    for k in range(4):
        down_ref[k * own : (k + 1) * own, :] = second[:, k * D : (k + 1) * D]


def unpack_in_kernel(first, second, tables_ref, in_ref, *refs):
    entries = 2 * WIN - 1
    tables = jnp.sum(tables_ref[...], axis=0)
    refs[-2][...] = tables[:entries, :HD]
    refs[-1][...] = tables[entries : 2 * entries, :HD]
    half = first.shape[1]
    in_ref[:, :half] = first
    in_ref[:, half:] = second[:, : 3 * D - half]
    own = first.shape[0]
    square = jnp.concatenate([second[:, 3 * D - half : 3 * D - half + 128], jnp.zeros((128 - own, 128), f32)], axis=0)
    rows = square.T
    for i in range(8):
        refs[i][...] = rows[i : i + 1, :own]
    refs[8][...] = jnp.concatenate([rows[i : i + 1, :own] for i in range(8, 12)], axis=1)


def params(steps=0):
    return pltpu.CompilerParams(
        vmem_limit_bytes=LIMIT, dimension_semantics=("arbitrary",) * steps if steps else None
    )


VMEM = pl.BlockSpec(memory_space=pltpu.VMEM)
SMEM = pl.BlockSpec(memory_space=pltpu.SMEM)


def whole(shape):
    return pl.BlockSpec(shape, lambda i: (0,) * len(shape))


def shaped(shape, dtype):
    return jax.ShapeDtypeStruct(shape, dtype)


def pack_feed(up, down):
    own = up.shape[0]
    return pl.pallas_call(
        pack_feed_kernel,
        out_shape=shaped((own, 2 * FF), bf16),
        in_specs=[VMEM] * 2,
        out_specs=VMEM,
        compiler_params=params(),
        name="pack_feed",
    )(up, down)


FLAG = pl.BlockSpec(memory_space=pltpu.SMEM)
ANY = pl.BlockSpec(memory_space=pl.ANY)
flag_shape = jax.ShapeDtypeStruct((1,), jnp.int32)


def begin(images, before):
    return pl.pallas_call(
        begin_kernel,
        out_shape=(shaped((WINDOWS * WIN, LINE, D), f32), flag_shape),
        in_specs=[VMEM] + [ANY] * len(before),
        out_specs=(VMEM, FLAG),
        compiler_params=params(),
        cost_estimate=pl.CostEstimate(flops=30_000_000, bytes_accessed=6_000_000, transcendentals=0),
        name="begin",
    )(images, *before)


def weigh(count, grad_out, rows, cols, valid, row_table, col_table, before):
    return pl.pallas_call(
        weight_kernel,
        out_shape=(
            shaped((DENSE, D), f32),
            shaped((DENSE, D), bf16),
            shaped((128, 256), bf16),
            shaped((128, 256), bf16),
            flag_shape,
        ),
        in_specs=[SMEM] + [VMEM] * 6 + [ANY] * len(before),
        out_specs=(VMEM,) * 4 + (FLAG,),
        compiler_params=params(),
        cost_estimate=pl.CostEstimate(flops=30_000_000, bytes_accessed=6_000_000, transcendentals=0),
        name="weigh",
    )(count, grad_out, rows, cols, valid, row_table, col_table, *before)


def forward(places, halves, unit, table, hot):
    per = lambda *shape: pl.BlockSpec(shape, lambda i: (i,) + (0,) * (len(shape) - 1))
    return pl.pallas_call(
        forward_kernel,
        grid=(WINDOWS,),
        out_shape=(
            shaped((WINDOWS * TOK, D), bf16),
            shaped((WINDOWS * TOK, 3 * D), bf16),
            shaped((WINDOWS * HEADS, TOK, TOK), bf16),
            shaped((WINDOWS * TOK, D), bf16),
            shaped((WINDOWS * TOK, D), bf16),
            shaped((16, D), f32),
            shaped((D, 128 + 2 * D), bf16),
            shaped((D, 2 * D), bf16),
        ),
        in_specs=[SMEM] + [ANY] * 4 + [per(TOK, D), whole((128, 256)), whole((2, TOK, 128))],
        out_specs=(
            per(TOK, D),
            per(TOK, 3 * D),
            per(HEADS, TOK, TOK),
            per(TOK, D),
            per(TOK, D),
            whole((16, D)),
            whole((D, 128 + 2 * D)),
            whole((D, 2 * D)),
        ),
        scratch_shapes=[pltpu.SemaphoreType.DMA((8,))],
        compiler_params=params(1),
        cost_estimate=pl.CostEstimate(flops=30_000_000_000, bytes_accessed=28_000_000, transcendentals=4_000_000),
        name="attend",
    )(places, *halves, unit, table, hot)


def middle(core, images, cot, gupd, vec, weights, branch, attended):
    steps = FF // CHUNK
    at = lambda i: jnp.minimum(i, steps - 1)
    return pl.pallas_call(
        middle_kernel,
        grid=(steps + 1,),
        out_shape=(
            shaped((GH, GW, D), bf16),
            shaped((WINDOWS * WIN, LINE, D), bf16),
            shaped((D // 2, FF + D), bf16),
            shaped((D // 2, FF + D), bf16),
            shaped((D // 2, FF), bf16),
            shaped((D // 2, FF), bf16),
            shaped((8, D), f32),
            shaped((8, D), f32),
        ),
        in_specs=[
            SMEM,
            whole((GH, GW, D)),
            ANY,
            ANY,
            whole((16, D)),
            pl.BlockSpec((D, CHUNK), lambda i: (0, at(i))),
            pl.BlockSpec((D, CHUNK), lambda i: (0, steps + at(i))),
        ]
        + [whole((WINDOWS * WIN, LINE, D)), ANY],
        out_specs=(
            whole((GH, GW, D)),
            whole((WINDOWS * WIN, LINE, D)),
            pl.BlockSpec((D // 2, CHUNK), lambda i: (0, i)),
            pl.BlockSpec((D // 2, CHUNK), lambda i: (0, i)),
            pl.BlockSpec((D // 2, CHUNK), lambda i: (0, at(i))),
            pl.BlockSpec((D // 2, CHUNK), lambda i: (0, at(i))),
            whole((8, D)),
            whole((8, D)),
        ),
        scratch_shapes=[
            pltpu.VMEM((DENSE, D), f32),
            pltpu.VMEM((DENSE, D), bf16),
            pltpu.VMEM((DENSE, D), f32),
            pltpu.VMEM((DENSE, D), f32),
            pltpu.VMEM((DENSE, CHUNK), bf16),
            pltpu.VMEM((DENSE, CHUNK), bf16),
            pltpu.VMEM((DENSE, D), f32),
            pltpu.VMEM((DENSE, D), bf16),
            pltpu.VMEM((WINDOWS * TOK, D), bf16),
            pltpu.SemaphoreType.DMA((3,)),
        ],
        compiler_params=params(1),
        cost_estimate=pl.CostEstimate(flops=50_000_000_000, bytes_accessed=36_000_000, transcendentals=6_000_000),
        name="feed",
    )(core, images, cot, gupd, vec, weights, weights, branch, attended)


def backward(start, count, packed, soft, att, gbr, two, table, hot, before=()):
    per = lambda *shape: pl.BlockSpec(shape, lambda i: (start + i,) + (0,) * (len(shape) - 1))
    return pl.pallas_call(
        backward_kernel,
        grid=(count,),
        out_shape=(
            shaped((count * TOK, 3 * D), bf16),
            shaped((8, D), f32),
            shaped((256, 128), f32),
            flag_shape,
        ),
        in_specs=[
            per(TOK, 3 * D),
            per(HEADS, TOK, TOK),
            per(TOK, D),
            per(TOK, D),
            whole((D, 2 * D)),
            whole((128, 256)),
            whole((2, TOK, 128)),
        ]
        + [ANY] * len(before),
        out_specs=(pl.BlockSpec((TOK, 3 * D), lambda i: (i, 0)), whole((8, D)), whole((256, 128)), FLAG),
        scratch_shapes=[pltpu.VMEM((TOK, D), bf16)],
        compiler_params=params(1),
        cost_estimate=pl.CostEstimate(flops=1_000_000_000, bytes_accessed=2_000_000, transcendentals=0),
        name="attend_back",
    )(packed, soft, att, gbr, two, table, hot, *before)


def attention_weights(core, sums, tiles, gpacked, gbias, before=()):
    return pl.pallas_call(
        attention_weights_kernel,
        grid=(1,),
        out_shape=(shaped((D // 2, 3 * D + 256), bf16),) * 2 + (flag_shape,),
        in_specs=[SMEM]
        + [whole((8, D))] * 3
        + [whole((WINDOWS * TOK, D))]
        + [ANY] * len(CALLS)
        + [whole((8, D))] * len(CALLS)
        + [ANY] * len(before),
        out_specs=(whole((D // 2, 3 * D + 256)),) * 2 + (FLAG,),
        scratch_shapes=[pltpu.VMEM((WINDOWS * TOK, 3 * D), bf16), pltpu.SemaphoreType.DMA((3 * len(CALLS),))],
        compiler_params=params(1),
        cost_estimate=pl.CostEstimate(flops=1_000_000_000, bytes_accessed=2_000_000, transcendentals=0),
        name="attend_weights",
    )(core, *sums, tiles, *gpacked, *gbias, *before)


def end(images, gbr, one, two, vec, gpacked, gtab, before=()):
    return pl.pallas_call(
        end_kernel,
        out_shape=(shaped((GH, GW, D), bf16), shaped((8, D), f32), shaped((64, 128), f32), flag_shape),
        in_specs=[ANY] * 2 + [VMEM] * 3 + [ANY] * len(CALLS) + [VMEM] * len(CALLS) + [ANY] * len(before),
        out_specs=(VMEM, VMEM, VMEM, FLAG),
        scratch_shapes=[
            pltpu.VMEM((WINDOWS * WIN, LINE, D), f32),
            pltpu.VMEM((WINDOWS * TOK, 3 * D), bf16),
            pltpu.VMEM((GH, GW, D), bf16),
            pltpu.VMEM((WINDOWS * WIN, LINE, D), bf16),
            pltpu.SemaphoreType.DMA((len(CALLS) + 2,)),
        ],
        compiler_params=params(),
        cost_estimate=pl.CostEstimate(flops=1_000_000_000, bytes_accessed=2_000_000, transcendentals=0),
        name="end",
    )(images, gbr, one, two, vec, *gpacked, *gtab, *before)


def pack(eight, up_bias, weight):
    return pl.pallas_call(
        pack_kernel,
        out_shape=shaped((weight.shape[0], 128 + 2 * D), bf16),
        in_specs=[VMEM] * 3,
        out_specs=VMEM,
        compiler_params=params(),
        name="pack",
    )(eight, up_bias, weight)


def one_hot_keys(flip):
    token = np.arange(TOK)
    row, col = token // LINE, token % LINE
    lane = np.arange(128)
    group, local = lane // 32, lane % 32
    hot = []
    for head in range(2):
        mine = (group % 2 == head)[None, :]
        value = ((local[None, :] == row[:, None]) & (local < WIN)[None, :]) | (
            (local[None, :] - 16 == (13 - col if flip else col)[:, None]) & (col < WIN)[:, None]
        )
        value = np.where(mine & value, 1.0, 0.0)
        value[:, 14] = np.where(col >= WIN, -1e30, 0.0)
        hot.append(value)
    return jnp.asarray(np.stack(hot), dtype=bf16)


AXES = ("dp", "fsdp")


class Exchange:
    def __init__(self, dp, fsdp):
        self.count = dp * fsdp
        self.bits = []
        bit = self.count // 2
        while bit:
            self.bits.append(bit)
            bit //= 2
        place = lax.axis_index(AXES).astype(jnp.int32)
        self.place = place
        self.mine = [(place >> (bit.bit_length() - 1)) & 1 for bit in self.bits]
        self.places = jnp.stack(self.mine)
        last = len(self.bits) - 1
        low = list(range(last - 1, 1, -1))
        self.orders = ([0, last] + low, [last, 0] + low)

    def swap(self, value, at):
        bit = self.bits[at]
        return lax.ppermute(value, AXES, [(i, i ^ bit) for i in range(self.count)])

    def spread(self, value):
        return value.reshape((1,) * len(self.bits) + value.shape)

    def join(self, value, at, flag=None):
        other = self.swap(value, at)
        mine = self.mine[at] if flag is None else self.mine[at] + flag[0]
        return jnp.where(
            mine == 0, jnp.concatenate([value, other], axis=at), jnp.concatenate([other, value], axis=at)
        )

    def own_part(self, piece, flag=None):
        terms, done, half = piece
        total = None
        for term in terms:
            for at in done:
                if term.shape[at] == 2:
                    mine = self.mine[at] if flag is None else self.mine[at] + flag[0]
                    term = lax.dynamic_index_in_dim(term, mine, at, keepdims=True)
            if half is not None:
                columns = term.shape[-1] // 2
                term = term[..., half * columns : (half + 1) * columns]
            term = term.astype(f32)
            total = term if total is None else total + term
        return total

    def halve(self, value, at):
        leave = lax.dynamic_index_in_dim(value, 1 - self.mine[at], at, keepdims=True).astype(bf16)
        stay = lax.dynamic_index_in_dim(value, self.mine[at], at, keepdims=True)
        return stay, self.swap(leave, at), leave

    def tie(self, values, before):
        count = len(values)

        def kernel(*refs):
            pass

        return pl.pallas_call(
            kernel,
            out_shape=tuple(shaped(v.shape, v.dtype) for v in values),
            in_specs=[ANY] * (count + len(before)),
            out_specs=(ANY,) * count,
            input_output_aliases={i: i for i in range(count)},
            name="tie",
        )(*values, *before)

    def flat(self, value):
        return value.reshape((self.count * value.shape[-2], value.shape[-1]))

    def cut(self, keep, send):
        rows, columns = keep.shape
        shape = (2, 1) + (2,) * (len(self.bits) - 2) + (2 * rows // self.count, columns)
        return [keep.reshape(shape), self.swap(send, 1).reshape(shape)]

    def blocks(self, piece, width, steps, leave=None):
        terms, done, half = piece
        specs = []
        for term in terms:
            shape = term.shape
            block, pick = [], []
            for at in range(len(self.bits)):
                cut = at in done or at == leave
                block.append(1 if cut else shape[at])
                pick.append((at, shape[at] == 2 and cut, at == leave))
            block += [shape[-2], width]
            first = half * steps if half and shape[-1] > width * steps else 0

            def index(i, places, pick=pick, first=first):
                where = [jnp.where(other, 1 - places[at], places[at]) if use else 0 for at, use, other in pick]
                return (*where, 0, first + jnp.minimum(i, steps - 1))

            specs.append(pl.BlockSpec(tuple(block), index))
        return specs

    def narrow(self, pieces, ats, widths, before=()):
        operands, specs, outs, out_specs, counts = [], [], [], [], []
        grid = 1
        for piece, at, width in zip(pieces, ats, widths):
            terms, done, half = piece
            columns = terms[-1].shape[-1] // (2 if half is not None and len(terms) == 2 else 1)
            steps = columns // width
            grid = max(grid, steps)
            specs += self.blocks(piece, width, steps, at)
            operands += terms
            counts.append(len(terms))
            shape = tuple(1 if i in done or i == at else n for i, n in enumerate(terms[0].shape[:-1]))
            outs.append(shaped(shape + (columns,), bf16))
            out_specs.append(
                pl.BlockSpec(
                    shape + (width,),
                    lambda i, places, n=len(shape), steps=steps: (0,) * n + (jnp.minimum(i, steps - 1),),
                )
            )
        count = len(pieces)

        def kernel(places, *refs):
            results = refs[-count - 1 : -1]
            refs[-1][0] = 0
            at = 0
            for i, terms in enumerate(counts):
                total = refs[at][...].astype(f32)
                for ref in refs[at + 1 : at + terms]:
                    total += ref[...].astype(f32)
                results[i][...] = total.astype(bf16)
                at += terms

        size = sum(int(np.prod(o.shape)) for o in outs)
        got = pl.pallas_call(
            kernel,
            grid_spec=pltpu.PrefetchScalarGridSpec(
                num_scalar_prefetch=1,
                grid=(grid,),
                in_specs=specs + [ANY] * len(before),
                out_specs=tuple(out_specs) + (FLAG,),
            ),
            out_shape=tuple(outs) + (flag_shape,),
            compiler_params=params(1),
            cost_estimate=pl.CostEstimate(flops=4 * size, bytes_accessed=8 * size, transcendentals=0),
            name="narrow",
        )(self.places, *operands, *before)
        results = []
        for (terms, done, half), at, leave in zip(pieces, ats, got):
            results.append((terms + [self.swap(leave, at)], done + [at], half))
        return results, [got[-1]]

    def close(self, pieces, kernel, out_shape, name, more=()):
        operands = [part.reshape(part.shape[-2:]) for piece in pieces for part in piece]

        def body(*refs):
            sums = [refs[2 * i][...] + refs[2 * i + 1][...].astype(f32) for i in range(len(pieces))]
            kernel(*sums, *refs[2 * len(pieces) :])

        return pl.pallas_call(
            body,
            out_shape=out_shape,
            in_specs=[VMEM] * (len(operands) + len(more)),
            out_specs=(VMEM,) * len(out_shape),
            compiler_params=params(),
            name=name,
        )(*operands, *more)


def local(
    dp,
    fsdp,
    images,
    grad_out,
    box_rows,
    box_cols,
    box_valid,
    box_count,
    in_weight,
    query_bias,
    value_bias,
    out_weight,
    out_bias,
    first_gain,
    first_shift,
    second_gain,
    second_shift,
    up_weight,
    up_bias,
    down_weight,
    down_bias,
    row_table,
    col_table,
):
    links = Exchange(dp, fsdp)
    image = images[0]
    core = (lax.axis_index("dp") & 1).astype(jnp.int32).reshape(1)
    hot = one_hot_keys(False)
    hot_back = one_hot_keys(True)
    eight = jnp.stack(
        [query_bias, value_bias, out_bias, first_gain, first_shift, second_gain, second_shift, down_bias]
    )
    first, second = links.orders[0][::-1], links.orders[1][::-1]
    last = len(first)
    two = links.spread(jnp.concatenate([in_weight[:, 2 * D :], out_weight], axis=1))
    one = links.spread(pack(eight, up_bias[None], in_weight))
    feed_weights = lax.all_gather(pack_feed(up_weight, down_weight), AXES, axis=0, tiled=True)
    for step in range(last - 2):
        two = links.join(two, second[step])
        one = links.join(one, first[step])
    cot, gupd, table, table_back, flag = weigh(
        box_count, grad_out[0], box_rows[0], box_cols[0], box_valid.reshape(NBOX, 1), row_table, col_table, [two, one]
    )
    two = links.join(two, second[last - 2], flag)
    one = links.join(one, first[last - 2], flag)
    unit, flag = begin(image, [two, one])
    unit = unit.reshape(WINDOWS * TOK, D)
    two = links.join(two, second[last - 1], flag)
    one = links.join(one, first[last - 1], flag)
    halves = [h.reshape(2, D // 4, -1) for h in (one, two, links.swap(one, 1), links.swap(two, 1))]

    tiles, packed, soft, att, branch, vec, one, two = forward(links.places, halves, unit, table, hot)
    block_out, gbr, gup_k, gup_s, gdown_k, gdown_s, gupb, sums2 = middle(
        core, image, cot, gupd, vec, feed_weights, branch.reshape(WINDOWS * WIN, LINE, D), att
    )

    first, second = links.orders
    gbr_flat = gbr.reshape(WINDOWS * TOK, D)
    feed = [(links.cut(gup_k, gup_s), [], None), (links.cut(gdown_k, gdown_s), [], None)]
    back = []
    flag = []
    start = 0
    for windows in CALLS:
        back.append(backward(start, windows, packed, soft, att, gbr_flat, two, table_back, hot_back, flag))
        flag = [back[-1][3]]
        if start == 0:
            feed, flag = links.narrow(feed, (first[0], second[0]), ((FF + D) // 2, FF // 2), flag)
        start += windows
    gpacked = [b[0] for b in back]
    image_grad, sums1, tables, flag = end(image, gbr, one, two, vec, gpacked, [b[2] for b in back], flag)
    feed, flag = links.narrow(feed, (first[1], second[1]), ((FF + D) // 2, FF // 2), [flag])
    all_tables = lax.all_gather(tables, AXES, axis=0, tiled=False)
    gin_k, gin_s, flag = attention_weights(core, (sums1, sums2, gupb), tiles, gpacked, [b[1] for b in back], flag)
    recv = links.tie([f[0][-1] for f in feed], [flag])
    feed = [(f[0][:-1] + [r], f[1], f[2]) for f, r in zip(feed, recv)]
    gin = links.cut(gin_k, gin_s)
    feed = [links.halve(links.own_part(f), at) for f, at in zip(feed, (first[2], second[2]))]
    gin = [(links.own_part((gin, [], half)),) for half in range(2)]
    for step in range(last):
        gin = [links.halve(sum(g), at) for g, at in zip([(g[0],) if len(g) == 1 else g[:2] for g in gin], (first[step], second[step]))]
        if 1 <= step < last - 2 or step == last - 1:
            late = links.tie([f[1] for f in feed], [g[2] for g in gin])
            feed = [(f[0], r) for f, r in zip(feed, late)]
        if 1 <= step < last - 2:
            ats = (first[step + 2], second[step + 2])
            feed = [links.halve(f[0] + f[1].astype(f32), at) for f, at in zip(feed, ats)]
    gin = [g[:2] for g in gin]
    feed = [f[:2] for f in feed]
    own = in_weight.shape[0]
    gup, gout, gdown = links.close(
        feed, unpack_feed_kernel, (shaped((own, FF), f32), shaped((own, D), f32), shaped((4 * own, D), f32)), "unpack_feed"
    )
    entries = 2 * WIN - 1
    gin, *out = links.close(
        gin,
        unpack_in_kernel,
        (shaped((own, 3 * D), f32),)
        + (shaped((1, own), f32),) * 8
        + (shaped((1, 4 * own), f32),)
        + (shaped((entries, HD), f32),) * 2,
        "unpack_in",
        [all_tables],
    )
    qb, vb, ob, g1, s1, g2, s2, db, ub = [o.reshape(-1) for o in out[:9]]
    row_grad, col_grad = out[9:]
    return (
        block_out[None],
        image_grad[None],
        gin,
        qb,
        vb,
        gout,
        ob,
        g1,
        s1,
        g2,
        s2,
        gup,
        ub,
        gdown,
        db,
        row_grad,
        col_grad,
    )


def solution(mesh):
    rows = P(AXES)
    dp, fsdp = mesh.shape["dp"], mesh.shape["fsdp"]
    return jax.shard_map(
        lambda *args: local(dp, fsdp, *args),
        mesh=mesh,
        in_specs=(rows,) * 19 + (P(), P()),
        out_specs=(rows,) * 15 + (P(), P()),
        check_vma=False,
    )
```
